512 devices in a mesh: ctx: 64 (over z_lo, y, core), head: 8 (over z_hi, x).
Axes of the slice: x: 4, y: 8, z: 8 (z_hi: 2, z_lo: 4; z = z_hi * 4 + z_lo), core: 2. Of those that a mesh axis runs over, the one named last changes fastest.
Arguments:
- q_attn: bfloat16 [128, 128, 576], P('ctx', 'head'), may hold values from -6 to 6
- latent: bfloat16 [65536, 576], P('ctx'), may hold values from -8 to 8
- lse_saved: float32 [128, 128], P('ctx', 'head'), may hold values from -2 to 2
- q_index: bfloat16 [128, 64, 128], P('ctx', 'head'), may hold values from -10 to 10
- k_index: bfloat16 [65536, 128], P('ctx'), may hold values from -6 to 6
- head_weight: float32 [128, 64], P('ctx', 'head'), may hold values from -1 to 1
Outputs:
- grad_query: float32 [128, 64, 128], P('ctx', 'head')
- grad_weight: float32 [128, 64], P('ctx', 'head')
- grad_key: float32 [65536, 128], P('ctx')
The draws below stay inside these ranges and needn't reach their ends.
All inputs are finite; a program needn't handle non-finite values.
Results may differ from the reference program's by a relative error of at most 0.0105.
Values may be sent and summed in bfloat16 or wider, within the bound.
A program may use at most 64 MiB of HBM per device.

```python
import jax
import jax.numpy as jnp
from jax import lax

HEADS = 128
D_LAT = 512
D_ROPE = 64
IX_HEADS = 64
IX_DIM = 128
ROWS = 128
KEY_DEV = 1024
KEYS = 65536


def shared_parts(key):
    base_key, weight_key, pick_key = jax.random.split(key, 3)
    keys_base = jax.random.normal(base_key, (KEYS, IX_DIM), jnp.float32)
    keys_base = jnp.clip(keys_base, -6.0, 6.0)
    weight_base = jnp.clip(jax.random.normal(weight_key, (ROWS, IX_HEADS), jnp.float32) * 0.18, -1.0, 1.0)
    picks = jax.random.permutation(pick_key, KEYS)[:8]
    second_keys = picks[4:]
    blended = keys_base[second_keys]
    keys_full = keys_base.at[second_keys].set(blended)
    return (keys_full, weight_base)


def draw_k_index(key, part):
    keys_full, weight_base = shared_parts(key)
    return keys_full.astype(jnp.bfloat16)


def draw_head_weight(key, part):
    keys_full, weight_base = shared_parts(key)
    return weight_base


def draw_q_index(key, part):
    key = jax.random.fold_in(key, 7)
    noise = jax.random.normal(key, (ROWS, IX_HEADS, IX_DIM), jnp.float32)
    noise = noise * IX_DIM ** (-0.5)
    tail_rows = noise[ROWS - 4:]
    values = jnp.concatenate([noise[:ROWS - 4], tail_rows], axis=0)
    return jnp.clip(values, -10.0, 10.0).astype(jnp.bfloat16)


def draw_latent(key, part):
    key = jax.random.fold_in(key, 3)
    value_key, block_key, jitter_key = jax.random.split(key, 3)
    width = D_LAT + D_ROPE
    position = jnp.arange(KEYS, dtype=jnp.float32) / KEYS
    block_part = jnp.repeat(jax.random.uniform(block_key, (KEYS // 32,), jnp.float32, -0.3, 0.3), 32)
    jitter = jax.random.uniform(jitter_key, (KEYS,), jnp.float32, -0.1, 0.1)
    row_scale = jnp.sqrt(0.2 + 2.0 * position) * jnp.exp(block_part + jitter)
    values = jax.random.normal(value_key, (KEYS, width), jnp.float32)
    return jnp.clip(values * row_scale[:, None], -8.0, 8.0).astype(jnp.bfloat16)


def block_scale(own_key, shape, pieces, least, largest):
    factor_of = 1.0
    for dim, parts in pieces:
        draws = jax.random.uniform(jax.random.fold_in(jax.random.fold_in(own_key, 6), dim), (parts,), jnp.float32, least / len(pieces), largest / len(pieces))
        factor_of = factor_of * jnp.repeat(jnp.exp(draws), shape[dim] // parts).reshape((-1,) + (1,) * (len(shape) - 1 - dim))
    return factor_of


def gaussian(rng, shape, scale, limit, pieces=(), held_as=jnp.bfloat16):
    entries = scale * jax.random.normal(rng, shape, jnp.float32)
    if pieces:
        entries = entries * block_scale(rng, shape, pieces, -0.22, 0.18)
    return jnp.clip(entries, -limit, limit).astype(held_as)


def setup_inputs(seed: int = 0) -> dict:
    arg_keys = jax.random.split(jax.random.key(seed), 7)
    return {
        "q_attn": gaussian(arg_keys[0], (ROWS, HEADS, D_LAT + D_ROPE), 1.0, 6.0, ((0, 64), (1, 8))),
        "latent": draw_latent(jax.random.fold_in(arg_keys[6], 71), 0),
        "lse_saved": jnp.clip(jax.random.uniform(arg_keys[2], (ROWS, HEADS), jnp.float32, -2.0, 2.0) * block_scale(arg_keys[2], (ROWS, HEADS), ((0, 64), (1, 8)), -0.4, 0.0), -2.0, 2.0),
        "q_index": draw_q_index(jax.random.fold_in(arg_keys[6], 71), 0),
        "k_index": draw_k_index(jax.random.fold_in(arg_keys[6], 71), 0),
        "head_weight": draw_head_weight(jax.random.fold_in(arg_keys[6], 71), 0),
    }


def contract(left, right):
    return lax.dot_general(left, right, (((1,), (1,)), ((), ())), preferred_element_type=jnp.float32)


def reference(q_attn, latent, lse_saved, q_index, k_index, head_weight):
    att_scale = (D_LAT + D_ROPE) ** -0.5
    blocks = KEYS // KEY_DEV
    latent_blocks = latent.reshape(blocks, KEY_DEV, D_LAT + D_ROPE)
    key_blocks = k_index.reshape(blocks, KEY_DEV, IX_DIM)
    query_flat = q_attn.reshape(ROWS * HEADS, D_LAT + D_ROPE)
    index_flat = q_index.reshape(ROWS * IX_HEADS, IX_DIM)

    def forward(pair):
        latent_block, key_block = pair
        scores = contract(query_flat, latent_block).reshape(ROWS, HEADS, KEY_DEV) * att_scale
        target_block = jnp.sum(jnp.exp(scores - lse_saved[:, :, None]), axis=1)
        index_raw = contract(index_flat, key_block).reshape(ROWS, IX_HEADS, KEY_DEV)
        score_block = jnp.sum(head_weight[:, :, None] * jnp.maximum(index_raw, 0.0), axis=1)
        return target_block, score_block

    target_raw, index_score = lax.map(forward, (latent_blocks, key_blocks))
    target_raw = jnp.moveaxis(target_raw, 0, 1).reshape(ROWS, KEYS)
    index_score = jnp.moveaxis(index_score, 0, 1).reshape(ROWS, KEYS)
    total_mass = jnp.sum(target_raw, axis=1, keepdims=True)
    peak_value = jnp.max(index_score, axis=1, keepdims=True)
    expo_terms = jnp.exp(index_score - peak_value)
    exp_total = jnp.sum(expo_terms, axis=1, keepdims=True)
    grad_scores = ((KEYS / 32.0) * (expo_terms / exp_total - target_raw / total_mass)).astype(jnp.bfloat16)
    grad_blocks = jnp.moveaxis(grad_scores.reshape(ROWS, blocks, KEY_DEV), 1, 0)

    def backward(carry, pair):
        key_block, grad_block = pair
        index_raw = contract(index_flat, key_block).reshape(ROWS, IX_HEADS, KEY_DEV)
        positive = index_raw > 0
        grad_f32 = grad_block.astype(jnp.float32)[:, None, :]
        weight_part = jnp.sum(grad_f32 * jnp.maximum(index_raw, 0.0), axis=2)
        masked = jnp.where(positive, grad_block[:, None, :], jnp.zeros((), jnp.bfloat16))
        masked = masked.reshape(ROWS * IX_HEADS, KEY_DEV)
        query_part = jnp.dot(masked, key_block, preferred_element_type=jnp.float32).reshape(ROWS, IX_HEADS, IX_DIM)
        coeffs = jnp.where(positive, grad_f32 * head_weight[:, :, None], 0.0).astype(jnp.bfloat16)
        coeffs = coeffs.reshape(ROWS * IX_HEADS, KEY_DEV)
        key_part = lax.dot_general(coeffs, index_flat, (((0,), (0,)), ((), ())), preferred_element_type=jnp.float32)
        return (carry[0] + query_part, carry[1] + weight_part), key_part

    start = (jnp.zeros((ROWS, IX_HEADS, IX_DIM), jnp.float32), jnp.zeros((ROWS, IX_HEADS), jnp.float32))
    (query_sum, grad_weight), key_parts = lax.scan(backward, start, (key_blocks, grad_blocks))
    grad_query = head_weight[:, :, None] * query_sum
    return grad_query, grad_weight, key_parts.reshape(KEYS, IX_DIM)
```

```python
import functools
import math

import jax
import jax.numpy as jnp
from jax import lax
from jax.experimental import pallas as pl
from jax.experimental.pallas import tpu as pltpu
from jax.sharding import PartitionSpec as P

MESH = pl.DeviceIdType.MESH
F32, BF16 = jnp.float32, jnp.bfloat16
DIMS = (4, 8, 2, 4)
NT = (((1,), (1,)), ((), ()))


def split3(v):
    hi = v.astype(BF16).astype(F32)
    mid = (v - hi).astype(BF16).astype(F32)
    return hi, mid, v - hi - mid


def column(row):
    n = row.shape[1]
    eye = lax.broadcasted_iota(jnp.int32, (n, n), 0) == lax.broadcasted_iota(jnp.int32, (n, n), 1)
    return jnp.sum(jnp.where(eye, row, 0.0), axis=1, keepdims=True)


def row_of(col):
    n = col.shape[0]
    eye = lax.broadcasted_iota(jnp.int32, (n, n), 0) == lax.broadcasted_iota(jnp.int32, (n, n), 1)
    return jnp.sum(jnp.where(eye, col, 0.0), axis=0, keepdims=True)


def kernel(
    dims, factor,
    q_ref, lat_ref, lse_ref, qi_ref, k_ref, w_ref,
    gq_ref, gw_ref, gk_ref,
    q_stage, i_stage, qbuf, ibuf, latbuf, kbuf, raw, wq, tacc, sacc, gbuf, masked,
    sy_buf, sz_buf, part, ry_buf, zsum, fq_buf,
    ck_own, ck_send, ck_recv, gx_sum, gx_send, gx_recv, gz_send, gz_recv, ga_buf,
    s_entry, r_entry, s_core, r_core, s_zq, s_zi, s_yp, s_ym, s_yi, r_q, r_i,
    s_sy, r_sy, s_sz, r_sz, s_ry, r_ry, s_fq, r_fq, s_gx, r_gx, s_gz, r_gz, s_ga, r_ga,
):
    NZ, NY, NZH, NX = dims
    ctx, head = lax.axis_index("ctx"), lax.axis_index("head")
    c = lax.rem(ctx, 2)
    y = lax.rem(lax.div(ctx, 2), NY)
    zl = lax.div(ctx, 2 * NY)
    x = lax.rem(head, NX)
    zh = lax.div(head, NX)
    rows, heads, width = q_ref.shape
    iheads, idim = qi_ref.shape[1:]
    nk = lat_ref.shape[0]
    wide = qbuf.shape[-1]
    R = NZ * rows
    K2 = 2 * nk
    base = wide - 128
    tail = width - base
    scale = width ** -0.5
    inv_scale = width ** 0.5
    log2e = math.log2(math.e)

    def ctx_of(zl_, y_, c_):
        return (zl_ * NY + y_) * 2 + c_

    def rcopy(src, dst, ssem, rsem, ctx_, head_):
        return pltpu.make_async_remote_copy(
            src_ref=src, dst_ref=dst, send_sem=ssem, recv_sem=rsem,
            device_id={"ctx": ctx_, "head": head_}, device_id_type=MESH,
        )

    def arrived(dst, rsem):
        pltpu.make_async_copy(dst, dst, rsem).wait()

    y_peers = [lax.rem(y + d, NY) for d in range(1, NY)]
    z_peers = [lax.rem(zl + d, NZ) for d in range(1, NZ)]
    x_peers = [lax.rem(x + d, NX) for d in range(1, NX)]
    fixed = head == y

    barrier = pltpu.get_barrier_semaphore()

    def greet(ctx_, head_):
        pl.semaphore_signal(barrier, inc=1, device_id={"ctx": ctx_, "head": head_}, device_id_type=MESH)

    greet(ctx_of(zl, y, 1 - c), head)
    for y_ in y_peers:
        greet(ctx_of(zl, y_, c), head)
    for z_ in z_peers:
        greet(ctx_of(z_, y, c), head)
        greet(ctx_of(z_, head, c), y)
    for x_ in x_peers:
        greet(ctx, zh * NX + x_)
    greet(ctx, (1 - zh) * NX + x)

    @pl.when(jnp.logical_not(fixed))
    def _():
        greet(ctx_of(zl, head, c), y)

    lane = lax.broadcasted_iota(jnp.int32, (heads, 128), 1)
    for r in range(rows):
        t3 = [v for v in split3(column(lse_ref[r : r + 1, :]))]
        w3 = [jnp.concatenate([v, jnp.zeros((heads - iheads, 1), F32)], axis=0)
              for v in split3(column(w_ref[r : r + 1, :]))]
        aug = jnp.zeros((heads, 128), F32)
        for n, v in enumerate(t3 + w3):
            aug = jnp.where(lane == tail + n, v, aug)
        q_stage[r * heads : (r + 1) * heads, :base] = q_ref[r, :, :base]
        last = jnp.concatenate([q_ref[r, :, base:].astype(F32), jnp.zeros((heads, 128 - tail), F32)], axis=1)
        q_stage[r * heads : (r + 1) * heads, base:] = (last + aug).astype(BF16)
    i_stage[...] = qi_ref[...].astype(F32).reshape(rows * iheads, idim).astype(BF16)
    latbuf[:nk, :base] = lat_ref[:, :base]
    klane = lax.broadcasted_iota(jnp.int32, (nk, 128 - tail), 1)
    kaug = jnp.where(klane < 3, -inv_scale, 0.0).astype(F32)
    latbuf[:nk, base:] = jnp.concatenate([lat_ref[:, base:].astype(F32), kaug], axis=1).astype(BF16)
    kbuf[:nk] = k_ref[...]

    pl.semaphore_wait(barrier, jnp.where(fixed, 1 + (NY - 1) + 2 * (NZ - 1) + (NX - 1) + 1,
                                         2 + (NY - 1) + 2 * (NZ - 1) + (NX - 1) + 1))

    @pl.when(jnp.logical_not(fixed))
    def _():
        rcopy(i_stage, ibuf.at[head, zl], s_entry.at[0], r_i.at[head, zl], ctx_of(zl, head, c), y).start()
        rcopy(q_stage, qbuf.at[head, zl], s_entry.at[1], r_q.at[head, zl], ctx_of(zl, head, c), y).start()

    @pl.when(fixed)
    def _():
        pltpu.make_async_copy(i_stage, ibuf.at[y, zl], r_i.at[y, zl]).start()
        pltpu.make_async_copy(q_stage, qbuf.at[y, zl], r_q.at[y, zl]).start()

    other = ctx_of(zl, y, 1 - c)
    k_copy = rcopy(kbuf.at[:nk], kbuf.at[nk:], s_core.at[0], r_core.at[0], other, head)
    lat_copy = rcopy(latbuf.at[:nk], latbuf.at[nk:], s_core.at[1], r_core.at[1], other, head)
    k_copy.start()
    lat_copy.start()

    tacc[...] = jnp.zeros_like(tacc)
    sacc[...] = jnp.zeros_like(sacc)

    sends = []
    up, down = lax.rem(y + 1, NY), lax.rem(y + NY - 1, NY)
    half_up = NY // 2
    half_down = NY - 1 - half_up

    def forward(y0, z0, step, plus, minus):
        if plus:
            cp = rcopy(qbuf.at[y0, z0], qbuf.at[y0, z0], s_yp.at[step, z0], r_q.at[y0, z0], ctx_of(zl, up, c), head)
            cp.start()
            sends.append(cp)
        if minus:
            cp = rcopy(qbuf.at[y0, z0], qbuf.at[y0, z0], s_ym.at[step, z0], r_q.at[y0, z0], ctx_of(zl, down, c), head)
            cp.start()
            sends.append(cp)

    arrived(ibuf.at[y, zl], r_i.at[y, zl])
    for n, z_ in enumerate(z_peers):
        cp = rcopy(ibuf.at[y, zl], ibuf.at[y, zl], s_zi.at[n], r_i.at[y, zl], ctx_of(z_, y, c), head)
        cp.start()
        sends.append(cp)
    arrived(qbuf.at[y, zl], r_q.at[y, zl])
    for n, z_ in enumerate(z_peers):
        cp = rcopy(qbuf.at[y, zl], qbuf.at[y, zl], s_zq.at[n], r_q.at[y, zl], ctx_of(z_, y, c), head)
        cp.start()
        sends.append(cp)
    forward(y, zl, 0, half_up > 0, half_down > 0)
    for z_ in z_peers:
        arrived(ibuf.at[y, z_], r_i.at[y, z_])
    for n, y_ in enumerate(y_peers):
        cp = rcopy(ibuf.at[y], ibuf.at[y], s_yi.at[n], r_yi(r_i, y), ctx_of(zl, y_, c), head)
        cp.start()
        sends.append(cp)
    for z_ in z_peers:
        arrived(qbuf.at[y, z_], r_q.at[y, z_])
        forward(y, z_, 0, half_up > 0, half_down > 0)

    CH = min(512, K2)

    def block(y0):
        q = qbuf[y0].reshape(R * heads, wide)
        qi = ibuf[y0].reshape(R * iheads, idim)
        aug = qbuf[y0, :, :, base:].astype(F32).reshape(R * heads, 128)
        ln = lax.broadcasted_iota(jnp.int32, aug.shape, 1)
        wide_col = jnp.sum(jnp.where((ln >= tail + 3) & (ln < tail + 6), aug, 0.0), axis=1, keepdims=True)
        wcol = wide_col.reshape(R, heads, 1)[:, :iheads, :]
        wq[y0] = (qi.astype(F32).reshape(R, iheads, idim) * wcol).reshape(R * iheads, idim).astype(BF16)

        @pl.loop(0, K2 // CH)
        def _(n):
            cols = pl.ds(pl.multiple_of(n * CH, CH), CH)
            s = lax.dot_general(q, latbuf[cols, :], NT, preferred_element_type=F32)
            e = jnp.exp2(s * (scale * log2e))
            tacc[:, :, cols] += jnp.sum(e.reshape(R, heads // 8, 8, CH), axis=1)
            rw = lax.dot_general(qi, kbuf[cols, :], NT, preferred_element_type=F32)
            raw[y0, :, cols] = rw
            sacc[:, :, cols] += wcol * jnp.maximum(rw, 0.0).reshape(R, iheads, CH)

    k_copy.wait_recv()
    lat_copy.wait_recv()
    block(y)
    for step in range(1, half_up + 1):
        yu = lax.rem(y + NY - step, NY)
        yd = lax.rem(y + step, NY)
        for n in range(NZ):
            z_ = lax.rem(zl + n, NZ)
            arrived(qbuf.at[yu, z_], r_q.at[yu, z_])
            forward(yu, z_, step, step < half_up, False)
            if step <= half_down:
                arrived(qbuf.at[yd, z_], r_q.at[yd, z_])
                forward(yd, z_, step, False, step < half_down)
        arrived(ibuf.at[yu], r_yi(r_i, yu))
        block(yu)
        if step <= half_down:
            arrived(ibuf.at[yd], r_yi(r_i, yd))
            block(yd)

    target = jnp.sum(tacc[...], axis=1)
    score = jnp.sum(sacc[...], axis=1)
    m = jnp.max(score, axis=1, keepdims=True)
    l = jnp.sum(jnp.exp(score - m), axis=1, keepdims=True)
    t = jnp.sum(target, axis=1, keepdims=True)
    sl = lax.broadcasted_iota(jnp.int32, (R, 128), 1)

    def exchange(buf, me, peers, where, ssem, rsem, m, l, t):
        buf[me] = jnp.where(sl == 0, m, jnp.where(sl == 1, l, t))
        for n, p in enumerate(peers):
            cp = rcopy(buf.at[me], buf.at[me], ssem.at[n], rsem.at[me], where(p), head)
            cp.start()
            sends.append(cp)
        for p in peers:
            arrived(buf.at[p], rsem.at[p])
        all_ = buf[...]
        mm = jnp.max(all_[:, :, 0:1], axis=0)
        ll = jnp.sum(all_[:, :, 1:2] * jnp.exp(all_[:, :, 0:1] - mm[None]), axis=0)
        tt = jnp.sum(all_[:, :, 2:3], axis=0)
        return mm, ll, tt

    m, l, t = exchange(sy_buf, y, y_peers, lambda p: ctx_of(zl, p, c), s_sy, r_sy, m, l, t)
    m, l, t = exchange(sz_buf, zl, z_peers, lambda p: ctx_of(p, y, c), s_sz, r_sz, m, l, t)
    grad = factor * (jnp.exp(score - m) / l - target / t)
    gbuf[...] = grad.astype(BF16).astype(F32)

    @pl.loop(0, NY)
    def _(y0):
        keep = raw[y0].reshape(R, iheads, K2) > 0
        g = jnp.where(keep, gbuf[...][:, None, :], 0.0)
        masked[y0] = g.reshape(R * iheads, K2).astype(BF16)

    mk = masked[...].reshape(NY * R * iheads, K2)
    wqt = wq[...].reshape(NY * R * iheads, idim).astype(F32).T.astype(BF16)
    gkt = jnp.dot(wqt, mk, preferred_element_type=F32)
    ck_send[...] = gkt[:, nk:].astype(BF16)
    ck_copy = rcopy(ck_send, ck_recv, s_core.at[2], r_core.at[2], other, head)
    ck_copy.start()
    ck_own[...] = gkt[:, :nk]
    part[...] = jnp.dot(mk, kbuf[...], preferred_element_type=F32).reshape(part.shape).astype(part.dtype)
    for n, y_ in enumerate(y_peers):
        cp = rcopy(part.at[y_], ry_buf.at[y], s_ry.at[n], r_ry.at[y], ctx_of(zl, y_, c), head)
        cp.start()
        sends.append(cp)

    ck_copy.wait_recv()
    nq = nk // NX
    for n in range(NX):
        v = ck_own[:, n * nq : (n + 1) * nq] + ck_recv[:, n * nq : (n + 1) * nq].astype(F32)
        gx_sum[n] = v
        gx_send[n] = v.astype(BF16)
    for n, x_ in enumerate(x_peers):
        cp = rcopy(gx_send.at[x_], gx_recv.at[x], s_gx.at[n], r_gx.at[x], ctx, zh * NX + x_)
        cp.start()
        sends.append(cp)

    total = part[y].astype(F32)
    for y_ in y_peers:
        arrived(ry_buf.at[y_], r_ry.at[y_])
        total = total + ry_buf[y_].astype(F32)
    zsum[...] = total.reshape(zsum.shape)

    for n in range(NZ):
        z_ = lax.rem(zl + n, NZ)
        if n == 0:
            @pl.when(jnp.logical_not(fixed))
            def _():
                rcopy(zsum.at[zl], fq_buf.at[zl], s_fq.at[0], r_fq.at[zl], ctx_of(zl, head, c), y).start()

            @pl.when(fixed)
            def _():
                pltpu.make_async_copy(zsum.at[zl], fq_buf.at[zl], r_fq.at[zl]).start()
        else:
            cp = rcopy(zsum.at[z_], fq_buf.at[zl], s_fq.at[n], r_fq.at[zl], ctx_of(z_, head, c), y)
            cp.start()
            sends.append(cp)

    gsum = gx_sum[x]
    for x_ in x_peers:
        arrived(gx_recv.at[x_], r_gx.at[x_])
        gsum = gsum + gx_recv[x_].astype(F32)
    gz_send[...] = gsum.astype(BF16)
    gz_copy = rcopy(gz_send, gz_recv, s_gz.at[0], r_gz.at[0], ctx, (1 - zh) * NX + x)
    gz_copy.start()
    gz_copy.wait_recv()
    gsum = gz_send[...].astype(F32) + gz_recv[...].astype(F32)
    ga_buf[x] = gsum.T.astype(BF16)
    for n, x_ in enumerate(x_peers):
        cp = rcopy(ga_buf.at[x], ga_buf.at[x], s_ga.at[n], r_ga.at[x], ctx, zh * NX + x_)
        cp.start()
        sends.append(cp)

    for n in range(NZ):
        z_ = lax.rem(zl + n, NZ)
        arrived(fq_buf.at[z_], r_fq.at[z_])
    qsum = jnp.sum(fq_buf[...], axis=0)
    for r in range(rows):
        own = qsum[r * iheads : (r + 1) * iheads]
        gq_ref[r] = own * column(w_ref[r : r + 1, :])
        gw_ref[r : r + 1, :] = row_of(jnp.sum(own * qi_ref[r].astype(F32), axis=1, keepdims=True))

    for x_ in x_peers:
        arrived(ga_buf.at[x_], r_ga.at[x_])
    gk_ref[...] = ga_buf[...].astype(F32).reshape(gk_ref.shape)

    for cp in sends:
        cp.wait_send()
    k_copy.wait_send()
    lat_copy.wait_send()
    ck_copy.wait_send()
    gz_copy.wait_send()

    @pl.when(jnp.logical_not(fixed))
    def _():
        rcopy(i_stage, ibuf.at[head, zl], s_entry.at[0], r_i.at[head, zl], ctx_of(zl, head, c), y).wait_send()
        rcopy(q_stage, qbuf.at[head, zl], s_entry.at[1], r_q.at[head, zl], ctx_of(zl, head, c), y).wait_send()
        rcopy(zsum.at[zl], fq_buf.at[zl], s_fq.at[0], r_fq.at[zl], ctx_of(zl, head, c), y).wait_send()


def r_yi(r_i, y0):
    return r_i.at[y0, r_i.shape[1] - 1]


def body(dims, keys, q_attn, latent, lse_saved, q_index, k_index, head_weight):
    NZ, NY, NZH, NX = dims
    rows, heads, width = q_attn.shape
    iheads, idim = q_index.shape[1:]
    nk = latent.shape[0]
    wide = -(-width // 128) * 128
    R = NZ * rows
    K2 = 2 * nk
    nq = nk // NX
    V, DMA = pltpu.VMEM, pltpu.SemaphoreType.DMA
    vm = pl.BlockSpec(memory_space=pltpu.VMEM)
    scratch = [
        V((rows * heads, wide), BF16), V((rows * iheads, idim), BF16),
        V((NY, NZ, rows * heads, wide), BF16), V((NY, NZ, rows * iheads, idim), BF16),
        V((K2, wide), BF16), V((K2, idim), BF16),
        V((NY, R * iheads, K2), F32), V((NY, R * iheads, idim), BF16),
        V((R, 8, K2), F32), V((R, iheads, K2), F32), V((R, K2), F32), V((NY, R * iheads, K2), BF16),
        V((NY, R, 128), F32), V((NZ, R, 128), F32),
        V((NY, R * iheads, idim), BF16), V((NY, R * iheads, idim), BF16),
        V((NZ, rows * iheads, idim), F32), V((NZ, rows * iheads, idim), F32),
        V((idim, nk), F32), V((idim, nk), BF16), V((idim, nk), BF16),
        V((NX, idim, nq), F32), V((NX, idim, nq), BF16), V((NX, idim, nq), BF16),
        V((idim, nq), BF16), V((idim, nq), BF16), V((NX, nq, idim), BF16),
        DMA((2,)), DMA((2,)), DMA((3,)), DMA((3,)), DMA((NZ,)), DMA((NZ,)),
        DMA((NY, NZ)), DMA((NY, NZ)), DMA((NY,)), DMA((NY, NZ)), DMA((NY, NZ + 1)),
        DMA((NY,)), DMA((NY,)), DMA((NZ,)), DMA((NZ,)), DMA((NY,)), DMA((NY,)), DMA((NZ,)), DMA((NZ,)),
        DMA((NX,)), DMA((NX,)), DMA((1,)), DMA((1,)), DMA((NX,)), DMA((NX,)),
    ]
    return pl.pallas_call(
        functools.partial(kernel, dims, keys / 32.0),
        out_shape=(
            jax.ShapeDtypeStruct((rows, iheads, idim), F32),
            jax.ShapeDtypeStruct((rows, iheads), F32),
            jax.ShapeDtypeStruct((nk, idim), F32),
        ),
        in_specs=[vm] * 6,
        out_specs=(vm, vm, vm),
        scratch_shapes=scratch,
        compiler_params=pltpu.CompilerParams(
            collective_id=0, has_side_effects=True, vmem_limit_bytes=48 * 1024 * 1024
        ),
        name="indexer_backward",
    )(q_attn, latent, lse_saved, q_index, k_index, head_weight)


def build(mesh, dims, keys):
    return jax.shard_map(
        functools.partial(body, dims, keys),
        mesh=mesh,
        in_specs=(
            P("ctx", "head", None),
            P("ctx", None),
            P("ctx", "head"),
            P("ctx", "head", None),
            P("ctx", None),
            P("ctx", "head"),
        ),
        out_specs=(P("ctx", "head", None), P("ctx", "head"), P("ctx", None)),
        check_vma=False,
    )


def solution(mesh):
    return build(mesh, DIMS, 65536)
```

```python
import functools
import math

import jax
import jax.numpy as jnp
from jax import lax
from jax.experimental import pallas as pl
from jax.experimental.pallas import tpu as pltpu
from jax.sharding import PartitionSpec as P

MESH = pl.DeviceIdType.MESH
F32, BF16 = jnp.float32, jnp.bfloat16
DIMS = (4, 8, 2, 4)
NT = (((1,), (1,)), ((), ()))


def split3(v):
    hi = v.astype(BF16).astype(F32)
    mid = (v - hi).astype(BF16).astype(F32)
    return hi, mid, v - hi - mid


def column(row):
    n = row.shape[1]
    eye = lax.broadcasted_iota(jnp.int32, (n, n), 0) == lax.broadcasted_iota(jnp.int32, (n, n), 1)
    return jnp.sum(jnp.where(eye, row, 0.0), axis=1, keepdims=True)


def row_of(col):
    n = col.shape[0]
    eye = lax.broadcasted_iota(jnp.int32, (n, n), 0) == lax.broadcasted_iota(jnp.int32, (n, n), 1)
    return jnp.sum(jnp.where(eye, col, 0.0), axis=0, keepdims=True)


def kernel(
    dims, factor,
    q_ref, lat_ref, lse_ref, qi_ref, k_ref, w_ref,
    gq_ref, gw_ref, gk_ref,
    q_stage, i_stage, qbuf, ientry, ibuf, latbuf, kbuf, raw, wq, tacc, sacc, gbuf, masked,
    sy_buf, sz_buf, part, ry_buf, zsum, fq_buf,
    ck_send, ck_recv, gx_sum, gx_send, gx_recv, gz_send, gz_recv, ga_buf,
    s_eq, s_ei, r_eq, r_ei, s_core, r_core, s_up, s_down, r_y,
    s_sy, r_sy, s_sz, r_sz, s_ry, r_ry, s_fq, r_fq, s_gx, r_gx, s_gz, r_gz, s_ga, r_ga,
):
    NZ, NY, NZH, NX = dims
    NH = NZH * NX
    ctx, head = lax.axis_index("ctx"), lax.axis_index("head")
    c = lax.rem(ctx, 2)
    y = lax.rem(lax.div(ctx, 2), NY)
    zl = lax.div(ctx, 2 * NY)
    x = lax.rem(head, NX)
    zh = lax.div(head, NX)
    rows, heads, width = q_ref.shape
    iheads, idim = qi_ref.shape[1:]
    nk = lat_ref.shape[1]
    wide = qbuf.shape[-1]
    K2 = 2 * nk
    J = NH * iheads
    base = wide - 128
    tail = width - base
    scale = width ** -0.5
    inv_scale = width ** 0.5
    log2e = math.log2(math.e)
    own_plane = x == zl

    def ctx_of(zl_, y_, c_):
        return (zl_ * NY + y_) * 2 + c_

    def rcopy(src, dst, ssem, rsem, ctx_, head_):
        return pltpu.make_async_remote_copy(
            src_ref=src, dst_ref=dst, send_sem=ssem, recv_sem=rsem,
            device_id={"ctx": ctx_, "head": head_}, device_id_type=MESH,
        )

    def arrived(dst, rsem):
        pltpu.make_async_copy(dst, dst, rsem).wait()

    sends = []

    def send(*args):
        cp = rcopy(*args)
        cp.start()
        sends.append(cp.wait_send)

    def send_unless(local, src, dst, ssem, rsem, ctx_, head_):
        @pl.when(jnp.logical_not(local))
        def _():
            rcopy(src, dst, ssem, rsem, ctx_, head_).start()

        @pl.when(local)
        def _():
            pltpu.make_async_copy(src, dst, rsem).start()

        def finish():
            @pl.when(jnp.logical_not(local))
            def _():
                rcopy(src, dst, ssem, rsem, ctx_, head_).wait_send()

        sends.append(finish)

    y_peers = [lax.rem(y + d, NY) for d in range(1, NY)]
    z_peers = [lax.rem(zl + d, NZ) for d in range(1, NZ)]
    x_peers = [lax.rem(x + d, NX) for d in range(1, NX)]
    zls = [zl] + z_peers
    hs = [lax.rem(head + d, NH) for d in range(NH)]

    barrier = pltpu.get_barrier_semaphore()

    def greet(ctx_, head_):
        pl.semaphore_signal(barrier, inc=1, device_id={"ctx": ctx_, "head": head_}, device_id_type=MESH)

    for d, h in enumerate(hs):
        if d == 0:
            @pl.when(jnp.logical_not(own_plane))
            def _():
                greet(ctx_of(x, y, c), head)
        else:
            greet(ctx_of(x, y, c), h)
    for r in range(NZH):
        for d, z_ in enumerate(zls):
            if d == 0:
                @pl.when(jnp.logical_not(own_plane & (zh == r)))
                def _():
                    greet(ctx_of(zl, y, c), r * NX + zl)
            else:
                greet(ctx_of(z_, y, c), r * NX + zl)
    greet(ctx_of(zl, y, 1 - c), head)
    for y_ in y_peers:
        greet(ctx_of(zl, y_, c), head)
    for z_ in z_peers:
        greet(ctx_of(z_, y, c), head)
    for x_ in x_peers:
        greet(ctx, zh * NX + x_)
    greet(ctx, (1 - zh) * NX + x)
    n_greet = 1 + (NY - 1) + (NZ - 1) + (NX - 1) + 1 + NH + NZH * NZ

    lane = lax.broadcasted_iota(jnp.int32, (heads, 128), 1)
    for r in range(rows):
        t3 = list(split3(column(lse_ref[r : r + 1, :])))
        w3 = [jnp.concatenate([v, jnp.zeros((heads - iheads, 1), F32)], axis=0)
              for v in split3(column(w_ref[r : r + 1, :]))]
        aug = jnp.zeros((heads, 128), F32)
        for n, v in enumerate(t3 + w3):
            aug = jnp.where(lane == tail + n, v, aug)
        q_stage[r, :, :base] = q_ref[r, :, :base]
        last = jnp.concatenate([q_ref[r, :, base:].astype(F32), jnp.zeros((heads, 128 - tail), F32)], axis=1)
        q_stage[r, :, base:] = (last + aug).astype(BF16)
        i_stage[r] = jnp.concatenate(
            [qi_ref[r].astype(F32), jnp.zeros((heads - iheads, idim), F32)], axis=0
        ).astype(BF16)
    krow = lax.broadcasted_iota(jnp.int32, (wide - width, nk), 0)
    latbuf[0, :width] = lat_ref[...]
    for side in range(2):
        latbuf[side, width:] = jnp.where(krow < 3, -inv_scale, 0.0).astype(BF16)
    kbuf[0] = k_ref[...]

    pl.semaphore_wait(barrier, jnp.where(own_plane, n_greet - 2, n_greet))

    for r in range(rows):
        for d, z_ in enumerate(zls):
            to = (ctx_of(z_, y, c), r * NX + zl)
            iargs = (i_stage.at[r], ientry.at[head], s_ei.at[r, d], r_ei.at[head], *to)
            qargs = (q_stage.at[r], qbuf.at[y, head], s_eq.at[r, d], r_eq.at[head], *to)
            if d == 0:
                send_unless(own_plane & (zh == r), *iargs)
                send_unless(own_plane & (zh == r), *qargs)
            else:
                send(*iargs)
                send(*qargs)
    other = ctx_of(zl, y, 1 - c)
    send(kbuf.at[0], kbuf.at[1], s_core.at[0], r_core.at[0], other, head)
    send(latbuf.at[0, :width], latbuf.at[1, :width], s_core.at[1], r_core.at[1], other, head)

    NC = NH // 2
    up, down = lax.rem(y + 1, NY), lax.rem(y + NY - 1, NY)
    half_up = NY // 2
    half_down = NY - 1 - half_up

    def piece(y0, n):
        return ibuf.at[y0] if n == 0 else qbuf.at[y0, 2 * (n - 1) : 2 * n]

    def forward(y0, n, step, plus, minus):
        if plus:
            send(piece(y0, n), piece(y0, n), s_up.at[step, n], r_y.at[y0, n], ctx_of(zl, up, c), head)
        if minus:
            send(piece(y0, n), piece(y0, n), s_down.at[step, n], r_y.at[y0, n], ctx_of(zl, down, c), head)

    for h in range(NH):
        arrived(ientry.at[h], r_ei.at[h])
    ibuf[y] = ientry[...].astype(F32)[:, :iheads, :].reshape(J, idim).astype(BF16)
    forward(y, 0, 0, half_up > 0, half_down > 0)
    for n in range(NC):
        for h in (2 * n, 2 * n + 1):
            arrived(qbuf.at[y, h], r_eq.at[h])
        forward(y, n + 1, 0, half_up > 0, half_down > 0)

    CH = min(512, nk)

    def block(y0):
        q = qbuf[y0].reshape(NH * heads, wide)
        qi = ibuf[y0]
        aug = qbuf[y0, :, :, base:].astype(F32).reshape(NH * heads, 128)
        ln = lax.broadcasted_iota(jnp.int32, aug.shape, 1)
        wide_col = jnp.sum(jnp.where((ln >= tail + 3) & (ln < tail + 6), aug, 0.0), axis=1, keepdims=True)
        wcol = wide_col.reshape(NH, heads, 1)[:, :iheads, :].reshape(J, 1)
        wq[y0] = (qi.astype(F32) * wcol).astype(BF16)
        for side in range(2):
            for n in range(nk // CH):
                cols = slice(n * CH, (n + 1) * CH)
                kcols = slice(side * nk + n * CH, side * nk + (n + 1) * CH)
                s = jnp.dot(q, latbuf[side, :, cols], preferred_element_type=F32)
                e = jnp.exp2(s * (scale * log2e))
                tacc[y0, :, kcols] = jnp.sum(e.reshape(NH * heads // 8, 8, CH), axis=0)
                rw = lax.dot_general(qi, kbuf[side, cols, :], NT, preferred_element_type=F32)
                raw[y0, :, kcols] = rw
                sacc[y0, :, kcols] = jnp.sum((wcol * jnp.maximum(rw, 0.0)).reshape(J // 8, 8, CH), axis=0)

    arrived(kbuf.at[1], r_core.at[0])
    arrived(latbuf.at[1, :width], r_core.at[1])
    block(y)
    for step in range(1, half_up + 1):
        yu = lax.rem(y + NY - step, NY)
        yd = lax.rem(y + step, NY)
        for n in range(NC + 1):
            arrived(piece(yu, n), r_y.at[yu, n])
            forward(yu, n, step, step < half_up, False)
            if step <= half_down:
                arrived(piece(yd, n), r_y.at[yd, n])
                forward(yd, n, step, False, step < half_down)
        block(yu)
        if step <= half_down:
            block(yd)

    target = jnp.sum(tacc[...], axis=1)
    score = jnp.sum(sacc[...], axis=1)
    m = jnp.max(score, axis=1, keepdims=True)
    l = jnp.sum(jnp.exp(score - m), axis=1, keepdims=True)
    t = jnp.sum(target, axis=1, keepdims=True)
    sl = lax.broadcasted_iota(jnp.int32, (NY, 128), 1)

    def exchange(buf, me, peers, where, ssem, rsem, m, l, t):
        buf[me] = jnp.where(sl == 0, m, jnp.where(sl == 1, l, t))
        for n, p in enumerate(peers):
            send(buf.at[me], buf.at[me], ssem.at[n], rsem.at[me], where(p), head)
        for p in peers:
            arrived(buf.at[p], rsem.at[p])
        all_ = buf[...]
        mm = jnp.max(all_[:, :, 0:1], axis=0)
        ll = jnp.sum(all_[:, :, 1:2] * jnp.exp(all_[:, :, 0:1] - mm[None]), axis=0)
        tt = jnp.sum(all_[:, :, 2:3], axis=0)
        return mm, ll, tt

    m, l, t = exchange(sy_buf, y, y_peers, lambda p: ctx_of(zl, p, c), s_sy, r_sy, m, l, t)
    m, l, t = exchange(sz_buf, zl, z_peers, lambda p: ctx_of(p, y, c), s_sz, r_sz, m, l, t)
    grad = factor * (jnp.exp(score - m) / l - target / t)
    gbuf[...] = grad.astype(BF16).astype(F32)

    wqt = wq[...].reshape(NY * J, idim).astype(F32).T.astype(BF16)

    def mask_half(side):
        kcols = slice(side * nk, (side + 1) * nk)
        for y0 in range(NY):
            g = jnp.where(raw[y0, :, kcols] > 0, gbuf[y0 : y0 + 1, kcols], 0.0)
            masked[side, y0 * J : (y0 + 1) * J] = g.astype(BF16)

    mask_half(1)
    ck_send[...] = jnp.dot(wqt, masked[1], preferred_element_type=F32).astype(BF16)
    send(ck_send, ck_recv, s_core.at[2], r_core.at[2], other, head)
    mask_half(0)
    nq = nk // NX
    own_key = jnp.dot(wqt, masked[0], preferred_element_type=F32)
    arrived(ck_recv, r_core.at[2])
    for n in range(NX):
        v = own_key[:, n * nq : (n + 1) * nq] + ck_recv[:, n * nq : (n + 1) * nq].astype(F32)
        gx_sum[n] = v
        gx_send[n] = v.astype(BF16)
    for n, x_ in enumerate(x_peers):
        send(gx_send.at[x_], gx_recv.at[x], s_gx.at[n], r_gx.at[x], ctx, zh * NX + x_)

    part[...] = (
        jnp.dot(masked[0], kbuf[0], preferred_element_type=F32)
        + jnp.dot(masked[1], kbuf[1], preferred_element_type=F32)
    ).reshape(part.shape).astype(part.dtype)
    for n, y_ in enumerate(y_peers):
        send(part.at[y_], ry_buf.at[y], s_ry.at[n], r_ry.at[y], ctx_of(zl, y_, c), head)

    gsum = gx_sum[x]
    for x_ in x_peers:
        arrived(gx_recv.at[x_], r_gx.at[x_])
        gsum = gsum + gx_recv[x_].astype(F32)
    gz_send[...] = gsum.astype(BF16)
    send(gz_send, gz_recv, s_gz.at[0], r_gz.at[0], ctx, (1 - zh) * NX + x)

    total = part[y].astype(F32)
    for y_ in y_peers:
        arrived(ry_buf.at[y_], r_ry.at[y_])
        total = total + ry_buf[y_].astype(F32)
    zsum[...] = total.reshape(zsum.shape)
    slot = zh * NZ + zl
    for d, h in enumerate(hs):
        args = (zsum.at[h], fq_buf.at[slot], s_fq.at[d], r_fq.at[slot], ctx_of(x, y, c), h)
        if d == 0:
            send_unless(own_plane, *args)
        else:
            send(*args)

    arrived(gz_recv, r_gz.at[0])
    ga_buf[x] = (gz_send[...].astype(F32) + gz_recv[...].astype(F32)).T.astype(BF16)
    for n, x_ in enumerate(x_peers):
        send(ga_buf.at[x], ga_buf.at[x], s_ga.at[n], r_ga.at[x], ctx, zh * NX + x_)

    for n in range(NZH * NZ):
        arrived(fq_buf.at[n], r_fq.at[n])
    for r in range(rows):
        own = jnp.sum(fq_buf[r * NZ : (r + 1) * NZ], axis=0)
        gq_ref[r] = own * column(w_ref[r : r + 1, :])
        gw_ref[r : r + 1, :] = row_of(jnp.sum(own * qi_ref[r].astype(F32), axis=1, keepdims=True))

    for x_ in x_peers:
        arrived(ga_buf.at[x_], r_ga.at[x_])
    gk_ref[...] = ga_buf[...].astype(F32).reshape(gk_ref.shape)

    for finish in sends:
        finish()


def body(dims, keys, q_attn, latent, lse_saved, q_index, k_index, head_weight):
    NZ, NY, NZH, NX = dims
    NH = NZH * NX
    rows, heads, width = q_attn.shape
    iheads, idim = q_index.shape[1:]
    nk = latent.shape[0]
    wide = -(-width // 128) * 128
    J = NH * iheads
    K2 = 2 * nk
    nq = nk // NX
    NP = NH // 2 + 1
    V, DMA = pltpu.VMEM, pltpu.SemaphoreType.DMA
    vm = pl.BlockSpec(memory_space=pltpu.VMEM)
    scratch = [
        V((rows, heads, wide), BF16), V((rows, heads, idim), BF16),
        V((NY, NH, heads, wide), BF16), V((NH, heads, idim), BF16), V((NY, J, idim), BF16),
        V((2, wide, nk), BF16), V((2, nk, idim), BF16),
        V((NY, J, K2), F32), V((NY, J, idim), BF16),
        V((NY, 8, K2), F32), V((NY, 8, K2), F32), V((NY, K2), F32), V((2, NY * J, nk), BF16),
        V((NY, NY, 128), F32), V((NZ, NY, 128), F32),
        V((NY, J, idim), BF16), V((NY, J, idim), BF16),
        V((NH, iheads, idim), F32), V((NZH * NZ, iheads, idim), F32),
        V((idim, nk), BF16), V((idim, nk), BF16),
        V((NX, idim, nq), F32), V((NX, idim, nq), BF16), V((NX, idim, nq), BF16),
        V((idim, nq), BF16), V((idim, nq), BF16), V((NX, nq, idim), BF16),
        DMA((rows, NZ)), DMA((rows, NZ)), DMA((NH,)), DMA((NH,)), DMA((3,)), DMA((3,)),
        DMA((NY, NP)), DMA((NY, NP)), DMA((NY, NP)),
        DMA((NY,)), DMA((NY,)), DMA((NZ,)), DMA((NZ,)), DMA((NY,)), DMA((NY,)), DMA((NH,)), DMA((NZH * NZ,)),
        DMA((NX,)), DMA((NX,)), DMA((1,)), DMA((1,)), DMA((NX,)), DMA((NX,)),
    ]
    return pl.pallas_call(
        functools.partial(kernel, dims, keys / 32.0),
        out_shape=(
            jax.ShapeDtypeStruct((rows, iheads, idim), F32),
            jax.ShapeDtypeStruct((rows, iheads), F32),
            jax.ShapeDtypeStruct((nk, idim), F32),
        ),
        in_specs=[vm] * 6,
        out_specs=(vm, vm, vm),
        scratch_shapes=scratch,
        compiler_params=pltpu.CompilerParams(
            collective_id=0, has_side_effects=True, vmem_limit_bytes=48 * 1024 * 1024
        ),
        name="indexer_backward",
    )(q_attn, latent.T, lse_saved, q_index, k_index, head_weight)


def build(mesh, dims, keys):
    return jax.shard_map(
        functools.partial(body, dims, keys),
        mesh=mesh,
        in_specs=(
            P("ctx", "head", None),
            P("ctx", None),
            P("ctx", "head"),
            P("ctx", "head", None),
            P("ctx", None),
            P("ctx", "head"),
        ),
        out_specs=(P("ctx", "head", None), P("ctx", "head"), P("ctx", None)),
        check_vma=False,
    )


def solution(mesh):
    return build(mesh, DIMS, 65536)
```

```python
import functools
import math

import jax
import jax.numpy as jnp
from jax import lax
from jax.experimental import pallas as pl
from jax.experimental.pallas import tpu as pltpu
from jax.sharding import PartitionSpec as P

MESH = pl.DeviceIdType.MESH
F32, BF16 = jnp.float32, jnp.bfloat16
DIMS = (4, 8, 2, 4)
KC = 2
NT = (((1,), (1,)), ((), ()))


def split3(v):
    hi = v.astype(BF16).astype(F32)
    mid = (v - hi).astype(BF16).astype(F32)
    return hi, mid, v - hi - mid


def column(row):
    n = row.shape[1]
    eye = lax.broadcasted_iota(jnp.int32, (n, n), 0) == lax.broadcasted_iota(jnp.int32, (n, n), 1)
    return jnp.sum(jnp.where(eye, row, 0.0), axis=1, keepdims=True)


def row_of(col):
    n = col.shape[0]
    eye = lax.broadcasted_iota(jnp.int32, (n, n), 0) == lax.broadcasted_iota(jnp.int32, (n, n), 1)
    return jnp.sum(jnp.where(eye, col, 0.0), axis=0, keepdims=True)


def kernel(
    dims, factor,
    q_hbm, lat_hbm, lse_hbm, qi_hbm, k_hbm, w_hbm,
    gq_ref, gw_ref, gk_ref,
    q_ref, lse_ref, qi_ref, w_ref, s_in,
    q_stage, i_stage, qbuf, ientry, ibuf, latbuf, kbuf, raw, wq, tacc, sacc, gbuf, masked,
    st_buf, part, ry_buf, zsum, fq_buf,
    ck_send, ck_recv, gx_sum, gx_send, gx_recv, gz_send, gz_recv, ga_buf,
    s_eq, s_ei, r_eq, r_ei, s_core, r_core, s_ck, r_ck, s_up, s_down, r_y,
    s_st, r_st, s_ry, r_ry, s_fq, r_fq, s_gx, r_gx, s_gz, r_gz, s_ga, r_ga,
):
    NZ, NY, NZH, NX = dims
    NH = NZH * NX
    ctx, head = lax.axis_index("ctx"), lax.axis_index("head")
    c = lax.rem(ctx, 2)
    y = lax.rem(lax.div(ctx, 2), NY)
    zl = lax.div(ctx, 2 * NY)
    x = lax.rem(head, NX)
    zh = lax.div(head, NX)
    rows, heads, width = q_ref.shape
    iheads, idim = qi_ref.shape[1:]
    nk = lat_hbm.shape[1]
    wide = qbuf.shape[-1]
    K2 = 2 * nk
    J = NH * iheads
    base = wide - 128
    tail = width - base
    scale = width ** -0.5
    inv_scale = width ** 0.5
    log2e = math.log2(math.e)
    own_plane = x == zl

    def ctx_of(zl_, y_, c_):
        return (zl_ * NY + y_) * 2 + c_

    def rcopy(src, dst, ssem, rsem, ctx_, head_):
        return pltpu.make_async_remote_copy(
            src_ref=src, dst_ref=dst, send_sem=ssem, recv_sem=rsem,
            device_id={"ctx": ctx_, "head": head_}, device_id_type=MESH,
        )

    def arrived(dst, rsem):
        pltpu.make_async_copy(dst, dst, rsem).wait()

    sends = []

    def send(*args):
        cp = rcopy(*args)
        cp.start()
        sends.append(cp.wait_send)

    def send_unless(local, src, dst, ssem, rsem, ctx_, head_):
        @pl.when(jnp.logical_not(local))
        def _():
            rcopy(src, dst, ssem, rsem, ctx_, head_).start()

        @pl.when(local)
        def _():
            pltpu.make_async_copy(src, dst, rsem).start()

        def finish():
            @pl.when(jnp.logical_not(local))
            def _():
                rcopy(src, dst, ssem, rsem, ctx_, head_).wait_send()

        sends.append(finish)

    y_peers = [lax.rem(y + d, NY) for d in range(1, NY)]
    z_peers = [lax.rem(zl + d, NZ) for d in range(1, NZ)]
    x_peers = [lax.rem(x + d, NX) for d in range(1, NX)]
    zls = [zl] + z_peers
    plane = [
        (ctx_of(lax.rem(zl + dz, NZ), lax.rem(y + dy, NY), c), lax.rem(zl + dz, NZ) * NY + lax.rem(y + dy, NY))
        for dy in sorted(range(NY), key=lambda d: -min(d, NY - d)) for dz in range(NZ) if dy or dz
    ]
    hs = [lax.rem(head + d, NH) for d in range(NH)]

    loads = [
        pltpu.make_async_copy(src, dst, s_in.at[n])
        for n, (src, dst) in enumerate((
            (q_hbm, q_ref), (lse_hbm, lse_ref), (qi_hbm, qi_ref), (w_hbm, w_ref),
            (k_hbm, kbuf.at[0]), (lat_hbm, latbuf.at[0, :width]),
        ))
    ]
    for cp in loads:
        cp.start()

    barrier = pltpu.get_barrier_semaphore()

    def greet(ctx_, head_):
        pl.semaphore_signal(barrier, inc=1, device_id={"ctx": ctx_, "head": head_}, device_id_type=MESH)

    for d, h in enumerate(hs):
        if d == 0:
            @pl.when(jnp.logical_not(own_plane))
            def _():
                greet(ctx_of(x, y, c), head)
        else:
            greet(ctx_of(x, y, c), h)
    for r in range(NZH):
        for d, z_ in enumerate(zls):
            if d == 0:
                @pl.when(jnp.logical_not(own_plane & (zh == r)))
                def _():
                    greet(ctx_of(zl, y, c), r * NX + zl)
            else:
                greet(ctx_of(z_, y, c), r * NX + zl)
    greet(ctx_of(zl, y, 1 - c), head)
    for p in plane:
        greet(p[0], head)
    for x_ in x_peers:
        greet(ctx, zh * NX + x_)
    greet(ctx, (1 - zh) * NX + x)
    n_greet = 1 + (NY * NZ - 1) + (NX - 1) + 1 + NH + NZH * NZ

    for cp in loads[:4]:
        cp.wait()
    lane = lax.broadcasted_iota(jnp.int32, (heads, 128), 1)
    for r in range(rows):
        t3 = list(split3(column(lse_ref[r : r + 1, :])))
        w3 = [jnp.concatenate([v, jnp.zeros((heads - iheads, 1), F32)], axis=0)
              for v in split3(column(w_ref[r : r + 1, :]))]
        aug = jnp.zeros((heads, 128), F32)
        for n, v in enumerate(t3 + w3):
            aug = jnp.where(lane == tail + n, v, aug)
        q_stage[r, :, :base] = q_ref[r, :, :base]
        last = jnp.concatenate([q_ref[r, :, base:].astype(F32), jnp.zeros((heads, 128 - tail), F32)], axis=1)
        q_stage[r, :, base:] = (last + aug).astype(BF16)
        i_stage[r] = jnp.concatenate(
            [qi_ref[r].astype(F32), jnp.zeros((heads - iheads, idim), F32)], axis=0
        ).astype(BF16)
    krow = lax.broadcasted_iota(jnp.int32, (wide - width, nk), 0)
    for side in range(2):
        latbuf[side, width:] = jnp.where(krow < 3, -inv_scale, 0.0).astype(BF16)
    for cp in loads[4:]:
        cp.wait()

    pl.semaphore_wait(barrier, jnp.where(own_plane, n_greet - 2, n_greet))

    for r in (1 - zh, zh) if NZH == 2 else range(NZH):
        for d, z_ in enumerate(zls):
            to = (ctx_of(z_, y, c), r * NX + zl)
            iargs = (i_stage.at[r], ientry.at[head], s_ei.at[r, d], r_ei.at[head], *to)
            qargs = (q_stage.at[r], qbuf.at[y, head], s_eq.at[r, d], r_eq.at[head], *to)
            if d == 0:
                send_unless(own_plane & (zh == r), *iargs)
                send_unless(own_plane & (zh == r), *qargs)
            else:
                send(*iargs)
                send(*qargs)
    other = ctx_of(zl, y, 1 - c)
    send(kbuf.at[0], kbuf.at[1], s_core.at[0], r_core.at[0], other, head)
    send(latbuf.at[0, :width], latbuf.at[1, :width], s_core.at[1], r_core.at[1], other, head)

    NC = NH // 2
    up, down = lax.rem(y + 1, NY), lax.rem(y + NY - 1, NY)
    far = NY // 2
    near = far - 1
    order = [lax.rem(zh * (NC // 2) + n, NC) for n in range(NC)]
    order.insert(NC // 2, NC)

    def piece(y0, n):
        return ibuf.at[y0] if n is NC else qbuf.at[y0, pl.ds(2 * n, 2)]

    def forward(y0, k, step, plus, minus):
        n = order[k]
        if plus:
            send(piece(y0, n), piece(y0, n), s_up.at[step, k], r_y.at[y0, n], ctx_of(zl, up, c), head)
        if minus:
            send(piece(y0, n), piece(y0, n), s_down.at[step, k], r_y.at[y0, n], ctx_of(zl, down, c), head)

    def by_up(k):
        return k <= NC // 2

    for k, n in enumerate(order):
        if n is NC:
            for h in range(NH):
                arrived(ientry.at[h], r_ei.at[h])
            ibuf[y] = ientry[...].astype(F32)[:, :iheads, :].reshape(J, idim).astype(BF16)
        else:
            for h in (2 * n, 2 * n + 1):
                arrived(qbuf.at[y, h], r_eq.at[h])
        forward(y, k, 0, near > 0 or by_up(k), near > 0 or not by_up(k))

    CH = min(512, nk)

    def block(y0):
        q = qbuf[y0].reshape(NH * heads, wide)
        qi = ibuf[y0]
        aug = qbuf[y0, :, :, base:].astype(F32).reshape(NH * heads, 128)
        ln = lax.broadcasted_iota(jnp.int32, aug.shape, 1)
        wide_col = jnp.sum(jnp.where((ln >= tail + 3) & (ln < tail + 6), aug, 0.0), axis=1, keepdims=True)
        wcol = wide_col.reshape(NH, heads, 1)[:, :iheads, :].reshape(J, 1)
        wq[y0] = (qi.astype(F32) * wcol).astype(BF16)
        for side in range(2):
            for n in range(nk // CH):
                cols = slice(n * CH, (n + 1) * CH)
                kcols = slice(side * nk + n * CH, side * nk + (n + 1) * CH)
                s = jnp.dot(q, latbuf[side, :, cols], preferred_element_type=F32)
                e = jnp.exp2(s * (scale * log2e))
                tacc[y0, :, kcols] = jnp.sum(e.reshape(NH * heads // 8, 8, CH), axis=0)
                rw = lax.dot_general(qi, kbuf[side, cols, :], NT, preferred_element_type=F32)
                raw[y0, :, kcols] = rw
                sacc[y0, :, kcols] = jnp.sum((wcol * jnp.maximum(rw, 0.0)).reshape(J // 8, 8, CH), axis=0)

    arrived(kbuf.at[1], r_core.at[0])
    arrived(latbuf.at[1, :width], r_core.at[1])
    block(y)
    for step in range(1, near + 1):
        yu = lax.rem(y + NY - step, NY)
        yd = lax.rem(y + step, NY)
        for k, n in enumerate(order):
            arrived(piece(yu, n), r_y.at[yu, n])
            forward(yu, k, step, step < near or by_up(k), False)
            arrived(piece(yd, n), r_y.at[yd, n])
            forward(yd, k, step, False, step < near or not by_up(k))
        block(yu)
        block(yd)
    yf = lax.rem(y + far, NY)
    for n in order:
        arrived(piece(yf, n), r_y.at[yf, n])
    block(yf)

    target = jnp.sum(tacc[...], axis=1)
    score = jnp.sum(sacc[...], axis=1)
    m = jnp.max(score, axis=1, keepdims=True)
    l = jnp.sum(jnp.exp(score - m), axis=1, keepdims=True)
    t = jnp.sum(target, axis=1, keepdims=True)
    sl = lax.broadcasted_iota(jnp.int32, (NY, 128), 1)
    ss = lax.broadcasted_iota(jnp.int32, (NY, 128), 0)
    at = [sl == ss + n * NY for n in range(3)]
    me = zl * NY + y
    mine = jnp.where(at[0], m, jnp.where(at[1], l, jnp.where(at[2], t, 0.0)))
    st_buf[pl.ds(me, 1), :] = jnp.sum(mine, axis=0, keepdims=True)
    for n, (dev, _) in enumerate(plane):
        send(st_buf.at[pl.ds(me, 1)], st_buf.at[pl.ds(me, 1)], s_st.at[n], r_st.at[me], dev, head)
    wqt = wq[...].reshape(NY * J, idim).astype(F32).T.astype(BF16)
    for _, slot in plane:
        arrived(st_buf.at[pl.ds(slot, 1)], r_st.at[slot])
    stats = st_buf[...]
    peak = pltpu.roll(stats, NY, 1)
    top = jnp.max(peak, axis=0, keepdims=True)
    in_l = lax.broadcasted_iota(jnp.int32, stats.shape, 1) // NY == 1
    mass = jnp.sum(jnp.where(in_l, stats * jnp.exp(jnp.where(in_l, peak - top, 0.0)), stats), axis=0, keepdims=True)
    m = jnp.sum(jnp.where(at[1], top, 0.0), axis=1, keepdims=True)
    l = jnp.sum(jnp.where(at[1], mass, 0.0), axis=1, keepdims=True)
    t = jnp.sum(jnp.where(at[2], mass, 0.0), axis=1, keepdims=True)
    grad = factor * (jnp.exp(score - m) / l - target / t)
    gbuf[...] = grad.astype(BF16).astype(F32)

    nc = nk // KC
    nq = nc // NX

    def mask(side, q):
        cols = slice(q * nc, (q + 1) * nc)
        kcols = slice(side * nk + q * nc, side * nk + (q + 1) * nc)
        for y0 in range(NY):
            g = jnp.where(raw[y0, :, kcols] > 0, gbuf[y0 : y0 + 1, kcols], 0.0)
            masked[side, y0 * J : (y0 + 1) * J, cols] = g.astype(BF16)
        return jnp.dot(wqt, masked[side, :, cols], preferred_element_type=F32)

    for q in range(KC):
        ck_send[q] = mask(1, q).astype(BF16)
        send(ck_send.at[q], ck_recv.at[q], s_ck.at[q], r_ck.at[q], other, head)
    for q in range(KC):
        own_key = mask(0, q)
        arrived(ck_recv.at[q], r_ck.at[q])
        own_key = own_key + ck_recv[q].astype(F32)
        for n in range(NX):
            gx_sum[q, n] = own_key[:, n * nq : (n + 1) * nq]
            gx_send[q, n] = own_key[:, n * nq : (n + 1) * nq].astype(BF16)
        for n, x_ in enumerate(x_peers):
            send(gx_send.at[q, x_], gx_recv.at[q, x], s_gx.at[q, n], r_gx.at[q, x], ctx, zh * NX + x_)

    part[...] = (
        jnp.dot(masked[0], kbuf[0], preferred_element_type=F32)
        + jnp.dot(masked[1], kbuf[1], preferred_element_type=F32)
    ).reshape(part.shape).astype(part.dtype)
    for n, y_ in enumerate(y_peers):
        send(part.at[y_], ry_buf.at[y], s_ry.at[n], r_ry.at[y], ctx_of(zl, y_, c), head)

    for q in range(KC):
        gsum = gx_sum[q, x]
        for x_ in x_peers:
            arrived(gx_recv.at[q, x_], r_gx.at[q, x_])
            gsum = gsum + gx_recv[q, x_].astype(F32)
        gz_send[q] = gsum.astype(BF16)
        send(gz_send.at[q], gz_recv.at[q], s_gz.at[q], r_gz.at[q], ctx, (1 - zh) * NX + x)

    total = part[y].astype(F32)
    for y_ in y_peers:
        arrived(ry_buf.at[y_], r_ry.at[y_])
        total = total + ry_buf[y_].astype(F32)
    zsum[...] = total.reshape(zsum.shape)
    slot = zh * NZ + zl
    for d, h in enumerate(hs):
        args = (zsum.at[h], fq_buf.at[slot], s_fq.at[d], r_fq.at[slot], ctx_of(x, y, c), h)
        if d == 0:
            send_unless(own_plane, *args)
        else:
            send(*args)

    for q in range(KC):
        arrived(gz_recv.at[q], r_gz.at[q])
        ga_buf[q, x] = (gz_send[q].astype(F32) + gz_recv[q].astype(F32)).T.astype(BF16)
        for n, x_ in enumerate(x_peers):
            send(ga_buf.at[q, x], ga_buf.at[q, x], s_ga.at[q, n], r_ga.at[q, x], ctx, zh * NX + x_)

    for n in range(NZH * NZ):
        arrived(fq_buf.at[n], r_fq.at[n])
    for r in range(rows):
        own = jnp.sum(fq_buf[r * NZ : (r + 1) * NZ], axis=0)
        gq_ref[r] = own * column(w_ref[r : r + 1, :])
        gw_ref[r : r + 1, :] = row_of(jnp.sum(own * qi_ref[r].astype(F32), axis=1, keepdims=True))

    for q in range(KC):
        for x_ in x_peers:
            arrived(ga_buf.at[q, x_], r_ga.at[q, x_])
    gk_ref[...] = ga_buf[...].astype(F32).reshape(gk_ref.shape)

    for finish in sends:
        finish()


def body(dims, keys, q_attn, latent, lse_saved, q_index, k_index, head_weight):
    NZ, NY, NZH, NX = dims
    NH = NZH * NX
    rows, heads, width = q_attn.shape
    iheads, idim = q_index.shape[1:]
    nk = latent.shape[0]
    wide = -(-width // 128) * 128
    J = NH * iheads
    K2 = 2 * nk
    nq = nk // NX // KC
    NP = NH // 2 + 1
    V, DMA = pltpu.VMEM, pltpu.SemaphoreType.DMA
    vm = pl.BlockSpec(memory_space=pltpu.VMEM)
    scratch = [
        V((rows, heads, width), BF16), V((rows, heads), F32), V((rows, iheads, idim), BF16), V((rows, iheads), F32), DMA((6,)),
        V((rows, heads, wide), BF16), V((rows, heads, idim), BF16),
        V((NY, NH, heads, wide), BF16), V((NH, heads, idim), BF16), V((NY, J, idim), BF16),
        V((2, wide, nk), BF16), V((2, nk, idim), BF16),
        V((NY, J, K2), F32), V((NY, J, idim), BF16),
        V((NY, 8, K2), F32), V((NY, 8, K2), F32), V((NY, K2), F32), V((2, NY * J, nk), BF16),
        V((NZ * NY, 128), F32),
        V((NY, J, idim), BF16), V((NY, J, idim), BF16),
        V((NH, iheads, idim), F32), V((NZH * NZ, iheads, idim), F32),
        V((KC, idim, nk // KC), BF16), V((KC, idim, nk // KC), BF16),
        V((KC, NX, idim, nq), F32), V((KC, NX, idim, nq), BF16), V((KC, NX, idim, nq), BF16),
        V((KC, idim, nq), BF16), V((KC, idim, nq), BF16), V((KC, NX, nq, idim), BF16),
        DMA((rows, NZ)), DMA((rows, NZ)), DMA((NH,)), DMA((NH,)), DMA((2,)), DMA((2,)), DMA((KC,)), DMA((KC,)),
        DMA((NY, NP)), DMA((NY, NP)), DMA((NY, NP)),
        DMA((NZ * NY,)), DMA((NZ * NY,)), DMA((NY,)), DMA((NY,)), DMA((NH,)), DMA((NZH * NZ,)),
        DMA((KC, NX)), DMA((KC, NX)), DMA((KC,)), DMA((KC,)), DMA((KC, NX)), DMA((KC, NX)),
    ]
    return pl.pallas_call(
        functools.partial(kernel, dims, keys / 32.0),
        out_shape=(
            jax.ShapeDtypeStruct((rows, iheads, idim), F32),
            jax.ShapeDtypeStruct((rows, iheads), F32),
            jax.ShapeDtypeStruct((nk, idim), F32),
        ),
        in_specs=[pl.BlockSpec(memory_space=pl.ANY)] * 6,
        out_specs=(vm, vm, vm),
        scratch_shapes=scratch,
        compiler_params=pltpu.CompilerParams(
            collective_id=0, has_side_effects=True, vmem_limit_bytes=56 * 1024 * 1024
        ),
        name="indexer_backward",
    )(q_attn, latent.T, lse_saved, q_index, k_index, head_weight)


def build(mesh, dims, keys):
    return jax.shard_map(
        functools.partial(body, dims, keys),
        mesh=mesh,
        in_specs=(
            P("ctx", "head", None),
            P("ctx", None),
            P("ctx", "head"),
            P("ctx", "head", None),
            P("ctx", None),
            P("ctx", "head"),
        ),
        out_specs=(P("ctx", "head", None), P("ctx", "head"), P("ctx", None)),
        check_vma=False,
    )


def solution(mesh):
    return build(mesh, DIMS, 65536)
```

```python
import functools
import math

import jax
import jax.numpy as jnp
from jax import lax
from jax.experimental import pallas as pl
from jax.experimental.pallas import tpu as pltpu
from jax.sharding import PartitionSpec as P

MESH = pl.DeviceIdType.MESH
F32, BF16 = jnp.float32, jnp.bfloat16
DIMS = (4, 8, 2, 4)
KC = 2
HC = 2
NT = (((1,), (1,)), ((), ()))


def split3(v):
    hi = v.astype(BF16).astype(F32)
    mid = (v - hi).astype(BF16).astype(F32)
    return hi, mid, v - hi - mid


def column(row):
    n = row.shape[1]
    eye = lax.broadcasted_iota(jnp.int32, (n, n), 0) == lax.broadcasted_iota(jnp.int32, (n, n), 1)
    return jnp.sum(jnp.where(eye, row, 0.0), axis=1, keepdims=True)


def row_of(col):
    n = col.shape[0]
    eye = lax.broadcasted_iota(jnp.int32, (n, n), 0) == lax.broadcasted_iota(jnp.int32, (n, n), 1)
    return jnp.sum(jnp.where(eye, col, 0.0), axis=0, keepdims=True)


def kernel(
    dims, factor,
    q_hbm, lat_hbm, lse_hbm, qi_hbm, k_hbm, w_hbm,
    gq_ref, gw_ref, gk_ref,
    q_ref, lse_ref, qi_ref, w_ref, s_in,
    q_stage, i_stage, qbuf, ientry, ibuf, latbuf, kbuf, keep, wq, tacc, sacc, gbuf, masked,
    st_buf, part, ry_buf, zsum, fq_buf,
    ck_send, ck_recv, gx_sum, gx_send, gx_recv, gz_send, gz_recv, ga_buf,
    s_eq, s_ei, r_eq, r_ei, s_core, r_core, s_ck, r_ck, s_up, s_down, r_y,
    s_st, r_st, s_ry, r_ry, s_fq, r_fq, s_gx, r_gx, s_gz, r_gz, s_ga, r_ga,
):
    NZ, NY, NZH, NX = dims
    NH = NZH * NX
    ctx, head = lax.axis_index("ctx"), lax.axis_index("head")
    c = lax.rem(ctx, 2)
    y = lax.rem(lax.div(ctx, 2), NY)
    zl = lax.div(ctx, 2 * NY)
    x = lax.rem(head, NX)
    zh = lax.div(head, NX)
    rows, heads, width = q_ref.shape
    iheads, idim = qi_ref.shape[1:]
    nk = lat_hbm.shape[1]
    wide = qbuf.shape[-1]
    K2 = 2 * nk
    J = NH * iheads
    base = wide - 128
    tail = width - base
    scale = width ** -0.5
    inv_scale = width ** 0.5
    log2e = math.log2(math.e)
    own_plane = x == zl

    def ctx_of(zl_, y_, c_):
        return (zl_ * NY + y_) * 2 + c_

    def rcopy(src, dst, ssem, rsem, ctx_, head_):
        return pltpu.make_async_remote_copy(
            src_ref=src, dst_ref=dst, send_sem=ssem, recv_sem=rsem,
            device_id={"ctx": ctx_, "head": head_}, device_id_type=MESH,
        )

    def arrived(dst, rsem):
        pltpu.make_async_copy(dst, dst, rsem).wait()

    sends = []

    def send(*args):
        cp = rcopy(*args)
        cp.start()
        sends.append(cp.wait_send)

    def send_unless(local, src, dst, ssem, rsem, ctx_, head_):
        @pl.when(jnp.logical_not(local))
        def _():
            rcopy(src, dst, ssem, rsem, ctx_, head_).start()

        @pl.when(local)
        def _():
            pltpu.make_async_copy(src, dst, rsem).start()

        def finish():
            @pl.when(jnp.logical_not(local))
            def _():
                rcopy(src, dst, ssem, rsem, ctx_, head_).wait_send()

        sends.append(finish)

    y_peers = [lax.rem(y + d, NY) for d in range(1, NY)]
    z_peers = [lax.rem(zl + d, NZ) for d in range(1, NZ)]
    x_peers = [lax.rem(x + d, NX) for d in range(1, NX)]
    zls = [zl] + z_peers
    plane = [
        (ctx_of(lax.rem(zl + dz, NZ), lax.rem(y + dy, NY), c), lax.rem(zl + dz, NZ) * NY + lax.rem(y + dy, NY))
        for dy in sorted(range(NY), key=lambda d: -min(d, NY - d)) for dz in range(NZ) if dy or dz
    ]
    hs = [lax.rem(head + d, NH) for d in range(NH)]

    loads = [
        pltpu.make_async_copy(src, dst, s_in.at[n])
        for n, (src, dst) in enumerate((
            (q_hbm, q_ref), (lse_hbm, lse_ref), (qi_hbm, qi_ref), (w_hbm, w_ref),
            (k_hbm, kbuf.at[0]), (lat_hbm, latbuf.at[0, :width]),
        ))
    ]
    for cp in loads:
        cp.start()

    barrier = pltpu.get_barrier_semaphore()

    def greet(ctx_, head_):
        pl.semaphore_signal(barrier, inc=1, device_id={"ctx": ctx_, "head": head_}, device_id_type=MESH)

    for d, h in enumerate(hs):
        if d == 0:
            @pl.when(jnp.logical_not(own_plane))
            def _():
                greet(ctx_of(x, y, c), head)
        else:
            greet(ctx_of(x, y, c), h)
    for r in range(NZH):
        for d, z_ in enumerate(zls):
            if d == 0:
                @pl.when(jnp.logical_not(own_plane & (zh == r)))
                def _():
                    greet(ctx_of(zl, y, c), r * NX + zl)
            else:
                greet(ctx_of(z_, y, c), r * NX + zl)
    greet(ctx_of(zl, y, 1 - c), head)
    for p in plane:
        greet(p[0], head)
    for x_ in x_peers:
        greet(ctx, zh * NX + x_)
    greet(ctx, (1 - zh) * NX + x)
    n_greet = 1 + (NY * NZ - 1) + (NX - 1) + 1 + NH + NZH * NZ

    for cp in loads[:4]:
        cp.wait()
    lane = lax.broadcasted_iota(jnp.int32, (heads, 128), 1)
    for r in range(rows):
        t3 = list(split3(column(lse_ref[r : r + 1, :])))
        w3 = [jnp.concatenate([v, jnp.zeros((heads - iheads, 1), F32)], axis=0)
              for v in split3(column(w_ref[r : r + 1, :]))]
        aug = jnp.zeros((heads, 128), F32)
        for n, v in enumerate(t3 + w3):
            aug = jnp.where(lane == tail + n, v, aug)
        q_stage[r, :, :base] = q_ref[r, :, :base]
        last = jnp.concatenate([q_ref[r, :, base:].astype(F32), jnp.zeros((heads, 128 - tail), F32)], axis=1)
        q_stage[r, :, base:] = (last + aug).astype(BF16)
        i_stage[r] = jnp.concatenate(
            [qi_ref[r].astype(F32), jnp.zeros((heads - iheads, idim), F32)], axis=0
        ).astype(BF16)
    krow = lax.broadcasted_iota(jnp.int32, (wide - width, nk), 0)
    for side in range(2):
        latbuf[side, width:] = jnp.where(krow < 3, -inv_scale, 0.0).astype(BF16)
    pl.semaphore_wait(barrier, jnp.where(own_plane, n_greet - 2, n_greet))

    for r in (1 - zh, zh) if NZH == 2 else range(NZH):
        for d, z_ in enumerate(zls):
            to = (ctx_of(z_, y, c), r * NX + zl)
            iargs = (i_stage.at[r], ientry.at[head], s_ei.at[r, d], r_ei.at[head], *to)
            qargs = (q_stage.at[r], qbuf.at[y, head], s_eq.at[r, d], r_eq.at[head], *to)
            if d == 0:
                send_unless(own_plane & (zh == r), *iargs)
                send_unless(own_plane & (zh == r), *qargs)
            else:
                send(*iargs)
                send(*qargs)
    other = ctx_of(zl, y, 1 - c)
    for cp in loads[4:]:
        cp.wait()
    send(kbuf.at[0], kbuf.at[1], s_core.at[0], r_core.at[0], other, head)
    send(latbuf.at[0, :width], latbuf.at[1, :width], s_core.at[1], r_core.at[1], other, head)

    NC = NH // HC
    up, down = lax.rem(y + 1, NY), lax.rem(y + NY - 1, NY)
    far = NY // 2
    near = far - 1
    order = [lax.rem(zh * (NC // 2) + n, NC) for n in range(NC)]
    order.insert(NC // 2, NC)

    def piece(y0, n):
        return ibuf.at[y0] if n is NC else qbuf.at[y0, pl.ds(HC * n, HC)]

    def forward(y0, k, step, plus, minus):
        n = order[k]
        if plus:
            send(piece(y0, n), piece(y0, n), s_up.at[step, k], r_y.at[y0, n], ctx_of(zl, up, c), head)
        if minus:
            send(piece(y0, n), piece(y0, n), s_down.at[step, k], r_y.at[y0, n], ctx_of(zl, down, c), head)

    def by_up(k):
        return k <= NC // 2

    for k, n in enumerate(order):
        if n is NC:
            for h in range(NH):
                arrived(ientry.at[h], r_ei.at[h])
            ibuf[y] = ientry[...].astype(F32)[:, :iheads, :].reshape(J, idim).astype(BF16)
        else:
            for h in range(HC):
                arrived(qbuf.at[y, HC * n + h], r_eq.at[HC * n + h])
        forward(y, k, 0, near > 0 or by_up(k), near > 0 or not by_up(k))

    CH = min(512, nk)

    def block(y0):
        q = qbuf[y0].reshape(NH * heads, wide)
        qi = ibuf[y0]
        aug = qbuf[y0, :, :, base:].astype(F32).reshape(NH * heads, 128)
        ln = lax.broadcasted_iota(jnp.int32, aug.shape, 1)
        wide_col = jnp.sum(jnp.where((ln >= tail + 3) & (ln < tail + 6), aug, 0.0), axis=1, keepdims=True)
        wcol = wide_col.reshape(NH, heads, 1)[:, :iheads, :].reshape(J, 1)
        wq[y0] = (qi.astype(F32) * wcol).astype(BF16)
        for side in range(2):
            for n in range(nk // CH):
                cols = slice(n * CH, (n + 1) * CH)
                kcols = slice(side * nk + n * CH, side * nk + (n + 1) * CH)
                s = jnp.dot(q, latbuf[side, :, cols], preferred_element_type=F32)
                e = jnp.exp2(s * (scale * log2e))
                tacc[y0, :, kcols] = jnp.sum(e.reshape(NH * heads // 8, 8, CH), axis=0)
                rw = lax.dot_general(qi, kbuf[side, cols, :], NT, preferred_element_type=F32)
                keep[y0, :, kcols] = jnp.where(rw > 0, 1.0, 0.0).astype(BF16)
                sacc[y0, :, kcols] = jnp.sum((wcol * jnp.maximum(rw, 0.0)).reshape(J // 8, 8, CH), axis=0)

    arrived(kbuf.at[1], r_core.at[0])
    arrived(latbuf.at[1, :width], r_core.at[1])
    block(y)
    for step in range(1, near + 1):
        yu = lax.rem(y + NY - step, NY)
        yd = lax.rem(y + step, NY)
        for k, n in enumerate(order):
            arrived(piece(yu, n), r_y.at[yu, n])
            forward(yu, k, step, step < near or by_up(k), False)
            arrived(piece(yd, n), r_y.at[yd, n])
            forward(yd, k, step, False, step < near or not by_up(k))
        block(yu)
        block(yd)
    yf = lax.rem(y + far, NY)
    for n in order:
        arrived(piece(yf, n), r_y.at[yf, n])
    block(yf)

    target = jnp.sum(tacc[...], axis=1)
    score = jnp.sum(sacc[...], axis=1)
    m = jnp.max(score, axis=1, keepdims=True)
    l = jnp.sum(jnp.exp(score - m), axis=1, keepdims=True)
    t = jnp.sum(target, axis=1, keepdims=True)
    sl = lax.broadcasted_iota(jnp.int32, (NY, 128), 1)
    ss = lax.broadcasted_iota(jnp.int32, (NY, 128), 0)
    at = [sl == ss + n * NY for n in range(3)]
    me = zl * NY + y
    mine = jnp.where(at[0], m, jnp.where(at[1], l, jnp.where(at[2], t, 0.0)))
    st_buf[pl.ds(me, 1), :] = jnp.sum(mine, axis=0, keepdims=True)
    for n, (dev, _) in enumerate(plane):
        send(st_buf.at[pl.ds(me, 1)], st_buf.at[pl.ds(me, 1)], s_st.at[n], r_st.at[me], dev, head)
    wqt = wq[...].reshape(NY * J, idim).astype(F32).T.astype(BF16)
    for _, slot in plane:
        arrived(st_buf.at[pl.ds(slot, 1)], r_st.at[slot])
    stats = st_buf[...]
    peak = pltpu.roll(stats, NY, 1)
    top = jnp.max(peak, axis=0, keepdims=True)
    in_l = lax.broadcasted_iota(jnp.int32, stats.shape, 1) // NY == 1
    mass = jnp.sum(jnp.where(in_l, stats * jnp.exp(jnp.where(in_l, peak - top, 0.0)), stats), axis=0, keepdims=True)
    m = jnp.sum(jnp.where(at[1], top, 0.0), axis=1, keepdims=True)
    l = jnp.sum(jnp.where(at[1], mass, 0.0), axis=1, keepdims=True)
    t = jnp.sum(jnp.where(at[2], mass, 0.0), axis=1, keepdims=True)
    grad = factor * (jnp.exp(score - m) / l - target / t)
    gbuf[...] = grad

    nc = nk // KC
    nq = nc // NX

    def mask(side, q):
        cols = slice(q * nc, (q + 1) * nc)
        kcols = slice(side * nk + q * nc, side * nk + (q + 1) * nc)
        for y0 in range(NY):
            g = jnp.broadcast_to(gbuf[y0 : y0 + 1, kcols], (16, nc)).astype(BF16)
            g = keep[y0, :, kcols].reshape(J // 16, 16, nc) * g[None]
            masked[side, y0 * J : (y0 + 1) * J, cols] = g.reshape(J, nc)
        return jnp.dot(wqt, masked[side, :, cols], preferred_element_type=F32)

    for q in range(KC):
        ck_send[q] = mask(1, q).astype(BF16)
        send(ck_send.at[q], ck_recv.at[q], s_ck.at[q], r_ck.at[q], other, head)
    for q in range(KC):
        own_key = mask(0, q)
        arrived(ck_recv.at[q], r_ck.at[q])
        own_key = own_key + ck_recv[q].astype(F32)
        for n in range(NX):
            gx_sum[q, n] = own_key[:, n * nq : (n + 1) * nq]
            gx_send[q, n] = own_key[:, n * nq : (n + 1) * nq].astype(BF16)
        for n, x_ in enumerate(x_peers):
            send(gx_send.at[q, x_], gx_recv.at[q, x], s_gx.at[q, n], r_gx.at[q, x], ctx, zh * NX + x_)

    part[...] = (
        jnp.dot(masked[0], kbuf[0], preferred_element_type=F32)
        + jnp.dot(masked[1], kbuf[1], preferred_element_type=F32)
    ).reshape(part.shape).astype(part.dtype)
    for n, y_ in enumerate(y_peers):
        send(part.at[y_], ry_buf.at[y], s_ry.at[n], r_ry.at[y], ctx_of(zl, y_, c), head)

    for q in range(KC):
        gsum = gx_sum[q, x]
        for x_ in x_peers:
            arrived(gx_recv.at[q, x_], r_gx.at[q, x_])
            gsum = gsum + gx_recv[q, x_].astype(F32)
        gz_send[q] = gsum.astype(BF16)
        send(gz_send.at[q], gz_recv.at[q], s_gz.at[q], r_gz.at[q], ctx, (1 - zh) * NX + x)

    total = part[y].astype(F32)
    for y_ in y_peers:
        arrived(ry_buf.at[y_], r_ry.at[y_])
        total = total + ry_buf[y_].astype(F32)
    zsum[...] = total.reshape(zsum.shape)
    slot = zh * NZ + zl
    for d, h in enumerate(hs):
        args = (zsum.at[h], fq_buf.at[slot], s_fq.at[d], r_fq.at[slot], ctx_of(x, y, c), h)
        if d == 0:
            send_unless(own_plane, *args)
        else:
            send(*args)

    for q in range(KC):
        arrived(gz_recv.at[q], r_gz.at[q])
        ga_buf[q, x] = (gz_send[q].astype(F32) + gz_recv[q].astype(F32)).T.astype(BF16)
        for n, x_ in enumerate(x_peers):
            send(ga_buf.at[q, x], ga_buf.at[q, x], s_ga.at[q, n], r_ga.at[q, x], ctx, zh * NX + x_)

    for n in range(NZH * NZ):
        arrived(fq_buf.at[n], r_fq.at[n])
    for r in range(rows):
        own = jnp.sum(fq_buf[r * NZ : (r + 1) * NZ], axis=0)
        gq_ref[r] = own * column(w_ref[r : r + 1, :])
        gw_ref[r : r + 1, :] = row_of(jnp.sum(own * qi_ref[r].astype(F32), axis=1, keepdims=True))

    for q in range(KC):
        for x_ in x_peers:
            arrived(ga_buf.at[q, x_], r_ga.at[q, x_])
    gk_ref[...] = ga_buf[...].astype(F32).reshape(gk_ref.shape)

    for finish in sends:
        finish()


def body(dims, keys, q_attn, latent, lse_saved, q_index, k_index, head_weight):
    NZ, NY, NZH, NX = dims
    NH = NZH * NX
    rows, heads, width = q_attn.shape
    iheads, idim = q_index.shape[1:]
    nk = latent.shape[0]
    wide = -(-width // 128) * 128
    J = NH * iheads
    K2 = 2 * nk
    nq = nk // NX // KC
    NP = NH // HC + 1
    V, DMA = pltpu.VMEM, pltpu.SemaphoreType.DMA
    vm = pl.BlockSpec(memory_space=pltpu.VMEM)
    scratch = [
        V((rows, heads, width), BF16), V((rows, heads), F32), V((rows, iheads, idim), BF16), V((rows, iheads), F32), DMA((6,)),
        V((rows, heads, wide), BF16), V((rows, heads, idim), BF16),
        V((NY, NH, heads, wide), BF16), V((NH, heads, idim), BF16), V((NY, J, idim), BF16),
        V((2, wide, nk), BF16), V((2, nk, idim), BF16),
        V((NY, J, K2), BF16), V((NY, J, idim), BF16),
        V((NY, 8, K2), F32), V((NY, 8, K2), F32), V((NY, K2), F32), V((2, NY * J, nk), BF16),
        V((NZ * NY, 128), F32),
        V((NY, J, idim), BF16), V((NY, J, idim), BF16),
        V((NH, iheads, idim), F32), V((NZH * NZ, iheads, idim), F32),
        V((KC, idim, nk // KC), BF16), V((KC, idim, nk // KC), BF16),
        V((KC, NX, idim, nq), F32), V((KC, NX, idim, nq), BF16), V((KC, NX, idim, nq), BF16),
        V((KC, idim, nq), BF16), V((KC, idim, nq), BF16), V((KC, NX, nq, idim), BF16),
        DMA((rows, NZ)), DMA((rows, NZ)), DMA((NH,)), DMA((NH,)), DMA((2,)), DMA((2,)), DMA((KC,)), DMA((KC,)),
        DMA((NY, NP)), DMA((NY, NP)), DMA((NY, NP)),
        DMA((NZ * NY,)), DMA((NZ * NY,)), DMA((NY,)), DMA((NY,)), DMA((NH,)), DMA((NZH * NZ,)),
        DMA((KC, NX)), DMA((KC, NX)), DMA((KC,)), DMA((KC,)), DMA((KC, NX)), DMA((KC, NX)),
    ]
    shapes = (
        jax.ShapeDtypeStruct((rows, iheads, idim), F32),
        jax.ShapeDtypeStruct((rows, iheads), F32),
        jax.ShapeDtypeStruct((nk, idim), F32),
    )
    outs = pl.pallas_call(
        functools.partial(kernel, dims, keys / 32.0),
        out_shape=shapes,
        in_specs=[pl.BlockSpec(memory_space=pl.ANY)] * 6,
        out_specs=(vm, vm, vm),
        scratch_shapes=scratch,
        compiler_params=pltpu.CompilerParams(
            collective_id=0, has_side_effects=True, vmem_limit_bytes=56 * 1024 * 1024
        ),
        name="indexer_backward",
    )(q_attn, latent.T, lse_saved, q_index, k_index, head_weight)
    return pl.pallas_call(
        store,
        out_shape=shapes,
        in_specs=[vm] * 3,
        out_specs=tuple(pl.BlockSpec(memory_space=pl.ANY) for _ in shapes),
        scratch_shapes=[DMA((3,))],
        compiler_params=pltpu.CompilerParams(vmem_limit_bytes=58 * 1024 * 1024),
        name="store_results",
    )(*outs)


def store(a_ref, b_ref, c_ref, a_out, b_out, c_out, sems):
    copies = [
        pltpu.make_async_copy(src, dst, sems.at[n])
        for n, (src, dst) in enumerate(((a_ref, a_out), (b_ref, b_out), (c_ref, c_out)))
    ]
    for cp in copies:
        cp.start()
    for cp in copies:
        cp.wait()


def build(mesh, dims, keys):
    return jax.shard_map(
        functools.partial(body, dims, keys),
        mesh=mesh,
        in_specs=(
            P("ctx", "head", None),
            P("ctx", None),
            P("ctx", "head"),
            P("ctx", "head", None),
            P("ctx", None),
            P("ctx", "head"),
        ),
        out_specs=(P("ctx", "head", None), P("ctx", "head"), P("ctx", None)),
        check_vma=False,
    )


def solution(mesh):
    return build(mesh, DIMS, 65536)
```

```python
import functools
import math

import jax
import jax.numpy as jnp
from jax import lax
from jax.experimental import pallas as pl
from jax.experimental.pallas import tpu as pltpu
from jax.sharding import PartitionSpec as P

MESH = pl.DeviceIdType.MESH
F32, BF16 = jnp.float32, jnp.bfloat16
DIMS = (4, 8, 2, 4)
KC = 2
HC = 2
NT = (((1,), (1,)), ((), ()))


def column(row):
    n = row.shape[1]
    eye = lax.broadcasted_iota(jnp.int32, (n, n), 0) == lax.broadcasted_iota(jnp.int32, (n, n), 1)
    return jnp.sum(jnp.where(eye, row, 0.0), axis=1, keepdims=True)


def row_of(col):
    n = col.shape[0]
    eye = lax.broadcasted_iota(jnp.int32, (n, n), 0) == lax.broadcasted_iota(jnp.int32, (n, n), 1)
    return jnp.sum(jnp.where(eye, col, 0.0), axis=0, keepdims=True)


def kernel(
    dims, factor,
    q_hbm, lat_hbm, lse_hbm, qi_hbm, k_hbm, w_hbm,
    gq_hbm, gw_hbm, gk_hbm,
    gq_ref, gw_ref, gk_ref, s_out,
    q_ref, lse_ref, qi_ref, w_ref, s_in,
    q_stage, a_stage, qbuf, abuf, latbuf, kbuf, keep, wq, tacc, sacc, gbuf, masked,
    st_buf, part, ry_buf, zsum, fq_buf,
    ck_send, ck_recv, gx_sum, gx_send, gx_recv, gz_send, gz_recv, ga_buf,
    s_eq, s_ea, r_eq, r_ea, s_core, r_core, s_ck, r_ck, s_up, s_down, r_y,
    s_st, r_st, s_ry, r_ry, s_fq, r_fq, s_gx, r_gx, s_gz, r_gz, s_ga, r_ga,
):
    NZ, NY, NZH, NX = dims
    NH = NZH * NX
    ctx, head = lax.axis_index("ctx"), lax.axis_index("head")
    c = lax.rem(ctx, 2)
    y = lax.rem(lax.div(ctx, 2), NY)
    zl = lax.div(ctx, 2 * NY)
    x = lax.rem(head, NX)
    zh = lax.div(head, NX)
    rows, heads, width = q_ref.shape
    iheads, idim = qi_ref.shape[1:]
    nk = lat_hbm.shape[1]
    wide = qbuf.shape[-1]
    K2 = 2 * nk
    J = NH * iheads
    base = wide - 128
    tail = width - base
    scale = width ** -0.5
    log2e = math.log2(math.e)
    own_plane = x == zl

    def ctx_of(zl_, y_, c_):
        return (zl_ * NY + y_) * 2 + c_

    def rcopy(src, dst, ssem, rsem, ctx_, head_):
        return pltpu.make_async_remote_copy(
            src_ref=src, dst_ref=dst, send_sem=ssem, recv_sem=rsem,
            device_id={"ctx": ctx_, "head": head_}, device_id_type=MESH,
        )

    def arrived(dst, rsem):
        pltpu.make_async_copy(dst, dst, rsem).wait()

    sends = []

    def send(*args):
        cp = rcopy(*args)
        cp.start()
        sends.append(cp.wait_send)

    def send_unless(local, src, dst, ssem, rsem, ctx_, head_):
        @pl.when(jnp.logical_not(local))
        def _():
            rcopy(src, dst, ssem, rsem, ctx_, head_).start()

        @pl.when(local)
        def _():
            pltpu.make_async_copy(src, dst, rsem).start()

        def finish():
            @pl.when(jnp.logical_not(local))
            def _():
                rcopy(src, dst, ssem, rsem, ctx_, head_).wait_send()

        sends.append(finish)

    y_peers = [lax.rem(y + d, NY) for d in range(1, NY)]
    z_peers = [lax.rem(zl + d, NZ) for d in range(1, NZ)]
    x_peers = [lax.rem(x + d, NX) for d in range(1, NX)]
    zls = [zl] + z_peers
    plane = [
        (ctx_of(lax.rem(zl + dz, NZ), lax.rem(y + dy, NY), c), lax.rem(zl + dz, NZ) * NY + lax.rem(y + dy, NY))
        for dy in sorted(range(NY), key=lambda d: -min(d, NY - d)) for dz in range(NZ) if dy or dz
    ]
    hs = [lax.rem(head + d, NH) for d in range(NH)]

    barrier = pltpu.get_barrier_semaphore()

    def greet(ctx_, head_):
        pl.semaphore_signal(barrier, inc=1, device_id={"ctx": ctx_, "head": head_}, device_id_type=MESH)

    for d, h in enumerate(hs):
        if d == 0:
            @pl.when(jnp.logical_not(own_plane))
            def _():
                greet(ctx_of(x, y, c), head)
        else:
            greet(ctx_of(x, y, c), h)
    for r in range(NZH):
        for d, z_ in enumerate(zls):
            if d == 0:
                @pl.when(jnp.logical_not(own_plane & (zh == r)))
                def _():
                    greet(ctx_of(zl, y, c), r * NX + zl)
            else:
                greet(ctx_of(z_, y, c), r * NX + zl)
    loads = [
        pltpu.make_async_copy(src, dst, s_in.at[n])
        for n, (src, dst) in enumerate((
            (q_hbm, q_ref), (lse_hbm, lse_ref), (qi_hbm, qi_ref), (w_hbm, w_ref),
            (k_hbm, kbuf.at[0]), (lat_hbm, latbuf.at[0, :width]),
        ))
    ]
    for cp in loads:
        cp.start()

    greet(ctx_of(zl, y, 1 - c), head)
    for p in plane:
        greet(p[0], head)
    for x_ in x_peers:
        greet(ctx, zh * NX + x_)
    greet(ctx, (1 - zh) * NX + x)
    n_greet = 1 + (NY * NZ - 1) + (NX - 1) + 1 + NH + NZH * NZ

    for cp in loads[:4]:
        cp.wait()
    lane = lax.broadcasted_iota(jnp.int32, (heads, 128), 1)
    for r in range(rows):
        q_stage[r, :, :base] = q_ref[r, :, :base]
        last = jnp.concatenate([q_ref[r, :, base:].astype(F32), jnp.zeros((heads, 128 - tail), F32)], axis=1)
        qi = qi_ref[r].astype(F32)
        qi = jnp.concatenate([pltpu.roll(qi, tail, 1), qi], axis=0)
        q_stage[r, :, base:] = jnp.where(lane < tail, last, qi).astype(BF16)
        a_stage[r : r + 1, :] = jnp.concatenate(
            [lse_ref[r : r + 1, :], w_ref[r : r + 1, :], jnp.zeros((1, 128 - heads - iheads), F32)], axis=1
        )
    for side in range(2):
        latbuf[side, width:] = jnp.zeros((wide - width, nk), BF16)
    pl.semaphore_wait(barrier, jnp.where(own_plane, n_greet - 2, n_greet))

    for r in (1 - zh, zh) if NZH == 2 else range(NZH):
        for d, z_ in enumerate(zls):
            to = (ctx_of(z_, y, c), r * NX + zl)
            aargs = (a_stage.at[pl.ds(r, 1)], abuf.at[y, pl.ds(head, 1)], s_ea.at[r, d], r_ea.at[head], *to)
            qargs = (q_stage.at[r], qbuf.at[y, head], s_eq.at[r, d], r_eq.at[head], *to)
            if d == 0:
                send_unless(own_plane & (zh == r), *aargs)
                send_unless(own_plane & (zh == r), *qargs)
            else:
                send(*aargs)
                send(*qargs)
    other = ctx_of(zl, y, 1 - c)
    for cp in loads[4:]:
        cp.wait()
    send(kbuf.at[0], kbuf.at[1], s_core.at[0], r_core.at[0], other, head)
    send(latbuf.at[0, :width], latbuf.at[1, :width], s_core.at[1], r_core.at[1], other, head)

    NC = NH // HC
    up, down = lax.rem(y + 1, NY), lax.rem(y + NY - 1, NY)
    far = NY // 2
    near = far - 1
    order = [lax.rem(zh * (NC // 2) + n, NC) for n in range(NC)]
    order.insert(NC // 2, NC)

    def piece(y0, n):
        return abuf.at[y0] if n is NC else qbuf.at[y0, pl.ds(HC * n, HC)]

    def forward(y0, k, step, plus, minus):
        n = order[k]
        if plus:
            send(piece(y0, n), piece(y0, n), s_up.at[step, k], r_y.at[y0, n], ctx_of(zl, up, c), head)
        if minus:
            send(piece(y0, n), piece(y0, n), s_down.at[step, k], r_y.at[y0, n], ctx_of(zl, down, c), head)

    def by_up(k):
        return k <= NC // 2

    for k, n in enumerate(order):
        if n is NC:
            for h in range(NH):
                arrived(abuf.at[y, pl.ds(h, 1)], r_ea.at[h])
        else:
            for h in range(HC):
                arrived(qbuf.at[y, HC * n + h], r_eq.at[HC * n + h])
        forward(y, k, 0, near > 0 or by_up(k), near > 0 or not by_up(k))

    CH = min(512, nk)

    def block(y0):
        q = qbuf[y0].reshape(NH * heads, wide)
        rest = qbuf[y0, :, :, base:].astype(F32)
        low, high = rest[:, :iheads].reshape(J, 128), rest[:, iheads:].reshape(J, 128)
        ln = lax.broadcasted_iota(jnp.int32, (J, 128), 1)
        qi32 = jnp.where(ln < tail, pltpu.roll(low, 128 - tail, 1), high)
        qi = qi32.astype(BF16)
        aux = abuf[y0][:, None, :]
        ln = lax.broadcasted_iota(jnp.int32, (NH, heads, 128), 2)
        sub = lax.broadcasted_iota(jnp.int32, (NH, heads, 128), 1)
        lse = jnp.sum(jnp.where(ln == sub, aux, 0.0), axis=2, keepdims=True).reshape(NH * heads, 1) * log2e
        wcol = jnp.sum(jnp.where(ln == sub + heads, aux, 0.0)[:, :iheads], axis=2, keepdims=True).reshape(J, 1)
        wq[y0] = (qi32 * wcol).astype(BF16)
        for side in range(2):
            for n in range(nk // CH):
                cols = slice(n * CH, (n + 1) * CH)
                kcols = slice(side * nk + n * CH, side * nk + (n + 1) * CH)
                s = jnp.dot(q, latbuf[side, :, cols], preferred_element_type=F32)
                e = jnp.exp2(s * (scale * log2e) - lse)
                tacc[y0, :, kcols] = jnp.sum(e.reshape(NH * heads // 8, 8, CH), axis=0)
                rw = lax.dot_general(qi, kbuf[side, cols, :], NT, preferred_element_type=F32)
                keep[y0, :, kcols] = jnp.where(rw > 0, 1.0, 0.0).astype(BF16)
                sacc[y0, :, kcols] = jnp.sum((wcol * jnp.maximum(rw, 0.0)).reshape(J // 8, 8, CH), axis=0)

    arrived(kbuf.at[1], r_core.at[0])
    arrived(latbuf.at[1, :width], r_core.at[1])
    block(y)
    for step in range(1, near + 1):
        yu = lax.rem(y + NY - step, NY)
        yd = lax.rem(y + step, NY)
        for k, n in enumerate(order):
            arrived(piece(yu, n), r_y.at[yu, n])
            forward(yu, k, step, step < near or by_up(k), False)
            arrived(piece(yd, n), r_y.at[yd, n])
            forward(yd, k, step, False, step < near or not by_up(k))
        block(yu)
        block(yd)
    yf = lax.rem(y + far, NY)
    for n in order:
        arrived(piece(yf, n), r_y.at[yf, n])
    block(yf)

    target = jnp.sum(tacc[...], axis=1)
    score = jnp.sum(sacc[...], axis=1)
    m = jnp.max(score, axis=1, keepdims=True)
    l = jnp.sum(jnp.exp(score - m), axis=1, keepdims=True)
    t = jnp.sum(target, axis=1, keepdims=True)
    sl = lax.broadcasted_iota(jnp.int32, (NY, 128), 1)
    ss = lax.broadcasted_iota(jnp.int32, (NY, 128), 0)
    at = [sl == ss + n * NY for n in range(3)]
    me = zl * NY + y
    mine = jnp.where(at[0], m, jnp.where(at[1], l, jnp.where(at[2], t, 0.0)))
    st_buf[pl.ds(me, 1), :] = jnp.sum(mine, axis=0, keepdims=True)
    for n, (dev, _) in enumerate(plane):
        send(st_buf.at[pl.ds(me, 1)], st_buf.at[pl.ds(me, 1)], s_st.at[n], r_st.at[me], dev, head)
    wqt = wq[...].reshape(NY * J, idim).astype(F32).T.astype(BF16)
    for _, slot in plane:
        arrived(st_buf.at[pl.ds(slot, 1)], r_st.at[slot])
    stats = st_buf[...]
    peak = pltpu.roll(stats, NY, 1)
    top = jnp.max(peak, axis=0, keepdims=True)
    in_l = lax.broadcasted_iota(jnp.int32, stats.shape, 1) // NY == 1
    mass = jnp.sum(jnp.where(in_l, stats * jnp.exp(jnp.where(in_l, peak - top, 0.0)), stats), axis=0, keepdims=True)
    m = jnp.sum(jnp.where(at[1], top, 0.0), axis=1, keepdims=True)
    l = jnp.sum(jnp.where(at[1], mass, 0.0), axis=1, keepdims=True)
    t = jnp.sum(jnp.where(at[2], mass, 0.0), axis=1, keepdims=True)
    grad = factor * (jnp.exp(score - m) / l - target / t)
    gbuf[...] = grad

    nc = nk // KC
    nq = nc // NX

    def mask(side, q):
        cols = slice(q * nc, (q + 1) * nc)
        kcols = slice(side * nk + q * nc, side * nk + (q + 1) * nc)
        for y0 in range(NY):
            g = jnp.broadcast_to(gbuf[y0 : y0 + 1, kcols], (16, nc)).astype(BF16)
            g = keep[y0, :, kcols].reshape(J // 16, 16, nc) * g[None]
            masked[side, y0 * J : (y0 + 1) * J, cols] = g.reshape(J, nc)
        return jnp.dot(wqt, masked[side, :, cols], preferred_element_type=F32)

    for q in range(KC):
        ck_send[q] = mask(1, q).astype(BF16)
        send(ck_send.at[q], ck_recv.at[q], s_ck.at[q], r_ck.at[q], other, head)
    for q in range(KC):
        own_key = mask(0, q)
        arrived(ck_recv.at[q], r_ck.at[q])
        own_key = own_key + ck_recv[q].astype(F32)
        for n in range(NX):
            gx_sum[q, n] = own_key[:, n * nq : (n + 1) * nq]
            gx_send[q, n] = own_key[:, n * nq : (n + 1) * nq].astype(BF16)
        for n, x_ in enumerate(x_peers):
            send(gx_send.at[q, x_], gx_recv.at[q, x], s_gx.at[q, n], r_gx.at[q, x], ctx, zh * NX + x_)

    part[...] = (
        jnp.dot(masked[0], kbuf[0], preferred_element_type=F32)
        + jnp.dot(masked[1], kbuf[1], preferred_element_type=F32)
    ).reshape(part.shape).astype(part.dtype)
    for n, y_ in enumerate(y_peers):
        send(part.at[y_], ry_buf.at[y], s_ry.at[n], r_ry.at[y], ctx_of(zl, y_, c), head)

    for q in range(KC):
        gsum = gx_sum[q, x]
        for x_ in x_peers:
            arrived(gx_recv.at[q, x_], r_gx.at[q, x_])
            gsum = gsum + gx_recv[q, x_].astype(F32)
        gz_send[q] = gsum.astype(BF16)
        send(gz_send.at[q], gz_recv.at[q], s_gz.at[q], r_gz.at[q], ctx, (1 - zh) * NX + x)

    total = part[y].astype(F32)
    for y_ in y_peers:
        arrived(ry_buf.at[y_], r_ry.at[y_])
        total = total + ry_buf[y_].astype(F32)
    zsum[...] = total.reshape(zsum.shape)
    slot = zh * NZ + zl
    for d, h in enumerate(hs):
        args = (zsum.at[h], fq_buf.at[slot], s_fq.at[d], r_fq.at[slot], ctx_of(x, y, c), h)
        if d == 0:
            send_unless(own_plane, *args)
        else:
            send(*args)

    for q in range(KC):
        arrived(gz_recv.at[q], r_gz.at[q])
        ga_buf[q, x] = (gz_send[q].astype(F32) + gz_recv[q].astype(F32)).T.astype(BF16)
        for n, x_ in enumerate(x_peers):
            send(ga_buf.at[q, x], ga_buf.at[q, x], s_ga.at[q, n], r_ga.at[q, x], ctx, zh * NX + x_)

    for n in range(NZH * NZ):
        arrived(fq_buf.at[n], r_fq.at[n])
    for r in range(rows):
        own = jnp.sum(fq_buf[r * NZ : (r + 1) * NZ], axis=0)
        gq_ref[r] = own * column(w_ref[r : r + 1, :])
        gw_ref[r : r + 1, :] = row_of(jnp.sum(own * qi_ref[r].astype(F32), axis=1, keepdims=True))

    stores = [
        pltpu.make_async_copy(gq_ref, gq_hbm, s_out.at[KC]),
        pltpu.make_async_copy(gw_ref, gw_hbm, s_out.at[KC + 1]),
    ]
    for cp in stores:
        cp.start()
    for q in range(KC):
        for x_ in x_peers:
            arrived(ga_buf.at[q, x_], r_ga.at[q, x_])
        part_q = slice(q * nc, (q + 1) * nc)
        gk_ref[part_q] = ga_buf[q].astype(F32).reshape(nc, idim)
        cp = pltpu.make_async_copy(gk_ref.at[part_q], gk_hbm.at[part_q], s_out.at[q])
        cp.start()
        stores.append(cp)

    for cp in stores:
        cp.wait()
    for finish in sends:
        finish()


def body(dims, keys, q_attn, latent, lse_saved, q_index, k_index, head_weight):
    NZ, NY, NZH, NX = dims
    NH = NZH * NX
    rows, heads, width = q_attn.shape
    iheads, idim = q_index.shape[1:]
    nk = latent.shape[0]
    wide = -(-width // 128) * 128
    J = NH * iheads
    K2 = 2 * nk
    nq = nk // NX // KC
    NP = NH // HC + 1
    V, DMA = pltpu.VMEM, pltpu.SemaphoreType.DMA
    vm = pl.BlockSpec(memory_space=pltpu.VMEM)
    scratch = [
        V((rows, iheads, idim), F32), V((rows, iheads), F32), V((nk, idim), F32), DMA((KC + 2,)),
        V((rows, heads, width), BF16), V((rows, heads), F32), V((rows, iheads, idim), BF16), V((rows, iheads), F32), DMA((6,)),
        V((rows, heads, wide), BF16), V((rows, 128), F32),
        V((NY, NH, heads, wide), BF16), V((NY, NH, 128), F32),
        V((2, wide, nk), BF16), V((2, nk, idim), BF16),
        V((NY, J, K2), BF16), V((NY, J, idim), BF16),
        V((NY, 8, K2), F32), V((NY, 8, K2), F32), V((NY, K2), F32), V((2, NY * J, nk), BF16),
        V((NZ * NY, 128), F32),
        V((NY, J, idim), BF16), V((NY, J, idim), BF16),
        V((NH, iheads, idim), F32), V((NZH * NZ, iheads, idim), F32),
        V((KC, idim, nk // KC), BF16), V((KC, idim, nk // KC), BF16),
        V((KC, NX, idim, nq), F32), V((KC, NX, idim, nq), BF16), V((KC, NX, idim, nq), BF16),
        V((KC, idim, nq), BF16), V((KC, idim, nq), BF16), V((KC, NX, nq, idim), BF16),
        DMA((rows, NZ)), DMA((rows, NZ)), DMA((NH,)), DMA((NH,)), DMA((2,)), DMA((2,)), DMA((KC,)), DMA((KC,)),
        DMA((NY, NP)), DMA((NY, NP)), DMA((NY, NP)),
        DMA((NZ * NY,)), DMA((NZ * NY,)), DMA((NY,)), DMA((NY,)), DMA((NH,)), DMA((NZH * NZ,)),
        DMA((KC, NX)), DMA((KC, NX)), DMA((KC,)), DMA((KC,)), DMA((KC, NX)), DMA((KC, NX)),
    ]
    shapes = (
        jax.ShapeDtypeStruct((rows, iheads, idim), F32),
        jax.ShapeDtypeStruct((rows, iheads), F32),
        jax.ShapeDtypeStruct((nk, idim), F32),
    )
    outs = pl.pallas_call(
        functools.partial(kernel, dims, keys / 32.0),
        out_shape=shapes,
        in_specs=[pl.BlockSpec(memory_space=pl.ANY)] * 6,
        out_specs=tuple(pl.BlockSpec(memory_space=pl.ANY) for _ in shapes),
        scratch_shapes=scratch,
        compiler_params=pltpu.CompilerParams(
            collective_id=0, has_side_effects=True, vmem_limit_bytes=56 * 1024 * 1024
        ),
        name="indexer_backward",
    )(q_attn, latent.T, lse_saved, q_index, k_index, head_weight)
    return pl.pallas_call(
        store,
        out_shape=shapes,
        in_specs=[vm] * 3,
        out_specs=tuple(pl.BlockSpec(memory_space=pl.ANY) for _ in shapes),
        scratch_shapes=[DMA((3,))],
        compiler_params=pltpu.CompilerParams(vmem_limit_bytes=58 * 1024 * 1024),
        name="store_results",
    )(*outs)


def store(a_ref, b_ref, c_ref, a_out, b_out, c_out, sems):
    copies = [
        pltpu.make_async_copy(src, dst, sems.at[n])
        for n, (src, dst) in enumerate(((a_ref, a_out), (b_ref, b_out), (c_ref, c_out)))
    ]
    for cp in copies:
        cp.start()
    for cp in copies:
        cp.wait()


def build(mesh, dims, keys):
    return jax.shard_map(
        functools.partial(body, dims, keys),
        mesh=mesh,
        in_specs=(
            P("ctx", "head", None),
            P("ctx", None),
            P("ctx", "head"),
            P("ctx", "head", None),
            P("ctx", None),
            P("ctx", "head"),
        ),
        out_specs=(P("ctx", "head", None), P("ctx", "head"), P("ctx", None)),
        check_vma=False,
    )


def solution(mesh):
    return build(mesh, DIMS, 65536)
```

```python
import functools
import math

import jax
import jax.numpy as jnp
from jax import lax
from jax.experimental import pallas as pl
from jax.experimental.pallas import tpu as pltpu
from jax.sharding import PartitionSpec as P

MESH = pl.DeviceIdType.MESH
F32, BF16 = jnp.float32, jnp.bfloat16
DIMS = (4, 8, 2, 4)
KC = 2
NT = (((1,), (1,)), ((), ()))


def column(row):
    n = row.shape[1]
    eye = lax.broadcasted_iota(jnp.int32, (n, n), 0) == lax.broadcasted_iota(jnp.int32, (n, n), 1)
    return jnp.sum(jnp.where(eye, row, 0.0), axis=1, keepdims=True)


def row_of(col):
    n = col.shape[0]
    eye = lax.broadcasted_iota(jnp.int32, (n, n), 0) == lax.broadcasted_iota(jnp.int32, (n, n), 1)
    return jnp.sum(jnp.where(eye, col, 0.0), axis=0, keepdims=True)


def kernel(
    dims, factor,
    q_hbm, lat_hbm, lse_hbm, qi_hbm, k_hbm, w_hbm,
    gq_hbm, gw_hbm, gk_hbm,
    gq_ref, gw_ref, gk_ref, s_out,
    q_ref, lse_ref, qi_ref, w_ref, s_in,
    q_stage, a_stage, qbuf, abuf, latbuf, kbuf, keep, wq, target, score, local, gbuf, masked,
    st_buf, part, ry_buf, zsum, fq_buf,
    ck_send, ck_recv, gx_sum, gx_send, gx_recv, gz_send, gz_recv, ga_buf,
    s_eq, s_ea, r_eq, r_ea, s_core, r_core, s_ck, r_ck, s_up, s_down, r_y,
    s_st, r_st, s_ry, r_ry, s_fq, r_fq, s_gx, r_gx, s_gz, r_gz, s_ga, r_ga,
):
    NZ, NY, NZH, NX = dims
    NH = NZH * NX
    ctx, head = lax.axis_index("ctx"), lax.axis_index("head")
    c = lax.rem(ctx, 2)
    y = lax.rem(lax.div(ctx, 2), NY)
    zl = lax.div(ctx, 2 * NY)
    x = lax.rem(head, NX)
    zh = lax.div(head, NX)
    rows, heads, width = q_ref.shape
    iheads, idim = qi_ref.shape[1:]
    nk = lat_hbm.shape[1]
    wide = qbuf.shape[-1]
    K2 = 2 * nk
    J = NH * iheads
    base = wide - 128
    tail = width - base
    scale = width ** -0.5
    log2e = math.log2(math.e)
    own_plane = x == zl

    def ctx_of(zl_, y_, c_):
        return (zl_ * NY + y_) * 2 + c_

    def rcopy(src, dst, ssem, rsem, ctx_, head_):
        return pltpu.make_async_remote_copy(
            src_ref=src, dst_ref=dst, send_sem=ssem, recv_sem=rsem,
            device_id={"ctx": ctx_, "head": head_}, device_id_type=MESH,
        )

    def arrived(dst, rsem):
        pltpu.make_async_copy(dst, dst, rsem).wait()

    sends = []

    def send(*args):
        cp = rcopy(*args)
        cp.start()
        sends.append(cp.wait_send)

    def drain(count):
        for finish in sends[:count]:
            finish()
        del sends[:count]

    def send_unless(local, src, dst, ssem, rsem, ctx_, head_):
        @pl.when(jnp.logical_not(local))
        def _():
            rcopy(src, dst, ssem, rsem, ctx_, head_).start()

        @pl.when(local)
        def _():
            pltpu.make_async_copy(src, dst, rsem).start()

        def finish():
            @pl.when(jnp.logical_not(local))
            def _():
                rcopy(src, dst, ssem, rsem, ctx_, head_).wait_send()

        sends.append(finish)

    y_peers = [lax.rem(y + d, NY) for d in range(1, NY)]
    z_peers = [lax.rem(zl + d, NZ) for d in range(1, NZ)]
    x_peers = [lax.rem(x + d, NX) for d in sorted(range(1, NX), key=lambda d: -min(d, NX - d))]
    zls = [zl] + z_peers
    plane = [
        (ctx_of(lax.rem(zl + dz, NZ), lax.rem(y + dy, NY), c), lax.rem(zl + dz, NZ) * NY + lax.rem(y + dy, NY))
        for dy in sorted(range(NY), key=lambda d: -min(d, NY - d)) for dz in range(NZ) if dy or dz
    ]
    hs = [lax.rem(head + d, NH) for d in range(NH)]

    barrier = pltpu.get_barrier_semaphore()

    def greet(ctx_, head_):
        pl.semaphore_signal(barrier, inc=1, device_id={"ctx": ctx_, "head": head_}, device_id_type=MESH)

    for d, h in enumerate(hs):
        if d == 0:
            @pl.when(jnp.logical_not(own_plane))
            def _():
                greet(ctx_of(x, y, c), head)
        else:
            greet(ctx_of(x, y, c), h)
    for r in range(NZH):
        for d, z_ in enumerate(zls):
            if d == 0:
                @pl.when(jnp.logical_not(own_plane & (zh == r)))
                def _():
                    greet(ctx_of(zl, y, c), r * NX + zl)
            else:
                greet(ctx_of(z_, y, c), r * NX + zl)
    loads = [
        pltpu.make_async_copy(src, dst, s_in.at[n])
        for n, (src, dst) in enumerate((
            (q_hbm, q_ref), (lse_hbm, lse_ref), (qi_hbm, qi_ref), (w_hbm, w_ref),
            (k_hbm, kbuf.at[0]), (lat_hbm, latbuf.at[0, :width]),
        ))
    ]
    for cp in loads:
        cp.start()

    greet(ctx_of(zl, y, 1 - c), head)
    for p in plane:
        greet(p[0], head)
    for x_ in x_peers:
        greet(ctx, zh * NX + x_)
    greet(ctx, (1 - zh) * NX + x)
    n_greet = 1 + (NY * NZ - 1) + (NX - 1) + 1 + NH + NZH * NZ

    for cp in loads[:4]:
        cp.wait()
    lane = lax.broadcasted_iota(jnp.int32, (heads, 128), 1)
    for r in range(rows):
        q_stage[r, :, :base] = q_ref[r, :, :base]
        last = jnp.concatenate([q_ref[r, :, base:].astype(F32), jnp.zeros((heads, 128 - tail), F32)], axis=1)
        qi = qi_ref[r].astype(F32)
        qi = jnp.concatenate([pltpu.roll(qi, tail, 1), qi], axis=0)
        q_stage[r, :, base:] = jnp.where(lane < tail, last, qi).astype(BF16)
        a_stage[r : r + 1, :] = jnp.concatenate(
            [lse_ref[r : r + 1, :], w_ref[r : r + 1, :], jnp.zeros((1, 128 - heads - iheads), F32)], axis=1
        )
    for side in range(2):
        latbuf[side, width:] = jnp.zeros((wide - width, nk), BF16)
    pl.semaphore_wait(barrier, jnp.where(own_plane, n_greet - 2, n_greet))

    for r in (1 - zh, zh) if NZH == 2 else range(NZH):
        for d, z_ in enumerate(zls):
            to = (ctx_of(z_, y, c), r * NX + zl)
            aargs = (a_stage.at[pl.ds(r, 1)], abuf.at[y, pl.ds(head, 1)], s_ea.at[r, d], r_ea.at[head], *to)
            qargs = (q_stage.at[r], qbuf.at[y, head], s_eq.at[r, d], r_eq.at[head], *to)
            if d == 0:
                send_unless(own_plane & (zh == r), *aargs)
                send_unless(own_plane & (zh == r), *qargs)
            else:
                send(*aargs)
                send(*qargs)
    other = ctx_of(zl, y, 1 - c)
    for cp in loads[4:]:
        cp.wait()
    send(kbuf.at[0], kbuf.at[1], s_core.at[0], r_core.at[0], other, head)
    send(latbuf.at[0, :width], latbuf.at[1, :width], s_core.at[1], r_core.at[1], other, head)

    NC = NH
    up, down = lax.rem(y + 1, NY), lax.rem(y + NY - 1, NY)
    far = NY // 2
    near = far - 1
    order = [
        lax.rem(zh + dz, NZH) * NX + lax.rem(x + dx, NX)
        for dz in range(NZH) for dx in sorted(range(NX), key=lambda d: min(d, NX - d))
    ]
    order.insert(NC // 2, NC)

    def piece(y0, n):
        return abuf.at[y0] if n is NC else qbuf.at[y0, n]

    def forward(y0, k, step, plus, minus):
        n = order[k]
        if plus:
            send(piece(y0, n), piece(y0, n), s_up.at[step, k], r_y.at[y0, n], ctx_of(zl, up, c), head)
        if minus:
            send(piece(y0, n), piece(y0, n), s_down.at[step, k], r_y.at[y0, n], ctx_of(zl, down, c), head)

    def by_up(k):
        return k <= NC // 2

    for k, n in enumerate(order):
        if n is NC:
            for h in range(NH):
                arrived(abuf.at[y, pl.ds(h, 1)], r_ea.at[h])
        else:
            arrived(qbuf.at[y, n], r_eq.at[n])
        forward(y, k, 0, near > 0 or by_up(k), near > 0 or not by_up(k))

    CH = min(512, nk)

    def block(y0):
        q = qbuf[y0].reshape(NH * heads, wide)
        rest = qbuf[y0, :, :, base:].astype(F32)
        low, high = rest[:, :iheads].reshape(J, 128), rest[:, iheads:].reshape(J, 128)
        ln = lax.broadcasted_iota(jnp.int32, (J, 128), 1)
        qi32 = jnp.where(ln < tail, pltpu.roll(low, 128 - tail, 1), high)
        qi = qi32.astype(BF16)
        aux = abuf[y0][:, None, :]
        ln = lax.broadcasted_iota(jnp.int32, (NH, heads, 128), 2)
        sub = lax.broadcasted_iota(jnp.int32, (NH, heads, 128), 1)
        lse = jnp.sum(jnp.where(ln == sub, aux, 0.0), axis=2, keepdims=True).reshape(NH * heads, 1) * log2e
        wcol = jnp.sum(jnp.where(ln == sub + heads, aux, 0.0)[:, :iheads], axis=2, keepdims=True).reshape(J, 1)
        wq[y0] = (qi32 * wcol).astype(BF16)
        for side in range(2):
            for n in range(nk // CH):
                cols = slice(n * CH, (n + 1) * CH)
                kcols = slice(side * nk + n * CH, side * nk + (n + 1) * CH)
                s = jnp.dot(q, latbuf[side, :, cols], preferred_element_type=F32)
                e = jnp.exp2(s * (scale * log2e) - lse)
                target[pl.ds(y0, 1), kcols] = jnp.sum(e, axis=0, keepdims=True)
                rw = lax.dot_general(qi, kbuf[side, cols, :], NT, preferred_element_type=F32)
                keep[y0, :, kcols] = jnp.where(rw > 0, 1.0, 0.0).astype(BF16)
                score[pl.ds(y0, 1), kcols] = jnp.sum(wcol * jnp.maximum(rw, 0.0), axis=0, keepdims=True)
        srow = score[pl.ds(y0, 1), :]
        m = jnp.max(srow, axis=1, keepdims=True)
        l = jnp.sum(jnp.exp(srow - m), axis=1, keepdims=True)
        t = jnp.sum(target[pl.ds(y0, 1), :], axis=1, keepdims=True)
        ln = lax.broadcasted_iota(jnp.int32, (1, 128), 1)
        local[pl.ds(y0, 1), :] = jnp.where(ln == 0, m, jnp.where(ln == 1, l, t))

    arrived(kbuf.at[1], r_core.at[0])
    arrived(latbuf.at[1, :width], r_core.at[1])
    block(y)
    for step in range(1, near + 1):
        yu = lax.rem(y + NY - step, NY)
        yd = lax.rem(y + step, NY)
        for k, n in enumerate(order):
            arrived(piece(yu, n), r_y.at[yu, n])
            forward(yu, k, step, step < near or by_up(k), False)
            arrived(piece(yd, n), r_y.at[yd, n])
            forward(yd, k, step, False, step < near or not by_up(k))
        block(yu)
        block(yd)
    yf = lax.rem(y + far, NY)
    for n in order:
        arrived(piece(yf, n), r_y.at[yf, n])
    block(yf)

    m, l, t = (local[:, n : n + 1] for n in range(3))
    sl = lax.broadcasted_iota(jnp.int32, (NY, 128), 1)
    ss = lax.broadcasted_iota(jnp.int32, (NY, 128), 0)
    at = [sl == ss + n * NY for n in range(3)]
    me = zl * NY + y
    mine = jnp.where(at[0], m, jnp.where(at[1], l, jnp.where(at[2], t, 0.0)))
    st_buf[pl.ds(me, 1), :] = jnp.sum(mine, axis=0, keepdims=True)
    before = len(sends)
    for n, (dev, _) in enumerate(plane):
        send(st_buf.at[pl.ds(me, 1)], st_buf.at[pl.ds(me, 1)], s_st.at[n], r_st.at[me], dev, head)
    wqt = wq[...].reshape(NY * J, idim).astype(F32).T.astype(BF16)
    drain(before)
    for _, slot in plane:
        arrived(st_buf.at[pl.ds(slot, 1)], r_st.at[slot])
    stats = st_buf[...]
    peak = pltpu.roll(stats, NY, 1)
    top = jnp.max(peak, axis=0, keepdims=True)
    in_l = lax.broadcasted_iota(jnp.int32, stats.shape, 1) // NY == 1
    mass = jnp.sum(jnp.where(in_l, stats * jnp.exp(jnp.where(in_l, peak - top, 0.0)), stats), axis=0, keepdims=True)
    m = jnp.sum(jnp.where(at[1], top, 0.0), axis=1, keepdims=True)
    l = jnp.sum(jnp.where(at[1], mass, 0.0), axis=1, keepdims=True)
    t = jnp.sum(jnp.where(at[2], mass, 0.0), axis=1, keepdims=True)
    grad = factor * (jnp.exp(score[...] - m) / l - target[...] / t)
    gbuf[...] = grad

    nc = nk // KC
    nq = nc // NX

    def mask(side, q):
        cols = slice(q * nc, (q + 1) * nc)
        kcols = slice(side * nk + q * nc, side * nk + (q + 1) * nc)
        for y0 in range(NY):
            g = jnp.broadcast_to(gbuf[y0 : y0 + 1, kcols], (16, nc)).astype(BF16)
            g = keep[y0, :, kcols].reshape(J // 16, 16, nc) * g[None]
            masked[side, y0 * J : (y0 + 1) * J, cols] = g.reshape(J, nc)
        return jnp.dot(wqt, masked[side, :, cols], preferred_element_type=F32)

    for q in range(KC):
        ck_send[q] = mask(1, q).astype(BF16)
        send(ck_send.at[q], ck_recv.at[q], s_ck.at[q], r_ck.at[q], other, head)
    for q in range(KC):
        own_key = mask(0, q)
        arrived(ck_recv.at[q], r_ck.at[q])
        own_key = own_key + ck_recv[q].astype(F32)
        for n in range(NX):
            gx_sum[q, n] = own_key[:, n * nq : (n + 1) * nq]
            gx_send[q, n] = own_key[:, n * nq : (n + 1) * nq].astype(BF16)
        for n, x_ in enumerate(x_peers):
            send(gx_send.at[q, x_], gx_recv.at[q, x], s_gx.at[q, n], r_gx.at[q, x], ctx, zh * NX + x_)

    part[...] = (
        jnp.dot(masked[0], kbuf[0], preferred_element_type=F32)
        + jnp.dot(masked[1], kbuf[1], preferred_element_type=F32)
    ).reshape(part.shape).astype(part.dtype)
    for n, y_ in enumerate(y_peers):
        send(part.at[y_], ry_buf.at[y], s_ry.at[n], r_ry.at[y], ctx_of(zl, y_, c), head)

    drain(len(sends) - len(y_peers) - KC * len(x_peers))

    for q in range(KC):
        gsum = gx_sum[q, x]
        for x_ in x_peers:
            arrived(gx_recv.at[q, x_], r_gx.at[q, x_])
            gsum = gsum + gx_recv[q, x_].astype(F32)
        gz_send[q] = gsum.astype(BF16)
        send(gz_send.at[q], gz_recv.at[q], s_gz.at[q], r_gz.at[q], ctx, (1 - zh) * NX + x)

    total = part[y].astype(F32)
    for y_ in y_peers:
        arrived(ry_buf.at[y_], r_ry.at[y_])
        total = total + ry_buf[y_].astype(F32)
    zsum[...] = total.reshape(zsum.shape)
    slot = zh * NZ + zl
    for d, h in enumerate(hs):
        args = (zsum.at[h], fq_buf.at[slot], s_fq.at[d], r_fq.at[slot], ctx_of(x, y, c), h)
        if d == 0:
            send_unless(own_plane, *args)
        else:
            send(*args)

    drain(len(sends) - NH - KC)

    for q in range(KC):
        arrived(gz_recv.at[q], r_gz.at[q])
        ga_buf[q, x] = (gz_send[q].astype(F32) + gz_recv[q].astype(F32)).T.astype(BF16)
        for n, x_ in enumerate(x_peers):
            send(ga_buf.at[q, x], ga_buf.at[q, x], s_ga.at[q, n], r_ga.at[q, x], ctx, zh * NX + x_)

    for n in range(NZH * NZ):
        arrived(fq_buf.at[n], r_fq.at[n])
    for r in range(rows):
        own = jnp.sum(fq_buf[r * NZ : (r + 1) * NZ], axis=0)
        gq_ref[r] = own * column(w_ref[r : r + 1, :])
        gw_ref[r : r + 1, :] = row_of(jnp.sum(own * qi_ref[r].astype(F32), axis=1, keepdims=True))

    stores = [
        pltpu.make_async_copy(gq_ref, gq_hbm, s_out.at[KC]),
        pltpu.make_async_copy(gw_ref, gw_hbm, s_out.at[KC + 1]),
    ]
    for cp in stores:
        cp.start()
    for q in range(KC):
        for x_ in x_peers:
            arrived(ga_buf.at[q, x_], r_ga.at[q, x_])
        part_q = slice(q * nc, (q + 1) * nc)
        gk_ref[part_q] = ga_buf[q].astype(F32).reshape(nc, idim)
        cp = pltpu.make_async_copy(gk_ref.at[part_q], gk_hbm.at[part_q], s_out.at[q])
        cp.start()
        stores.append(cp)

    for cp in stores:
        cp.wait()
    drain(len(sends))


def body(dims, keys, q_attn, latent, lse_saved, q_index, k_index, head_weight):
    NZ, NY, NZH, NX = dims
    NH = NZH * NX
    rows, heads, width = q_attn.shape
    iheads, idim = q_index.shape[1:]
    nk = latent.shape[0]
    wide = -(-width // 128) * 128
    J = NH * iheads
    K2 = 2 * nk
    nq = nk // NX // KC
    NP = NH + 1
    V, DMA = pltpu.VMEM, pltpu.SemaphoreType.DMA
    vm = pl.BlockSpec(memory_space=pltpu.VMEM)
    scratch = [
        V((rows, iheads, idim), F32), V((rows, iheads), F32), V((nk, idim), F32), DMA((KC + 2,)),
        V((rows, heads, width), BF16), V((rows, heads), F32), V((rows, iheads, idim), BF16), V((rows, iheads), F32), DMA((6,)),
        V((rows, heads, wide), BF16), V((rows, 128), F32),
        V((NY, NH, heads, wide), BF16), V((NY, NH, 128), F32),
        V((2, wide, nk), BF16), V((2, nk, idim), BF16),
        V((NY, J, K2), BF16), V((NY, J, idim), BF16),
        V((NY, K2), F32), V((NY, K2), F32), V((NY, 128), F32), V((NY, K2), F32), V((2, NY * J, nk), BF16),
        V((NZ * NY, 128), F32),
        V((NY, J, idim), BF16), V((NY, J, idim), BF16),
        V((NH, iheads, idim), F32), V((NZH * NZ, iheads, idim), F32),
        V((KC, idim, nk // KC), BF16), V((KC, idim, nk // KC), BF16),
        V((KC, NX, idim, nq), F32), V((KC, NX, idim, nq), BF16), V((KC, NX, idim, nq), BF16),
        V((KC, idim, nq), BF16), V((KC, idim, nq), BF16), V((KC, NX, nq, idim), BF16),
        DMA((rows, NZ)), DMA((rows, NZ)), DMA((NH,)), DMA((NH,)), DMA((2,)), DMA((2,)), DMA((KC,)), DMA((KC,)),
        DMA((NY, NP)), DMA((NY, NP)), DMA((NY, NP)),
        DMA((NZ * NY,)), DMA((NZ * NY,)), DMA((NY,)), DMA((NY,)), DMA((NH,)), DMA((NZH * NZ,)),
        DMA((KC, NX)), DMA((KC, NX)), DMA((KC,)), DMA((KC,)), DMA((KC, NX)), DMA((KC, NX)),
    ]
    shapes = (
        jax.ShapeDtypeStruct((rows, iheads, idim), F32),
        jax.ShapeDtypeStruct((rows, iheads), F32),
        jax.ShapeDtypeStruct((nk, idim), F32),
    )
    outs = pl.pallas_call(
        functools.partial(kernel, dims, keys / 32.0),
        out_shape=shapes,
        in_specs=[pl.BlockSpec(memory_space=pl.ANY)] * 6,
        out_specs=tuple(pl.BlockSpec(memory_space=pl.ANY) for _ in shapes),
        scratch_shapes=scratch,
        compiler_params=pltpu.CompilerParams(
            collective_id=0, has_side_effects=True, vmem_limit_bytes=56 * 1024 * 1024
        ),
        name="indexer_backward",
    )(q_attn, latent.T, lse_saved, q_index, k_index, head_weight)
    return pl.pallas_call(
        store,
        out_shape=shapes,
        in_specs=[vm] * 3,
        out_specs=tuple(pl.BlockSpec(memory_space=pl.ANY) for _ in shapes),
        scratch_shapes=[DMA((10,))],
        compiler_params=pltpu.CompilerParams(vmem_limit_bytes=58 * 1024 * 1024),
        name="store_results",
    )(*outs)


def store(a_ref, b_ref, c_ref, a_out, b_out, c_out, sems):
    n = c_ref.shape[0] // 8
    pairs = [(c_ref.at[pl.ds(i * n, n)], c_out.at[pl.ds(i * n, n)]) for i in range(8)]
    pairs += [(a_ref, a_out), (b_ref, b_out)]
    copies = [pltpu.make_async_copy(src, dst, sems.at[i]) for i, (src, dst) in enumerate(pairs)]
    for cp in copies:
        cp.start()
    for cp in copies:
        cp.wait()


def build(mesh, dims, keys):
    return jax.shard_map(
        functools.partial(body, dims, keys),
        mesh=mesh,
        in_specs=(
            P("ctx", "head", None),
            P("ctx", None),
            P("ctx", "head"),
            P("ctx", "head", None),
            P("ctx", None),
            P("ctx", "head"),
        ),
        out_specs=(P("ctx", "head", None), P("ctx", "head"), P("ctx", None)),
        check_vma=False,
    )


def solution(mesh):
    return build(mesh, DIMS, 65536)
```

```python
import functools
import math

import jax
import jax.numpy as jnp
from jax import lax
from jax.experimental import pallas as pl
from jax.experimental.pallas import tpu as pltpu
from jax.sharding import PartitionSpec as P

MESH = pl.DeviceIdType.MESH
F32, BF16 = jnp.float32, jnp.bfloat16
DIMS = (4, 8, 2, 4)
KC = 2


def column(row):
    n = row.shape[1]
    eye = lax.broadcasted_iota(jnp.int32, (n, n), 0) == lax.broadcasted_iota(jnp.int32, (n, n), 1)
    return jnp.sum(jnp.where(eye, row, 0.0), axis=1, keepdims=True)


def row_of(col):
    n = col.shape[0]
    eye = lax.broadcasted_iota(jnp.int32, (n, n), 0) == lax.broadcasted_iota(jnp.int32, (n, n), 1)
    return jnp.sum(jnp.where(eye, col, 0.0), axis=0, keepdims=True)


def kernel(
    dims, factor,
    q_hbm, lat_hbm, lse_hbm, qi_hbm, k_hbm, w_hbm,
    gq_hbm, gw_hbm, gk_hbm,
    gq_ref, gw_ref, gk_ref, s_out,
    q_ref, lse_ref, qi_ref, w_ref, s_in,
    q_stage, a_stage, qbuf, abuf, latbuf, kbuf, ktbuf, keep, wq, target, score, local, masked,
    st_buf, part, ry_buf, zsum, fq_buf,
    ck_send, ck_recv, gx_sum, gx_send, gx_recv, gz_send, gz_recv, ga_buf,
    s_eq, s_ea, r_eq, r_ea, s_core, r_core, s_ck, r_ck, s_up, s_down, r_y,
    s_st, r_st, s_ry, r_ry, s_fq, r_fq, s_gx, r_gx, s_gz, r_gz, s_ga, r_ga,
):
    NZ, NY, NZH, NX = dims
    NH = NZH * NX
    ctx, head = lax.axis_index("ctx"), lax.axis_index("head")
    c = lax.rem(ctx, 2)
    y = lax.rem(lax.div(ctx, 2), NY)
    zl = lax.div(ctx, 2 * NY)
    x = lax.rem(head, NX)
    zh = lax.div(head, NX)
    rows, heads, width = q_ref.shape
    iheads, idim = qi_ref.shape[1:]
    nk = lat_hbm.shape[1]
    wide = qbuf.shape[-1]
    K2 = 2 * nk
    J = NH * iheads
    base = wide - 128
    tail = width - base
    scale = width ** -0.5
    log2e = math.log2(math.e)
    own_plane = x == zl

    def ctx_of(zl_, y_, c_):
        return (zl_ * NY + y_) * 2 + c_

    def rcopy(src, dst, ssem, rsem, ctx_, head_):
        return pltpu.make_async_remote_copy(
            src_ref=src, dst_ref=dst, send_sem=ssem, recv_sem=rsem,
            device_id={"ctx": ctx_, "head": head_}, device_id_type=MESH,
        )

    def arrived(dst, rsem):
        pltpu.make_async_copy(dst, dst, rsem).wait()

    sends = []

    def send(*args):
        cp = rcopy(*args)
        cp.start()
        sends.append(cp.wait_send)

    def drain(count):
        for finish in sends[:count]:
            finish()
        del sends[:count]

    def send_unless(local, src, dst, ssem, rsem, ctx_, head_):
        @pl.when(jnp.logical_not(local))
        def _():
            rcopy(src, dst, ssem, rsem, ctx_, head_).start()

        @pl.when(local)
        def _():
            pltpu.make_async_copy(src, dst, rsem).start()

        def finish():
            @pl.when(jnp.logical_not(local))
            def _():
                rcopy(src, dst, ssem, rsem, ctx_, head_).wait_send()

        sends.append(finish)

    y_peers = [lax.rem(y + d, NY) for d in range(1, NY)]
    z_peers = [lax.rem(zl + d, NZ) for d in range(1, NZ)]
    x_peers = [lax.rem(x + d, NX) for d in sorted(range(1, NX), key=lambda d: -min(d, NX - d))]
    zls = [zl] + z_peers
    plane = [
        (ctx_of(lax.rem(zl + dz, NZ), lax.rem(y + dy, NY), c), lax.rem(zl + dz, NZ) * NY + lax.rem(y + dy, NY))
        for dy in sorted(range(NY), key=lambda d: -min(d, NY - d)) for dz in range(NZ) if dy or dz
    ]
    hs = [lax.rem(head + d, NH) for d in range(NH)]

    barrier = pltpu.get_barrier_semaphore()

    def greet(ctx_, head_):
        pl.semaphore_signal(barrier, inc=1, device_id={"ctx": ctx_, "head": head_}, device_id_type=MESH)

    for d, h in enumerate(hs):
        if d == 0:
            @pl.when(jnp.logical_not(own_plane))
            def _():
                greet(ctx_of(x, y, c), head)
        else:
            greet(ctx_of(x, y, c), h)
    for r in range(NZH):
        for d, z_ in enumerate(zls):
            if d == 0:
                @pl.when(jnp.logical_not(own_plane & (zh == r)))
                def _():
                    greet(ctx_of(zl, y, c), r * NX + zl)
            else:
                greet(ctx_of(z_, y, c), r * NX + zl)
    loads = [
        pltpu.make_async_copy(src, dst, s_in.at[n])
        for n, (src, dst) in enumerate((
            (q_hbm, q_ref), (lse_hbm, lse_ref), (qi_hbm, qi_ref), (w_hbm, w_ref),
            (k_hbm, kbuf.at[0]), (lat_hbm, latbuf.at[0, :width]),
        ))
    ]
    for cp in loads:
        cp.start()

    greet(ctx_of(zl, y, 1 - c), head)
    for p in plane:
        greet(p[0], head)
    for x_ in x_peers:
        greet(ctx, zh * NX + x_)
    greet(ctx, (1 - zh) * NX + x)
    n_greet = 1 + (NY * NZ - 1) + (NX - 1) + 1 + NH + NZH * NZ

    for cp in loads[:4]:
        cp.wait()
    lane = lax.broadcasted_iota(jnp.int32, (heads, 128), 1)
    for r in range(rows):
        q_stage[r, :, :base] = q_ref[r, :, :base]
        last = jnp.concatenate([q_ref[r, :, base:].astype(F32), jnp.zeros((heads, 128 - tail), F32)], axis=1)
        qi = qi_ref[r].astype(F32)
        qi = jnp.concatenate([pltpu.roll(qi, tail, 1), qi], axis=0)
        q_stage[r, :, base:] = jnp.where(lane < tail, last, qi).astype(BF16)
        a_stage[r : r + 1, :] = jnp.concatenate(
            [lse_ref[r : r + 1, :], w_ref[r : r + 1, :], jnp.zeros((1, 128 - heads - iheads), F32)], axis=1
        )
    for side in range(2):
        latbuf[side, width:] = jnp.zeros((wide - width, nk), BF16)
    pl.semaphore_wait(barrier, jnp.where(own_plane, n_greet - 2, n_greet))

    for r in (1 - zh, zh) if NZH == 2 else range(NZH):
        for d, z_ in enumerate(zls):
            to = (ctx_of(z_, y, c), r * NX + zl)
            aargs = (a_stage.at[pl.ds(r, 1)], abuf.at[y, pl.ds(head, 1)], s_ea.at[r, d], r_ea.at[head], *to)
            qargs = (q_stage.at[r], qbuf.at[y, head], s_eq.at[r, d], r_eq.at[head], *to)
            if d == 0:
                send_unless(own_plane & (zh == r), *aargs)
                send_unless(own_plane & (zh == r), *qargs)
            else:
                send(*aargs)
                send(*qargs)
    other = ctx_of(zl, y, 1 - c)
    for cp in loads[4:]:
        cp.wait()
    send(kbuf.at[0], kbuf.at[1], s_core.at[0], r_core.at[0], other, head)
    send(latbuf.at[0, :width], latbuf.at[1, :width], s_core.at[1], r_core.at[1], other, head)

    ktbuf[0] = kbuf[0].astype(F32).T.astype(BF16)

    NC = NH
    up, down = lax.rem(y + 1, NY), lax.rem(y + NY - 1, NY)
    far = NY // 2
    near = far - 1
    order = [
        lax.rem(zh + dz, NZH) * NX + lax.rem(x + dx, NX)
        for dz in range(NZH) for dx in sorted(range(NX), key=lambda d: min(d, NX - d))
    ]
    order.insert(NC // 2, NC)

    def piece(y0, n):
        return abuf.at[y0] if n is NC else qbuf.at[y0, n]

    def forward(y0, k, step, plus, minus):
        n = order[k]
        if plus:
            send(piece(y0, n), piece(y0, n), s_up.at[step, k], r_y.at[y0, n], ctx_of(zl, up, c), head)
        if minus:
            send(piece(y0, n), piece(y0, n), s_down.at[step, k], r_y.at[y0, n], ctx_of(zl, down, c), head)

    def by_up(k):
        return k <= NC // 2

    for k, n in enumerate(order):
        if n is NC:
            for h in range(NH):
                arrived(abuf.at[y, pl.ds(h, 1)], r_ea.at[h])
        else:
            arrived(qbuf.at[y, n], r_eq.at[n])
        forward(y, k, 0, near > 0 or by_up(k), near > 0 or not by_up(k))

    CH = min(512, nk)

    def block(y0):
        q = qbuf[y0].reshape(NH * heads, wide)
        rest = qbuf[y0, :, :, base:].astype(F32)
        low, high = rest[:, :iheads].reshape(J, 128), rest[:, iheads:].reshape(J, 128)
        ln = lax.broadcasted_iota(jnp.int32, (J, 128), 1)
        qi32 = jnp.where(ln < tail, pltpu.roll(low, 128 - tail, 1), high)
        qi = qi32.astype(BF16)
        aux = abuf[y0][:, None, :]
        ln = lax.broadcasted_iota(jnp.int32, (NH, heads, 128), 2)
        sub = lax.broadcasted_iota(jnp.int32, (NH, heads, 128), 1)
        lse = jnp.sum(jnp.where(ln == sub, aux, 0.0), axis=2, keepdims=True).reshape(NH * heads, 1) * log2e
        wcol = jnp.sum(jnp.where(ln == sub + heads, aux, 0.0)[:, :iheads], axis=2, keepdims=True).reshape(J, 1)
        wq[y0] = (qi32 * wcol).astype(BF16)
        for side in range(2):
            for n in range(nk // CH):
                cols = slice(n * CH, (n + 1) * CH)
                kcols = slice(side * nk + n * CH, side * nk + (n + 1) * CH)
                s = jnp.dot(q, latbuf[side, :, cols], preferred_element_type=F32)
                e = jnp.exp2(s * (scale * log2e) - lse)
                target[pl.ds(y0, 1), kcols] = jnp.sum(e, axis=0, keepdims=True)
                rw = jnp.dot(qi, ktbuf[side, :, cols], preferred_element_type=F32)
                keep[y0, :, kcols] = jnp.where(rw > 0, 1.0, 0.0).astype(BF16)
                score[pl.ds(y0, 1), kcols] = jnp.sum(wcol * jnp.maximum(rw, 0.0), axis=0, keepdims=True)
        srow = score[pl.ds(y0, 1), :]
        m = jnp.max(srow, axis=1, keepdims=True)
        erow = jnp.exp(srow - m)
        score[pl.ds(y0, 1), :] = erow
        l = jnp.sum(erow, axis=1, keepdims=True)
        t = jnp.sum(target[pl.ds(y0, 1), :], axis=1, keepdims=True)
        ln = lax.broadcasted_iota(jnp.int32, (1, 128), 1)
        local[pl.ds(y0, 1), :] = jnp.where(ln == 0, m, jnp.where(ln == 1, l, t))

    arrived(kbuf.at[1], r_core.at[0])
    ktbuf[1] = kbuf[1].astype(F32).T.astype(BF16)
    arrived(latbuf.at[1, :width], r_core.at[1])
    block(y)
    for step in range(1, near + 1):
        yu = lax.rem(y + NY - step, NY)
        yd = lax.rem(y + step, NY)
        for k, n in enumerate(order):
            arrived(piece(yu, n), r_y.at[yu, n])
            forward(yu, k, step, step < near or by_up(k), False)
            arrived(piece(yd, n), r_y.at[yd, n])
            forward(yd, k, step, False, step < near or not by_up(k))
        block(yu)
        block(yd)
    yf = lax.rem(y + far, NY)
    for n in order:
        arrived(piece(yf, n), r_y.at[yf, n])
    block(yf)

    m, l, t = (local[:, n : n + 1] for n in range(3))
    m_local = m
    sl = lax.broadcasted_iota(jnp.int32, (NY, 128), 1)
    ss = lax.broadcasted_iota(jnp.int32, (NY, 128), 0)
    at = [sl == ss + n * NY for n in range(3)]
    me = zl * NY + y
    mine = jnp.where(at[0], m, jnp.where(at[1], l, jnp.where(at[2], t, 0.0)))
    st_buf[pl.ds(me, 1), :] = jnp.sum(mine, axis=0, keepdims=True)
    before = len(sends)
    for n, (dev, _) in enumerate(plane):
        send(st_buf.at[pl.ds(me, 1)], st_buf.at[pl.ds(me, 1)], s_st.at[n], r_st.at[me], dev, head)
    wqt = wq[...].reshape(NY * J, idim).astype(F32).T.astype(BF16)
    drain(before)
    for _, slot in plane:
        arrived(st_buf.at[pl.ds(slot, 1)], r_st.at[slot])
    stats = st_buf[...]
    peak = pltpu.roll(stats, NY, 1)
    top = jnp.max(peak, axis=0, keepdims=True)
    in_l = lax.broadcasted_iota(jnp.int32, stats.shape, 1) // NY == 1
    mass = jnp.sum(jnp.where(in_l, stats * jnp.exp(jnp.where(in_l, peak - top, 0.0)), stats), axis=0, keepdims=True)
    m = jnp.sum(jnp.where(at[1], top, 0.0), axis=1, keepdims=True)
    l = jnp.sum(jnp.where(at[1], mass, 0.0), axis=1, keepdims=True)
    t = jnp.sum(jnp.where(at[2], mass, 0.0), axis=1, keepdims=True)
    on_soft = jnp.exp(m_local - m) / l
    on_target = 1.0 / t

    nc = nk // KC
    nq = nc // NX

    def mask(side, q):
        cols = slice(q * nc, (q + 1) * nc)
        kcols = slice(side * nk + q * nc, side * nk + (q + 1) * nc)
        grad = factor * (score[:, kcols] * on_soft - target[:, kcols] * on_target)
        for y0 in range(NY):
            g = jnp.broadcast_to(grad[y0 : y0 + 1], (16, nc)).astype(BF16)
            g = keep[y0, :, kcols].reshape(J // 16, 16, nc) * g[None]
            masked[side, y0 * J : (y0 + 1) * J, cols] = g.reshape(J, nc)
        return jnp.dot(wqt, masked[side, :, cols], preferred_element_type=F32)

    for q in range(KC):
        ck_send[q] = mask(1, q).astype(BF16)
        send(ck_send.at[q], ck_recv.at[q], s_ck.at[q], r_ck.at[q], other, head)
    for q in range(KC):
        own_key = mask(0, q)
        arrived(ck_recv.at[q], r_ck.at[q])
        own_key = own_key + ck_recv[q].astype(F32)
        for n in range(NX):
            gx_sum[q, n] = own_key[:, n * nq : (n + 1) * nq]
            gx_send[q, n] = own_key[:, n * nq : (n + 1) * nq].astype(BF16)
        for n, x_ in enumerate(x_peers):
            send(gx_send.at[q, x_], gx_recv.at[q, x], s_gx.at[q, n], r_gx.at[q, x], ctx, zh * NX + x_)

    part[...] = (
        jnp.dot(masked[0], kbuf[0], preferred_element_type=F32)
        + jnp.dot(masked[1], kbuf[1], preferred_element_type=F32)
    ).reshape(part.shape).astype(part.dtype)
    for n, y_ in enumerate(y_peers):
        send(part.at[y_], ry_buf.at[y], s_ry.at[n], r_ry.at[y], ctx_of(zl, y_, c), head)

    drain(len(sends) - len(y_peers) - KC * len(x_peers))

    for q in range(KC):
        gsum = gx_sum[q, x]
        for x_ in x_peers:
            arrived(gx_recv.at[q, x_], r_gx.at[q, x_])
            gsum = gsum + gx_recv[q, x_].astype(F32)
        gz_send[q] = gsum.astype(BF16)
        send(gz_send.at[q], gz_recv.at[q], s_gz.at[q], r_gz.at[q], ctx, (1 - zh) * NX + x)

    total = part[y].astype(F32)
    for y_ in y_peers:
        arrived(ry_buf.at[y_], r_ry.at[y_])
        total = total + ry_buf[y_].astype(F32)
    zsum[...] = total.reshape(zsum.shape)
    slot = zh * NZ + zl
    for d, h in enumerate(hs):
        args = (zsum.at[h], fq_buf.at[slot], s_fq.at[d], r_fq.at[slot], ctx_of(x, y, c), h)
        if d == 0:
            send_unless(own_plane, *args)
        else:
            send(*args)

    drain(len(sends) - NH - KC)

    for q in range(KC):
        arrived(gz_recv.at[q], r_gz.at[q])
        ga_buf[q, x] = (gz_send[q].astype(F32) + gz_recv[q].astype(F32)).T.astype(BF16)
        for n, x_ in enumerate(x_peers):
            send(ga_buf.at[q, x], ga_buf.at[q, x], s_ga.at[q, n], r_ga.at[q, x], ctx, zh * NX + x_)

    for n in range(NZH * NZ):
        arrived(fq_buf.at[n], r_fq.at[n])
    for r in range(rows):
        own = jnp.sum(fq_buf[r * NZ : (r + 1) * NZ], axis=0)
        gq_ref[r] = own * column(w_ref[r : r + 1, :])
        gw_ref[r : r + 1, :] = row_of(jnp.sum(own * qi_ref[r].astype(F32), axis=1, keepdims=True))

    stores = [
        pltpu.make_async_copy(gq_ref, gq_hbm, s_out.at[KC]),
        pltpu.make_async_copy(gw_ref, gw_hbm, s_out.at[KC + 1]),
    ]
    for cp in stores:
        cp.start()
    for q in range(KC):
        for x_ in x_peers:
            arrived(ga_buf.at[q, x_], r_ga.at[q, x_])
        part_q = slice(q * nc, (q + 1) * nc)
        gk_ref[part_q] = ga_buf[q].astype(F32).reshape(nc, idim)
        cp = pltpu.make_async_copy(gk_ref.at[part_q], gk_hbm.at[part_q], s_out.at[q])
        cp.start()
        stores.append(cp)

    for cp in stores:
        cp.wait()
    drain(len(sends))


def body(dims, keys, q_attn, latent, lse_saved, q_index, k_index, head_weight):
    NZ, NY, NZH, NX = dims
    NH = NZH * NX
    rows, heads, width = q_attn.shape
    iheads, idim = q_index.shape[1:]
    nk = latent.shape[0]
    wide = -(-width // 128) * 128
    J = NH * iheads
    K2 = 2 * nk
    nq = nk // NX // KC
    NP = NH + 1
    V, DMA = pltpu.VMEM, pltpu.SemaphoreType.DMA
    vm = pl.BlockSpec(memory_space=pltpu.VMEM)
    scratch = [
        V((rows, iheads, idim), F32), V((rows, iheads), F32), V((nk, idim), F32), DMA((KC + 2,)),
        V((rows, heads, width), BF16), V((rows, heads), F32), V((rows, iheads, idim), BF16), V((rows, iheads), F32), DMA((6,)),
        V((rows, heads, wide), BF16), V((rows, 128), F32),
        V((NY, NH, heads, wide), BF16), V((NY, NH, 128), F32),
        V((2, wide, nk), BF16), V((2, nk, idim), BF16), V((2, idim, nk), BF16),
        V((NY, J, K2), BF16), V((NY, J, idim), BF16),
        V((NY, K2), F32), V((NY, K2), F32), V((NY, 128), F32), V((2, NY * J, nk), BF16),
        V((NZ * NY, 128), F32),
        V((NY, J, idim), BF16), V((NY, J, idim), BF16),
        V((NH, iheads, idim), F32), V((NZH * NZ, iheads, idim), F32),
        V((KC, idim, nk // KC), BF16), V((KC, idim, nk // KC), BF16),
        V((KC, NX, idim, nq), F32), V((KC, NX, idim, nq), BF16), V((KC, NX, idim, nq), BF16),
        V((KC, idim, nq), BF16), V((KC, idim, nq), BF16), V((KC, NX, nq, idim), BF16),
        DMA((rows, NZ)), DMA((rows, NZ)), DMA((NH,)), DMA((NH,)), DMA((2,)), DMA((2,)), DMA((KC,)), DMA((KC,)),
        DMA((NY, NP)), DMA((NY, NP)), DMA((NY, NP)),
        DMA((NZ * NY,)), DMA((NZ * NY,)), DMA((NY,)), DMA((NY,)), DMA((NH,)), DMA((NZH * NZ,)),
        DMA((KC, NX)), DMA((KC, NX)), DMA((KC,)), DMA((KC,)), DMA((KC, NX)), DMA((KC, NX)),
    ]
    shapes = (
        jax.ShapeDtypeStruct((rows, iheads, idim), F32),
        jax.ShapeDtypeStruct((rows, iheads), F32),
        jax.ShapeDtypeStruct((nk, idim), F32),
    )
    outs = pl.pallas_call(
        functools.partial(kernel, dims, keys / 32.0),
        out_shape=shapes,
        in_specs=[pl.BlockSpec(memory_space=pl.ANY)] * 6,
        out_specs=tuple(pl.BlockSpec(memory_space=pl.ANY) for _ in shapes),
        scratch_shapes=scratch,
        compiler_params=pltpu.CompilerParams(
            collective_id=0, has_side_effects=True, vmem_limit_bytes=56 * 1024 * 1024
        ),
        name="indexer_backward",
    )(q_attn, latent.T, lse_saved, q_index, k_index, head_weight)
    return pl.pallas_call(
        store,
        out_shape=shapes,
        in_specs=[vm] * 3,
        out_specs=tuple(pl.BlockSpec(memory_space=pl.ANY) for _ in shapes),
        scratch_shapes=[DMA((10,))],
        compiler_params=pltpu.CompilerParams(vmem_limit_bytes=58 * 1024 * 1024),
        name="store_results",
    )(*outs)


def store(a_ref, b_ref, c_ref, a_out, b_out, c_out, sems):
    n = c_ref.shape[0] // 8
    pairs = [(c_ref.at[pl.ds(i * n, n)], c_out.at[pl.ds(i * n, n)]) for i in range(8)]
    pairs += [(a_ref, a_out), (b_ref, b_out)]
    copies = [pltpu.make_async_copy(src, dst, sems.at[i]) for i, (src, dst) in enumerate(pairs)]
    for cp in copies:
        cp.start()
    for cp in copies:
        cp.wait()


def build(mesh, dims, keys):
    return jax.shard_map(
        functools.partial(body, dims, keys),
        mesh=mesh,
        in_specs=(
            P("ctx", "head", None),
            P("ctx", None),
            P("ctx", "head"),
            P("ctx", "head", None),
            P("ctx", None),
            P("ctx", "head"),
        ),
        out_specs=(P("ctx", "head", None), P("ctx", "head"), P("ctx", None)),
        check_vma=False,
    )


def solution(mesh):
    return build(mesh, DIMS, 65536)
```

```python
import functools
import math

import jax
import jax.numpy as jnp
from jax import lax
from jax.experimental import pallas as pl
from jax.experimental.pallas import tpu as pltpu
from jax.sharding import PartitionSpec as P

MESH = pl.DeviceIdType.MESH
F32, BF16 = jnp.float32, jnp.bfloat16
DIMS = (4, 8, 2, 4)
KC = 2
NT = (((1,), (1,)), ((), ()))


def column(row):
    n = row.shape[1]
    eye = lax.broadcasted_iota(jnp.int32, (n, n), 0) == lax.broadcasted_iota(jnp.int32, (n, n), 1)
    return jnp.sum(jnp.where(eye, row, 0.0), axis=1, keepdims=True)


def row_of(col):
    n = col.shape[0]
    eye = lax.broadcasted_iota(jnp.int32, (n, n), 0) == lax.broadcasted_iota(jnp.int32, (n, n), 1)
    return jnp.sum(jnp.where(eye, col, 0.0), axis=0, keepdims=True)


def kernel(
    dims, factor,
    q_hbm, lat_hbm, lse_hbm, qi_hbm, k_hbm, w_hbm,
    gq_hbm, gw_hbm, gk_hbm,
    gq_ref, gw_ref, gk_ref, s_out,
    q_ref, lse_ref, qi_ref, w_ref, s_in,
    q_stage, a_stage, qbuf, abuf, latbuf, kbuf, keep, wq, target, score, local, gbuf, masked,
    st_buf, part, ry_buf, zsum, fq_buf,
    ck_send, ck_recv, gx_sum, gx_send, gx_recv, gz_send, gz_recv, ga_buf,
    s_eq, s_ea, r_eq, r_ea, s_core, r_core, s_ck, r_ck, s_up, s_down, r_y,
    s_st, r_st, s_ry, r_ry, s_fq, r_fq, s_gx, r_gx, s_gz, r_gz, s_ga, r_ga,
):
    NZ, NY, NZH, NX = dims
    NH = NZH * NX
    ctx, head = lax.axis_index("ctx"), lax.axis_index("head")
    c = lax.rem(ctx, 2)
    y = lax.rem(lax.div(ctx, 2), NY)
    zl = lax.div(ctx, 2 * NY)
    x = lax.rem(head, NX)
    zh = lax.div(head, NX)
    rows, heads, width = q_ref.shape
    iheads, idim = qi_ref.shape[1:]
    nk = lat_hbm.shape[1]
    wide = qbuf.shape[-1]
    K2 = 2 * nk
    J = NH * iheads
    base = wide - 128
    tail = width - base
    scale = width ** -0.5
    log2e = math.log2(math.e)
    own_plane = x == zl

    def ctx_of(zl_, y_, c_):
        return (zl_ * NY + y_) * 2 + c_

    def rcopy(src, dst, ssem, rsem, ctx_, head_):
        return pltpu.make_async_remote_copy(
            src_ref=src, dst_ref=dst, send_sem=ssem, recv_sem=rsem,
            device_id={"ctx": ctx_, "head": head_}, device_id_type=MESH,
        )

    def arrived(dst, rsem):
        pltpu.make_async_copy(dst, dst, rsem).wait()

    sends = []

    def send(*args):
        cp = rcopy(*args)
        cp.start()
        sends.append(cp.wait_send)

    def drain(count):
        for finish in sends[:count]:
            finish()
        del sends[:count]

    def send_unless(local, src, dst, ssem, rsem, ctx_, head_):
        @pl.when(jnp.logical_not(local))
        def _():
            rcopy(src, dst, ssem, rsem, ctx_, head_).start()

        @pl.when(local)
        def _():
            pltpu.make_async_copy(src, dst, rsem).start()

        def finish():
            @pl.when(jnp.logical_not(local))
            def _():
                rcopy(src, dst, ssem, rsem, ctx_, head_).wait_send()

        sends.append(finish)

    y_peers = [lax.rem(y + d, NY) for d in range(1, NY)]
    z_peers = [lax.rem(zl + d, NZ) for d in range(1, NZ)]
    x_peers = [lax.rem(x + d, NX) for d in sorted(range(1, NX), key=lambda d: -min(d, NX - d))]
    zls = [zl] + z_peers
    plane = [
        (ctx_of(lax.rem(zl + dz, NZ), lax.rem(y + dy, NY), c), lax.rem(zl + dz, NZ) * NY + lax.rem(y + dy, NY))
        for dy in sorted(range(NY), key=lambda d: -min(d, NY - d)) for dz in range(NZ) if dy or dz
    ]
    hs = [lax.rem(head + d, NH) for d in range(NH)]

    barrier = pltpu.get_barrier_semaphore()

    def greet(ctx_, head_):
        pl.semaphore_signal(barrier, inc=1, device_id={"ctx": ctx_, "head": head_}, device_id_type=MESH)

    for d, h in enumerate(hs):
        if d == 0:
            @pl.when(jnp.logical_not(own_plane))
            def _():
                greet(ctx_of(x, y, c), head)
        else:
            greet(ctx_of(x, y, c), h)
    for r in range(NZH):
        for d, z_ in enumerate(zls):
            if d == 0:
                @pl.when(jnp.logical_not(own_plane & (zh == r)))
                def _():
                    greet(ctx_of(zl, y, c), r * NX + zl)
            else:
                greet(ctx_of(z_, y, c), r * NX + zl)
    loads = [
        pltpu.make_async_copy(src, dst, s_in.at[n])
        for n, (src, dst) in enumerate((
            (q_hbm, q_ref), (lse_hbm, lse_ref), (qi_hbm, qi_ref), (w_hbm, w_ref),
            (k_hbm, kbuf.at[0]), (lat_hbm, latbuf.at[0, :width]),
        ))
    ]
    for cp in loads:
        cp.start()

    greet(ctx_of(zl, y, 1 - c), head)
    for p in plane:
        greet(p[0], head)
    for x_ in x_peers:
        greet(ctx, zh * NX + x_)
    greet(ctx, (1 - zh) * NX + x)
    n_greet = 1 + (NY * NZ - 1) + (NX - 1) + 1 + NH + NZH * NZ

    for cp in loads[:4]:
        cp.wait()
    lane = lax.broadcasted_iota(jnp.int32, (heads, 128), 1)
    for r in range(rows):
        q_stage[r, :, :base] = q_ref[r, :, :base]
        last = jnp.concatenate([q_ref[r, :, base:].astype(F32), jnp.zeros((heads, 128 - tail), F32)], axis=1)
        qi = qi_ref[r].astype(F32)
        qi = jnp.concatenate([pltpu.roll(qi, tail, 1), qi], axis=0)
        q_stage[r, :, base:] = jnp.where(lane < tail, last, qi).astype(BF16)
        a_stage[r : r + 1, :] = jnp.concatenate(
            [lse_ref[r : r + 1, :], w_ref[r : r + 1, :], jnp.zeros((1, 128 - heads - iheads), F32)], axis=1
        )
    for side in range(2):
        latbuf[side, width:] = jnp.zeros((wide - width, nk), BF16)
    pl.semaphore_wait(barrier, jnp.where(own_plane, n_greet - 2, n_greet))

    for r in (1 - zh, zh) if NZH == 2 else range(NZH):
        for d, z_ in enumerate(zls):
            to = (ctx_of(z_, y, c), r * NX + zl)
            aargs = (a_stage.at[pl.ds(r, 1)], abuf.at[y, pl.ds(head, 1)], s_ea.at[r, d], r_ea.at[head], *to)
            qargs = (q_stage.at[r], qbuf.at[y, head], s_eq.at[r, d], r_eq.at[head], *to)
            if d == 0:
                send_unless(own_plane & (zh == r), *aargs)
                send_unless(own_plane & (zh == r), *qargs)
            else:
                send(*aargs)
                send(*qargs)
    other = ctx_of(zl, y, 1 - c)
    for cp in loads[4:]:
        cp.wait()
    send(kbuf.at[0], kbuf.at[1], s_core.at[0], r_core.at[0], other, head)
    send(latbuf.at[0, :width], latbuf.at[1, :width], s_core.at[1], r_core.at[1], other, head)

    NC = NH
    up, down = lax.rem(y + 1, NY), lax.rem(y + NY - 1, NY)
    far = NY // 2
    near = far - 1
    order = [
        lax.rem(zh + dz, NZH) * NX + lax.rem(x + dx, NX)
        for dz in range(NZH) for dx in sorted(range(NX), key=lambda d: min(d, NX - d))
    ]
    order.insert(NC // 2, NC)

    def piece(y0, n):
        return abuf.at[y0] if n is NC else qbuf.at[y0, n]

    def forward(y0, k, step, plus, minus):
        n = order[k]
        if plus:
            send(piece(y0, n), piece(y0, n), s_up.at[step, k], r_y.at[y0, n], ctx_of(zl, up, c), head)
        if minus:
            send(piece(y0, n), piece(y0, n), s_down.at[step, k], r_y.at[y0, n], ctx_of(zl, down, c), head)

    first, second = range(NC // 2), range(NC // 2, NC + 1)

    def by_up(k):
        return (k if k in first else k - second[0]) % 2 == 0

    def take(step, k):
        n = order[k]
        if step == 0:
            if n is NC:
                for h in range(NH):
                    arrived(abuf.at[y, pl.ds(h, 1)], r_ea.at[h])
            else:
                arrived(qbuf.at[y, n], r_eq.at[n])
            forward(y, k, 0, near > 0 or by_up(k), near > 0 or not by_up(k))
        elif step <= near:
            yu, yd = lax.rem(y + NY - step, NY), lax.rem(y + step, NY)
            arrived(piece(yu, n), r_y.at[yu, n])
            forward(yu, k, step, step < near or by_up(k), False)
            arrived(piece(yd, n), r_y.at[yd, n])
            forward(yd, k, step, False, step < near or not by_up(k))
        else:
            yf = lax.rem(y + far, NY)
            arrived(piece(yf, n), r_y.at[yf, n])

    def stage(step):
        ahead = [(step, k) for k in first] if step <= far else []
        behind = [(step - 1, k) for k in second] if step > 0 else []
        for n in range(max(len(ahead), len(behind))):
            for s_, k in ahead[n : n + 1] + behind[n : n + 1]:
                take(s_, k)

    stage(0)
    stage(1)

    CH = min(512, nk)

    def block(y0):
        q = qbuf[y0].reshape(NH * heads, wide)
        rest = qbuf[y0, :, :, base:].astype(F32)
        low, high = rest[:, :iheads].reshape(J, 128), rest[:, iheads:].reshape(J, 128)
        ln = lax.broadcasted_iota(jnp.int32, (J, 128), 1)
        qi32 = jnp.where(ln < tail, pltpu.roll(low, 128 - tail, 1), high)
        qi = qi32.astype(BF16)
        aux = abuf[y0][:, None, :]
        ln = lax.broadcasted_iota(jnp.int32, (NH, heads, 128), 2)
        sub = lax.broadcasted_iota(jnp.int32, (NH, heads, 128), 1)
        lse = jnp.sum(jnp.where(ln == sub, aux, 0.0), axis=2, keepdims=True).reshape(NH * heads, 1) * log2e
        wcol = jnp.sum(jnp.where(ln == sub + heads, aux, 0.0)[:, :iheads], axis=2, keepdims=True).reshape(J, 1)
        wq[y0] = (qi32 * wcol).astype(BF16)
        for side in range(2):
            for n in range(nk // CH):
                cols = slice(n * CH, (n + 1) * CH)
                kcols = slice(side * nk + n * CH, side * nk + (n + 1) * CH)
                s = jnp.dot(q, latbuf[side, :, cols], preferred_element_type=F32)
                e = jnp.exp2(s * (scale * log2e) - lse)
                target[pl.ds(y0, 1), kcols] = jnp.sum(e, axis=0, keepdims=True)
                rw = lax.dot_general(qi, kbuf[side, cols, :], NT, preferred_element_type=F32)
                keep[y0, :, kcols] = jnp.where(rw > 0, 1.0, 0.0).astype(BF16)
                score[pl.ds(y0, 1), kcols] = jnp.sum(wcol * jnp.maximum(rw, 0.0), axis=0, keepdims=True)
        srow = score[pl.ds(y0, 1), :]
        m = jnp.max(srow, axis=1, keepdims=True)
        l = jnp.sum(jnp.exp(srow - m), axis=1, keepdims=True)
        t = jnp.sum(target[pl.ds(y0, 1), :], axis=1, keepdims=True)
        ln = lax.broadcasted_iota(jnp.int32, (1, 128), 1)
        local[pl.ds(y0, 1), :] = jnp.where(ln == 0, m, jnp.where(ln == 1, l, t))

    arrived(kbuf.at[1], r_core.at[0])
    arrived(latbuf.at[1, :width], r_core.at[1])
    block(y)
    for step in range(1, near + 1):
        stage(step + 1)
        block(lax.rem(y + NY - step, NY))
        block(lax.rem(y + step, NY))
    stage(far + 1)
    block(lax.rem(y + far, NY))

    m, l, t = (local[:, n : n + 1] for n in range(3))
    sl = lax.broadcasted_iota(jnp.int32, (NY, 128), 1)
    ss = lax.broadcasted_iota(jnp.int32, (NY, 128), 0)
    at = [sl == ss + n * NY for n in range(3)]
    me = zl * NY + y
    mine = jnp.where(at[0], m, jnp.where(at[1], l, jnp.where(at[2], t, 0.0)))
    st_buf[pl.ds(me, 1), :] = jnp.sum(mine, axis=0, keepdims=True)
    before = len(sends)
    for n, (dev, _) in enumerate(plane):
        send(st_buf.at[pl.ds(me, 1)], st_buf.at[pl.ds(me, 1)], s_st.at[n], r_st.at[me], dev, head)
    wqt = wq[...].reshape(NY * J, idim).astype(F32).T.astype(BF16)
    drain(before)
    for _, slot in plane:
        arrived(st_buf.at[pl.ds(slot, 1)], r_st.at[slot])
    stats = st_buf[...]
    peak = pltpu.roll(stats, NY, 1)
    top = jnp.max(peak, axis=0, keepdims=True)
    in_l = lax.broadcasted_iota(jnp.int32, stats.shape, 1) // NY == 1
    mass = jnp.sum(jnp.where(in_l, stats * jnp.exp(jnp.where(in_l, peak - top, 0.0)), stats), axis=0, keepdims=True)
    m = jnp.sum(jnp.where(at[1], top, 0.0), axis=1, keepdims=True)
    l = jnp.sum(jnp.where(at[1], mass, 0.0), axis=1, keepdims=True)
    t = jnp.sum(jnp.where(at[2], mass, 0.0), axis=1, keepdims=True)
    grad = factor * (jnp.exp(score[...] - m) / l - target[...] / t)
    gbuf[...] = grad

    nc = nk // KC
    nq = nc // NX

    def mask(side, q):
        cols = slice(q * nc, (q + 1) * nc)
        kcols = slice(side * nk + q * nc, side * nk + (q + 1) * nc)
        for y0 in range(NY):
            g = jnp.broadcast_to(gbuf[y0 : y0 + 1, kcols], (16, nc)).astype(BF16)
            g = keep[y0, :, kcols].reshape(J // 16, 16, nc) * g[None]
            masked[side, y0 * J : (y0 + 1) * J, cols] = g.reshape(J, nc)
        return jnp.dot(wqt, masked[side, :, cols], preferred_element_type=F32)

    for q in range(KC):
        ck_send[q] = mask(1, q).astype(BF16)
        send(ck_send.at[q], ck_recv.at[q], s_ck.at[q], r_ck.at[q], other, head)
    for q in range(KC):
        own_key = mask(0, q)
        arrived(ck_recv.at[q], r_ck.at[q])
        own_key = own_key + ck_recv[q].astype(F32)
        for n in range(NX):
            gx_sum[q, n] = own_key[:, n * nq : (n + 1) * nq]
            gx_send[q, n] = own_key[:, n * nq : (n + 1) * nq].astype(BF16)
        for n, x_ in enumerate(x_peers):
            send(gx_send.at[q, x_], gx_recv.at[q, x], s_gx.at[q, n], r_gx.at[q, x], ctx, zh * NX + x_)

    part[...] = (
        jnp.dot(masked[0], kbuf[0], preferred_element_type=F32)
        + jnp.dot(masked[1], kbuf[1], preferred_element_type=F32)
    ).reshape(part.shape).astype(part.dtype)
    for n, y_ in enumerate(y_peers):
        send(part.at[y_], ry_buf.at[y], s_ry.at[n], r_ry.at[y], ctx_of(zl, y_, c), head)

    drain(len(sends) - len(y_peers) - KC * len(x_peers))

    for q in range(KC):
        gsum = gx_sum[q, x]
        for x_ in x_peers:
            arrived(gx_recv.at[q, x_], r_gx.at[q, x_])
            gsum = gsum + gx_recv[q, x_].astype(F32)
        gz_send[q] = gsum.astype(BF16)
        send(gz_send.at[q], gz_recv.at[q], s_gz.at[q], r_gz.at[q], ctx, (1 - zh) * NX + x)

    total = part[y].astype(F32)
    for y_ in y_peers:
        arrived(ry_buf.at[y_], r_ry.at[y_])
        total = total + ry_buf[y_].astype(F32)
    zsum[...] = total.reshape(zsum.shape)
    slot = zh * NZ + zl
    for d, h in enumerate(hs):
        args = (zsum.at[h], fq_buf.at[slot], s_fq.at[d], r_fq.at[slot], ctx_of(x, y, c), h)
        if d == 0:
            send_unless(own_plane, *args)
        else:
            send(*args)

    drain(len(sends) - NH - KC)

    for q in range(KC):
        arrived(gz_recv.at[q], r_gz.at[q])
        ga_buf[q, x] = (gz_send[q].astype(F32) + gz_recv[q].astype(F32)).T.astype(BF16)
        for n, x_ in enumerate(x_peers):
            send(ga_buf.at[q, x], ga_buf.at[q, x], s_ga.at[q, n], r_ga.at[q, x], ctx, zh * NX + x_)

    for n in range(NZH * NZ):
        arrived(fq_buf.at[n], r_fq.at[n])
    for r in range(rows):
        own = jnp.sum(fq_buf[r * NZ : (r + 1) * NZ], axis=0)
        gq_ref[r] = own * column(w_ref[r : r + 1, :])
        gw_ref[r : r + 1, :] = row_of(jnp.sum(own * qi_ref[r].astype(F32), axis=1, keepdims=True))

    stores = [
        pltpu.make_async_copy(gq_ref, gq_hbm, s_out.at[KC]),
        pltpu.make_async_copy(gw_ref, gw_hbm, s_out.at[KC + 1]),
    ]
    for cp in stores:
        cp.start()
    for q in range(KC):
        for x_ in x_peers:
            arrived(ga_buf.at[q, x_], r_ga.at[q, x_])
        part_q = slice(q * nc, (q + 1) * nc)
        gk_ref[part_q] = ga_buf[q].astype(F32).reshape(nc, idim)
        cp = pltpu.make_async_copy(gk_ref.at[part_q], gk_hbm.at[part_q], s_out.at[q])
        cp.start()
        stores.append(cp)

    for cp in stores:
        cp.wait()
    drain(len(sends))


def body(dims, keys, q_attn, latent, lse_saved, q_index, k_index, head_weight):
    NZ, NY, NZH, NX = dims
    NH = NZH * NX
    rows, heads, width = q_attn.shape
    iheads, idim = q_index.shape[1:]
    nk = latent.shape[0]
    wide = -(-width // 128) * 128
    J = NH * iheads
    K2 = 2 * nk
    nq = nk // NX // KC
    NP = NH + 1
    V, DMA = pltpu.VMEM, pltpu.SemaphoreType.DMA
    vm = pl.BlockSpec(memory_space=pltpu.VMEM)
    scratch = [
        V((rows, iheads, idim), F32), V((rows, iheads), F32), V((nk, idim), F32), DMA((KC + 2,)),
        V((rows, heads, width), BF16), V((rows, heads), F32), V((rows, iheads, idim), BF16), V((rows, iheads), F32), DMA((6,)),
        V((rows, heads, wide), BF16), V((rows, 128), F32),
        V((NY, NH, heads, wide), BF16), V((NY, NH, 128), F32),
        V((2, wide, nk), BF16), V((2, nk, idim), BF16),
        V((NY, J, K2), BF16), V((NY, J, idim), BF16),
        V((NY, K2), F32), V((NY, K2), F32), V((NY, 128), F32), V((NY, K2), F32), V((2, NY * J, nk), BF16),
        V((NZ * NY, 128), F32),
        V((NY, J, idim), BF16), V((NY, J, idim), BF16),
        V((NH, iheads, idim), F32), V((NZH * NZ, iheads, idim), F32),
        V((KC, idim, nk // KC), BF16), V((KC, idim, nk // KC), BF16),
        V((KC, NX, idim, nq), F32), V((KC, NX, idim, nq), BF16), V((KC, NX, idim, nq), BF16),
        V((KC, idim, nq), BF16), V((KC, idim, nq), BF16), V((KC, NX, nq, idim), BF16),
        DMA((rows, NZ)), DMA((rows, NZ)), DMA((NH,)), DMA((NH,)), DMA((2,)), DMA((2,)), DMA((KC,)), DMA((KC,)),
        DMA((NY, NP)), DMA((NY, NP)), DMA((NY, NP)),
        DMA((NZ * NY,)), DMA((NZ * NY,)), DMA((NY,)), DMA((NY,)), DMA((NH,)), DMA((NZH * NZ,)),
        DMA((KC, NX)), DMA((KC, NX)), DMA((KC,)), DMA((KC,)), DMA((KC, NX)), DMA((KC, NX)),
    ]
    shapes = (
        jax.ShapeDtypeStruct((rows, iheads, idim), F32),
        jax.ShapeDtypeStruct((rows, iheads), F32),
        jax.ShapeDtypeStruct((nk, idim), F32),
    )
    outs = pl.pallas_call(
        functools.partial(kernel, dims, keys / 32.0),
        out_shape=shapes,
        in_specs=[pl.BlockSpec(memory_space=pl.ANY)] * 6,
        out_specs=tuple(pl.BlockSpec(memory_space=pl.ANY) for _ in shapes),
        scratch_shapes=scratch,
        compiler_params=pltpu.CompilerParams(
            collective_id=0, has_side_effects=True, vmem_limit_bytes=56 * 1024 * 1024
        ),
        name="indexer_backward",
    )(q_attn, latent.T, lse_saved, q_index, k_index, head_weight)
    return pl.pallas_call(
        store,
        out_shape=shapes,
        in_specs=[vm] * 3,
        out_specs=tuple(pl.BlockSpec(memory_space=pl.ANY) for _ in shapes),
        scratch_shapes=[DMA((10,))],
        compiler_params=pltpu.CompilerParams(vmem_limit_bytes=58 * 1024 * 1024),
        name="store_results",
    )(*outs)


def store(a_ref, b_ref, c_ref, a_out, b_out, c_out, sems):
    n = c_ref.shape[0] // 8
    pairs = [(c_ref.at[pl.ds(i * n, n)], c_out.at[pl.ds(i * n, n)]) for i in range(8)]
    pairs += [(a_ref, a_out), (b_ref, b_out)]
    copies = [pltpu.make_async_copy(src, dst, sems.at[i]) for i, (src, dst) in enumerate(pairs)]
    for cp in copies:
        cp.start()
    for cp in copies:
        cp.wait()


def build(mesh, dims, keys):
    return jax.shard_map(
        functools.partial(body, dims, keys),
        mesh=mesh,
        in_specs=(
            P("ctx", "head", None),
            P("ctx", None),
            P("ctx", "head"),
            P("ctx", "head", None),
            P("ctx", None),
            P("ctx", "head"),
        ),
        out_specs=(P("ctx", "head", None), P("ctx", "head"), P("ctx", None)),
        check_vma=False,
    )


def solution(mesh):
    return build(mesh, DIMS, 65536)
```

```python
import functools
import math

import jax
import jax.numpy as jnp
from jax import lax
from jax.experimental import pallas as pl
from jax.experimental.pallas import tpu as pltpu
from jax.sharding import PartitionSpec as P

MESH = pl.DeviceIdType.MESH
F32, BF16 = jnp.float32, jnp.bfloat16
DIMS = (4, 8, 2, 4)
KC = 2
NT = (((1,), (1,)), ((), ()))


def column(row):
    n = row.shape[1]
    eye = lax.broadcasted_iota(jnp.int32, (n, n), 0) == lax.broadcasted_iota(jnp.int32, (n, n), 1)
    return jnp.sum(jnp.where(eye, row, 0.0), axis=1, keepdims=True)


def row_of(col):
    n = col.shape[0]
    eye = lax.broadcasted_iota(jnp.int32, (n, n), 0) == lax.broadcasted_iota(jnp.int32, (n, n), 1)
    return jnp.sum(jnp.where(eye, col, 0.0), axis=0, keepdims=True)


def kernel(
    dims, factor,
    q_hbm, lat_hbm, lse_hbm, qi_hbm, k_hbm, w_hbm,
    gq_hbm, gw_hbm, gk_hbm,
    gq_ref, gw_ref, gk_ref, s_out,
    q_ref, lse_ref, qi_ref, w_ref, s_in,
    q_stage, a_stage, qbuf, abuf, latbuf, kbuf, keep, wq, target, score, local, masked,
    st_buf, part, ry_buf, zsum, fq_buf,
    ck_send, ck_recv, gx_sum, gx_send, gx_recv, gz_send, gz_recv, ga_buf,
    s_eq, s_ea, r_eq, r_ea, s_core, r_core, s_ck, r_ck, s_up, s_down, r_y,
    s_st, r_st, s_ry, r_ry, s_fq, r_fq, s_gx, r_gx, s_gz, r_gz, s_ga, r_ga,
):
    NZ, NY, NZH, NX = dims
    NH = NZH * NX
    ctx, head = lax.axis_index("ctx"), lax.axis_index("head")
    c = lax.rem(ctx, 2)
    y = lax.rem(lax.div(ctx, 2), NY)
    zl = lax.div(ctx, 2 * NY)
    x = lax.rem(head, NX)
    zh = lax.div(head, NX)
    rows, heads, width = q_ref.shape
    iheads, idim = qi_ref.shape[1:]
    nk = lat_hbm.shape[1]
    wide = qbuf.shape[-1]
    K2 = 2 * nk
    J = NH * iheads
    base = wide - 128
    tail = width - base
    scale = width ** -0.5
    log2e = math.log2(math.e)
    own_plane = x == zl

    def ctx_of(zl_, y_, c_):
        return (zl_ * NY + y_) * 2 + c_

    def rcopy(src, dst, ssem, rsem, ctx_, head_):
        return pltpu.make_async_remote_copy(
            src_ref=src, dst_ref=dst, send_sem=ssem, recv_sem=rsem,
            device_id={"ctx": ctx_, "head": head_}, device_id_type=MESH,
        )

    def arrived(dst, rsem):
        pltpu.make_async_copy(dst, dst, rsem).wait()

    sends = []

    def send(*args):
        cp = rcopy(*args)
        cp.start()
        sends.append(cp.wait_send)

    def drain(count):
        for finish in sends[:count]:
            finish()
        del sends[:count]

    def send_unless(local, src, dst, ssem, rsem, ctx_, head_):
        @pl.when(jnp.logical_not(local))
        def _():
            rcopy(src, dst, ssem, rsem, ctx_, head_).start()

        @pl.when(local)
        def _():
            pltpu.make_async_copy(src, dst, rsem).start()

        def finish():
            @pl.when(jnp.logical_not(local))
            def _():
                rcopy(src, dst, ssem, rsem, ctx_, head_).wait_send()

        sends.append(finish)

    y_peers = [lax.rem(y + d, NY) for d in range(1, NY)]
    z_peers = [lax.rem(zl + d, NZ) for d in range(1, NZ)]
    x_peers = [lax.rem(x + d, NX) for d in sorted(range(1, NX), key=lambda d: -min(d, NX - d))]
    zls = [zl] + z_peers
    plane = [
        (ctx_of(lax.rem(zl + dz, NZ), lax.rem(y + dy, NY), c), lax.rem(zl + dz, NZ) * NY + lax.rem(y + dy, NY))
        for dy in sorted(range(NY), key=lambda d: -min(d, NY - d)) for dz in range(NZ) if dy or dz
    ]
    hs = [lax.rem(head + d, NH) for d in range(NH)]

    barrier = pltpu.get_barrier_semaphore()

    def greet(ctx_, head_):
        pl.semaphore_signal(barrier, inc=1, device_id={"ctx": ctx_, "head": head_}, device_id_type=MESH)

    for d, h in enumerate(hs):
        if d == 0:
            @pl.when(jnp.logical_not(own_plane))
            def _():
                greet(ctx_of(x, y, c), head)
        else:
            greet(ctx_of(x, y, c), h)
    for r in range(NZH):
        for d, z_ in enumerate(zls):
            if d == 0:
                @pl.when(jnp.logical_not(own_plane & (zh == r)))
                def _():
                    greet(ctx_of(zl, y, c), r * NX + zl)
            else:
                greet(ctx_of(z_, y, c), r * NX + zl)
    loads = [
        pltpu.make_async_copy(src, dst, s_in.at[n])
        for n, (src, dst) in enumerate((
            (q_hbm, q_ref), (lse_hbm, lse_ref), (qi_hbm, qi_ref), (w_hbm, w_ref),
            (k_hbm, kbuf.at[0]), (lat_hbm, latbuf.at[0, :width]),
        ))
    ]
    for cp in loads:
        cp.start()

    greet(ctx_of(zl, y, 1 - c), head)
    for p in plane:
        greet(p[0], head)
    for x_ in x_peers:
        greet(ctx, zh * NX + x_)
    greet(ctx, (1 - zh) * NX + x)
    n_greet = 1 + (NY * NZ - 1) + (NX - 1) + 1 + NH + NZH * NZ

    for cp in loads[:4]:
        cp.wait()
    lane = lax.broadcasted_iota(jnp.int32, (heads, 128), 1)
    for r in range(rows):
        q_stage[r, :, :base] = q_ref[r, :, :base]
        last = jnp.concatenate([q_ref[r, :, base:].astype(F32), jnp.zeros((heads, 128 - tail), F32)], axis=1)
        qi = qi_ref[r].astype(F32)
        qi = jnp.concatenate([pltpu.roll(qi, tail, 1), qi], axis=0)
        q_stage[r, :, base:] = jnp.where(lane < tail, last, qi).astype(BF16)
        a_stage[r : r + 1, :] = jnp.concatenate(
            [lse_ref[r : r + 1, :], w_ref[r : r + 1, :], jnp.zeros((1, 128 - heads - iheads), F32)], axis=1
        )
    for side in range(2):
        latbuf[side, width:] = jnp.zeros((wide - width, nk), BF16)
    pl.semaphore_wait(barrier, jnp.where(own_plane, n_greet - 2, n_greet))

    for r in (zh, 1 - zh) if NZH == 2 else range(NZH):
        for d, z_ in enumerate(zls):
            to = (ctx_of(z_, y, c), r * NX + zl)
            aargs = (a_stage.at[pl.ds(r, 1)], abuf.at[y, pl.ds(head, 1)], s_ea.at[r, d], r_ea.at[head], *to)
            qargs = (q_stage.at[r], qbuf.at[y, head], s_eq.at[r, d], r_eq.at[head], *to)
            if d == 0:
                send_unless(own_plane & (zh == r), *aargs)
                send_unless(own_plane & (zh == r), *qargs)
            else:
                send(*aargs)
                send(*qargs)
    other = ctx_of(zl, y, 1 - c)
    for cp in loads[4:]:
        cp.wait()
    send(kbuf.at[0], kbuf.at[1], s_core.at[0], r_core.at[0], other, head)
    send(latbuf.at[0, :width], latbuf.at[1, :width], s_core.at[1], r_core.at[1], other, head)

    NC = NH
    up, down = lax.rem(y + 1, NY), lax.rem(y + NY - 1, NY)
    far = NY // 2
    near = far - 1
    order = [
        lax.rem(zh + dz, NZH) * NX + lax.rem(x + dx, NX)
        for dz in range(NZH) for dx in sorted(range(NX), key=lambda d: min(d, NX - d))
    ]
    order.insert(NC // 2, NC)

    def piece(y0, n):
        return abuf.at[y0] if n is NC else qbuf.at[y0, n]

    def forward(y0, k, step, plus, minus):
        n = order[k]
        if plus:
            send(piece(y0, n), piece(y0, n), s_up.at[step, k], r_y.at[y0, n], ctx_of(zl, up, c), head)
        if minus:
            send(piece(y0, n), piece(y0, n), s_down.at[step, k], r_y.at[y0, n], ctx_of(zl, down, c), head)

    def by_up(k):
        return k <= NC // 2

    for k, n in enumerate(order):
        if n is NC:
            for h in range(NH):
                arrived(abuf.at[y, pl.ds(h, 1)], r_ea.at[h])
        else:
            arrived(qbuf.at[y, n], r_eq.at[n])
        forward(y, k, 0, near > 0 or by_up(k), near > 0 or not by_up(k))

    CH = min(512, nk)

    def block(y0):
        q = qbuf[y0].reshape(NH * heads, wide)
        rest = qbuf[y0, :, :, base:].astype(F32)
        low, high = rest[:, :iheads].reshape(J, 128), rest[:, iheads:].reshape(J, 128)
        ln = lax.broadcasted_iota(jnp.int32, (J, 128), 1)
        qi32 = jnp.where(ln < tail, pltpu.roll(low, 128 - tail, 1), high)
        qi = qi32.astype(BF16)
        aux = abuf[y0][:, None, :]
        ln = lax.broadcasted_iota(jnp.int32, (NH, heads, 128), 2)
        sub = lax.broadcasted_iota(jnp.int32, (NH, heads, 128), 1)
        lse = jnp.sum(jnp.where(ln == sub, aux, 0.0), axis=2, keepdims=True).reshape(NH * heads, 1) * log2e
        wcol = jnp.sum(jnp.where(ln == sub + heads, aux, 0.0)[:, :iheads], axis=2, keepdims=True).reshape(J, 1)
        wq[y0] = (qi32 * wcol).astype(BF16)
        for side in range(2):
            for n in range(nk // CH):
                cols = slice(n * CH, (n + 1) * CH)
                kcols = slice(side * nk + n * CH, side * nk + (n + 1) * CH)
                s = jnp.dot(q, latbuf[side, :, cols], preferred_element_type=F32)
                e = jnp.exp2(s * (scale * log2e) - lse)
                target[pl.ds(y0, 1), kcols] = jnp.sum(e, axis=0, keepdims=True)
                rw = lax.dot_general(qi, kbuf[side, cols, :], NT, preferred_element_type=F32)
                keep[y0, :, kcols] = jnp.where(rw > 0, 1.0, 0.0).astype(BF16)
                score[pl.ds(y0, 1), kcols] = jnp.sum(wcol * jnp.maximum(rw, 0.0), axis=0, keepdims=True)
        srow = score[pl.ds(y0, 1), :]
        m = jnp.max(srow, axis=1, keepdims=True)
        erow = jnp.exp(srow - m)
        score[pl.ds(y0, 1), :] = erow
        l = jnp.sum(erow, axis=1, keepdims=True)
        t = jnp.sum(target[pl.ds(y0, 1), :], axis=1, keepdims=True)
        ln = lax.broadcasted_iota(jnp.int32, (1, 128), 1)
        local[pl.ds(y0, 1), :] = jnp.where(ln == 0, m, jnp.where(ln == 1, l, t))

    arrived(kbuf.at[1], r_core.at[0])
    arrived(latbuf.at[1, :width], r_core.at[1])
    block(y)
    for step in range(1, near + 1):
        yu = lax.rem(y + NY - step, NY)
        yd = lax.rem(y + step, NY)
        for k, n in enumerate(order):
            arrived(piece(yu, n), r_y.at[yu, n])
            forward(yu, k, step, step < near or by_up(k), False)
            arrived(piece(yd, n), r_y.at[yd, n])
            forward(yd, k, step, False, step < near or not by_up(k))
        block(yu)
        block(yd)
    yf = lax.rem(y + far, NY)
    for n in order:
        arrived(piece(yf, n), r_y.at[yf, n])
    block(yf)

    m, l, t = (local[:, n : n + 1] for n in range(3))
    m_local = m
    sl = lax.broadcasted_iota(jnp.int32, (NY, 128), 1)
    ss = lax.broadcasted_iota(jnp.int32, (NY, 128), 0)
    at = [sl == ss + n * NY for n in range(3)]
    me = zl * NY + y
    mine = jnp.where(at[0], m, jnp.where(at[1], l, jnp.where(at[2], t, 0.0)))
    st_buf[pl.ds(me, 1), :] = jnp.sum(mine, axis=0, keepdims=True)
    before = len(sends)
    for n, (dev, _) in enumerate(plane):
        send(st_buf.at[pl.ds(me, 1)], st_buf.at[pl.ds(me, 1)], s_st.at[n], r_st.at[me], dev, head)
    wqt = wq[...].reshape(NY * J, idim).astype(F32).T.astype(BF16)
    drain(before)
    for _, slot in plane:
        arrived(st_buf.at[pl.ds(slot, 1)], r_st.at[slot])
    stats = st_buf[...]
    peak = pltpu.roll(stats, NY, 1)
    top = jnp.max(peak, axis=0, keepdims=True)
    in_l = lax.broadcasted_iota(jnp.int32, stats.shape, 1) // NY == 1
    mass = jnp.sum(jnp.where(in_l, stats * jnp.exp(jnp.where(in_l, peak - top, 0.0)), stats), axis=0, keepdims=True)
    m = jnp.sum(jnp.where(at[1], top, 0.0), axis=1, keepdims=True)
    l = jnp.sum(jnp.where(at[1], mass, 0.0), axis=1, keepdims=True)
    t = jnp.sum(jnp.where(at[2], mass, 0.0), axis=1, keepdims=True)
    on_soft = jnp.exp(m_local - m) / l
    on_target = 1.0 / t

    nc = nk // KC
    nq = nc // NX

    def mask(side, q):
        cols = slice(q * nc, (q + 1) * nc)
        kcols = slice(side * nk + q * nc, side * nk + (q + 1) * nc)
        grad = factor * (score[:, kcols] * on_soft - target[:, kcols] * on_target)
        for y0 in range(NY):
            g = jnp.broadcast_to(grad[y0 : y0 + 1], (16, nc)).astype(BF16)
            g = keep[y0, :, kcols].reshape(J // 16, 16, nc) * g[None]
            masked[side, y0 * J : (y0 + 1) * J, cols] = g.reshape(J, nc)
        return jnp.dot(wqt, masked[side, :, cols], preferred_element_type=F32)

    for q in range(KC):
        ck_send[q] = mask(1, q).astype(BF16)
        send(ck_send.at[q], ck_recv.at[q], s_ck.at[q], r_ck.at[q], other, head)
    for q in range(KC):
        own_key = mask(0, q)
        arrived(ck_recv.at[q], r_ck.at[q])
        own_key = own_key + ck_recv[q].astype(F32)
        for n in range(NX):
            gx_sum[q, n] = own_key[:, n * nq : (n + 1) * nq]
            gx_send[q, n] = own_key[:, n * nq : (n + 1) * nq].astype(BF16)
        for n, x_ in enumerate(x_peers):
            send(gx_send.at[q, x_], gx_recv.at[q, x], s_gx.at[q, n], r_gx.at[q, x], ctx, zh * NX + x_)

    part[...] = (
        jnp.dot(masked[0], kbuf[0], preferred_element_type=F32)
        + jnp.dot(masked[1], kbuf[1], preferred_element_type=F32)
    ).reshape(part.shape).astype(part.dtype)
    for n, y_ in enumerate(y_peers):
        send(part.at[y_], ry_buf.at[y], s_ry.at[n], r_ry.at[y], ctx_of(zl, y_, c), head)

    drain(len(sends) - len(y_peers) - KC * len(x_peers))

    for q in range(KC):
        gsum = gx_sum[q, x]
        for x_ in x_peers:
            arrived(gx_recv.at[q, x_], r_gx.at[q, x_])
            gsum = gsum + gx_recv[q, x_].astype(F32)
        gz_send[q] = gsum.astype(BF16)
        send(gz_send.at[q], gz_recv.at[q], s_gz.at[q], r_gz.at[q], ctx, (1 - zh) * NX + x)

    total = part[y].astype(F32)
    for y_ in y_peers:
        arrived(ry_buf.at[y_], r_ry.at[y_])
        total = total + ry_buf[y_].astype(F32)
    zsum[...] = total.reshape(zsum.shape)
    slot = zh * NZ + zl
    for d, h in enumerate(hs):
        args = (zsum.at[h], fq_buf.at[slot], s_fq.at[d], r_fq.at[slot], ctx_of(x, y, c), h)
        if d == 0:
            send_unless(own_plane, *args)
        else:
            send(*args)

    drain(len(sends) - NH - KC)

    for q in range(KC):
        arrived(gz_recv.at[q], r_gz.at[q])
        ga_buf[q, x] = (gz_send[q].astype(F32) + gz_recv[q].astype(F32)).T.astype(BF16)
        for n, x_ in enumerate(x_peers):
            send(ga_buf.at[q, x], ga_buf.at[q, x], s_ga.at[q, n], r_ga.at[q, x], ctx, zh * NX + x_)

    for n in range(NZH * NZ):
        arrived(fq_buf.at[n], r_fq.at[n])
    for r in range(rows):
        own = jnp.sum(fq_buf[r * NZ : (r + 1) * NZ], axis=0)
        gq_ref[r] = own * column(w_ref[r : r + 1, :])
        gw_ref[r : r + 1, :] = row_of(jnp.sum(own * qi_ref[r].astype(F32), axis=1, keepdims=True))

    stores = [
        pltpu.make_async_copy(gq_ref, gq_hbm, s_out.at[KC]),
        pltpu.make_async_copy(gw_ref, gw_hbm, s_out.at[KC + 1]),
    ]
    for cp in stores:
        cp.start()
    for q in range(KC):
        for x_ in x_peers:
            arrived(ga_buf.at[q, x_], r_ga.at[q, x_])
        part_q = slice(q * nc, (q + 1) * nc)
        gk_ref[part_q] = ga_buf[q].astype(F32).reshape(nc, idim)
        cp = pltpu.make_async_copy(gk_ref.at[part_q], gk_hbm.at[part_q], s_out.at[q])
        cp.start()
        stores.append(cp)

    for cp in stores:
        cp.wait()
    drain(len(sends))


def body(dims, keys, q_attn, latent, lse_saved, q_index, k_index, head_weight):
    NZ, NY, NZH, NX = dims
    NH = NZH * NX
    rows, heads, width = q_attn.shape
    iheads, idim = q_index.shape[1:]
    nk = latent.shape[0]
    wide = -(-width // 128) * 128
    J = NH * iheads
    K2 = 2 * nk
    nq = nk // NX // KC
    NP = NH + 1
    V, DMA = pltpu.VMEM, pltpu.SemaphoreType.DMA
    vm = pl.BlockSpec(memory_space=pltpu.VMEM)
    scratch = [
        V((rows, iheads, idim), F32), V((rows, iheads), F32), V((nk, idim), F32), DMA((KC + 2,)),
        V((rows, heads, width), BF16), V((rows, heads), F32), V((rows, iheads, idim), BF16), V((rows, iheads), F32), DMA((6,)),
        V((rows, heads, wide), BF16), V((rows, 128), F32),
        V((NY, NH, heads, wide), BF16), V((NY, NH, 128), F32),
        V((2, wide, nk), BF16), V((2, nk, idim), BF16),
        V((NY, J, K2), BF16), V((NY, J, idim), BF16),
        V((NY, K2), F32), V((NY, K2), F32), V((NY, 128), F32), V((2, NY * J, nk), BF16),
        V((NZ * NY, 128), F32),
        V((NY, J, idim), BF16), V((NY, J, idim), BF16),
        V((NH, iheads, idim), F32), V((NZH * NZ, iheads, idim), F32),
        V((KC, idim, nk // KC), BF16), V((KC, idim, nk // KC), BF16),
        V((KC, NX, idim, nq), F32), V((KC, NX, idim, nq), BF16), V((KC, NX, idim, nq), BF16),
        V((KC, idim, nq), BF16), V((KC, idim, nq), BF16), V((KC, NX, nq, idim), BF16),
        DMA((rows, NZ)), DMA((rows, NZ)), DMA((NH,)), DMA((NH,)), DMA((2,)), DMA((2,)), DMA((KC,)), DMA((KC,)),
        DMA((NY, NP)), DMA((NY, NP)), DMA((NY, NP)),
        DMA((NZ * NY,)), DMA((NZ * NY,)), DMA((NY,)), DMA((NY,)), DMA((NH,)), DMA((NZH * NZ,)),
        DMA((KC, NX)), DMA((KC, NX)), DMA((KC,)), DMA((KC,)), DMA((KC, NX)), DMA((KC, NX)),
    ]
    shapes = (
        jax.ShapeDtypeStruct((rows, iheads, idim), F32),
        jax.ShapeDtypeStruct((rows, iheads), F32),
        jax.ShapeDtypeStruct((nk, idim), F32),
    )
    outs = pl.pallas_call(
        functools.partial(kernel, dims, keys / 32.0),
        out_shape=shapes,
        in_specs=[pl.BlockSpec(memory_space=pl.ANY)] * 6,
        out_specs=tuple(pl.BlockSpec(memory_space=pl.ANY) for _ in shapes),
        scratch_shapes=scratch,
        compiler_params=pltpu.CompilerParams(
            collective_id=0, has_side_effects=True, vmem_limit_bytes=56 * 1024 * 1024
        ),
        name="indexer_backward",
    )(q_attn, latent.T, lse_saved, q_index, k_index, head_weight)
    return pl.pallas_call(
        store,
        out_shape=shapes,
        in_specs=[vm] * 3,
        out_specs=tuple(pl.BlockSpec(memory_space=pl.ANY) for _ in shapes),
        scratch_shapes=[DMA((10,))],
        compiler_params=pltpu.CompilerParams(vmem_limit_bytes=58 * 1024 * 1024),
        name="store_results",
    )(*outs)


def store(a_ref, b_ref, c_ref, a_out, b_out, c_out, sems):
    n = c_ref.shape[0] // 8
    pairs = [(c_ref.at[pl.ds(i * n, n)], c_out.at[pl.ds(i * n, n)]) for i in range(8)]
    pairs += [(a_ref, a_out), (b_ref, b_out)]
    copies = [pltpu.make_async_copy(src, dst, sems.at[i]) for i, (src, dst) in enumerate(pairs)]
    for cp in copies:
        cp.start()
    for cp in copies:
        cp.wait()


def build(mesh, dims, keys):
    return jax.shard_map(
        functools.partial(body, dims, keys),
        mesh=mesh,
        in_specs=(
            P("ctx", "head", None),
            P("ctx", None),
            P("ctx", "head"),
            P("ctx", "head", None),
            P("ctx", None),
            P("ctx", "head"),
        ),
        out_specs=(P("ctx", "head", None), P("ctx", "head"), P("ctx", None)),
        check_vma=False,
    )


def solution(mesh):
    return build(mesh, DIMS, 65536)
```
